32 devices in a mesh: dp: 16 (over z, y, core), tensor: 2 (over x).
Axes of the slice: x: 2, y: 2, z: 4, core: 2. Of those that a mesh axis runs over, the one named last changes fastest.
Arguments:
- inputs: bfloat16 [64, 288, 768], P('dp'), may hold values from -32 to 32
- memory: bfloat16 [64, 1024, 768], P('dp'), may hold values from -8 to 8
- dec_segments: int32 [64, 288], P('dp'), may hold values from 0 to 3, as said below
- mem_segments: int32 [64, 1024], P('dp'), may hold values from 0 to 3, as said below
- mem_lengths: int32 [64], P('dp'), may hold values from 512 to 1024, as said below
- buckets: int32 [288], replicated, may hold values from 0 to 31, as said below
- cotangent: bfloat16 [64, 288, 768], P('dp'), may hold values from -8 to 8
- attention_in: float32 [768, 6, 768], P('dp', None, 'tensor'), may hold values from -4 to 4
- attention_out: float32 [768, 2, 768], P('dp', None, 'tensor'), may hold values from -4 to 4
- expand_weight: float32 [768, 3072], P('dp', 'tensor'), may hold values from -4 to 4
- contract_weight: float32 [768, 3072], P('dp', 'tensor'), may hold values from -4 to 4
- norm_gains: float32 [768, 3], replicated, may hold values from 0.3 to 2.4
- position_bias: float32 [32, 12], P(None, 'tensor'), may hold values from -4 to 4
- moment_attention_in: float32 [768, 6, 768], P('dp', None, 'tensor'), may hold values from -1 to 1
- square_attention_in: float32 [768, 6, 768], P('dp', None, 'tensor'), may hold values from 0 to 1, as said below
- moment_attention_out: float32 [768, 2, 768], P('dp', None, 'tensor'), may hold values from -1 to 1
- square_attention_out: float32 [768, 2, 768], P('dp', None, 'tensor'), may hold values from 0 to 1, as said below
- moment_expand: float32 [768, 3072], P('dp', 'tensor'), may hold values from -1 to 1
- square_expand: float32 [768, 3072], P('dp', 'tensor'), may hold values from 0 to 1, as said below
- moment_contract: float32 [768, 3072], P('dp', 'tensor'), may hold values from -1 to 1
- square_contract: float32 [768, 3072], P('dp', 'tensor'), may hold values from 0 to 1, as said below
- moment_gains: float32 [768, 3], P('dp'), may hold values from -1 to 1
- square_gains: float32 [768, 3], P('dp'), may hold values from 0 to 1, as said below
- moment_bias: float32 [32, 12], P(None, 'tensor'), may hold values from -1 to 1
- square_bias: float32 [32, 12], P(None, 'tensor'), may hold values from 0 to 1, as said below
Outputs:
- output: float32 [64, 288, 768], P(('dp', 'tensor'))
- input_grad: float32 [64, 288, 768], P('dp')
- memory_grad: float32 [64, 1024, 768], P(('dp', 'tensor'))
- grad_norm: float32 [], replicated
- new_moment_attention_in: float32 [768, 6, 768], P('dp', None, 'tensor')
- new_square_attention_in: float32 [768, 6, 768], P('dp', None, 'tensor')
- new_attention_in: float32 [768, 6, 768], P('dp', None, 'tensor')
- new_moment_attention_out: float32 [768, 2, 768], P('dp', None, 'tensor')
- new_square_attention_out: float32 [768, 2, 768], P('dp', None, 'tensor')
- new_attention_out: float32 [768, 2, 768], P('dp', None, 'tensor')
- new_moment_expand: float32 [768, 3072], P('dp', 'tensor')
- new_square_expand: float32 [768, 3072], P('dp', 'tensor')
- new_expand_weight: float32 [768, 3072], P('dp', 'tensor')
- new_moment_contract: float32 [768, 3072], P('dp', 'tensor')
- new_square_contract: float32 [768, 3072], P('dp', 'tensor')
- new_contract_weight: float32 [768, 3072], P('dp', 'tensor')
- new_moment_gains: float32 [768, 3], P('dp')
- new_square_gains: float32 [768, 3], P('dp')
- new_norm_gains: float32 [768, 3], P('dp')
- new_moment_bias: float32 [32, 12], P(None, 'tensor')
- new_square_bias: float32 [32, 12], P(None, 'tensor')
- new_position_bias: float32 [32, 12], P(None, 'tensor')
The draws below stay inside these ranges and needn't reach their ends.
Inputs may be any that keep to these rules, and one draw needn't show every extreme that they name: `dec_segments`: in every row the ids never fall, start at 0 and end at 3, so each of the 4 documents holds one or more decoder positions. `mem_segments`: in every row the ids never fall and start at 0; memory document s belongs to decoder document s of the same row; every document has one or more positions below the row's mem_lengths entry, and positions at or past it carry 4 - 1. `mem_lengths`: among each device's 4 rows one has length 1024. `buckets`: entry d is d for d < 16, never falls as d grows, and is 31 for d >= 128. `square_attention_in`: Positive. `square_attention_out`: Positive. `square_expand`: Positive. `square_contract`: Positive. `square_gains`: Positive. `square_bias`: Positive.
All inputs are finite; a program needn't handle non-finite values.
Results may differ from the reference program's by a relative error of at most 0.022.
Values may be sent and summed in bfloat16 or wider, within the bound.
No kernel may reach another device: no remote copies, remote signals or barrier semaphores. Data moves between devices by JAX's collectives and lax.ppermute only.
A program may use at most 256 MiB of HBM per device.

```python
import math
import jax
import jax.numpy as jnp
from jax import lax

D = 768
H = 12
DH = 64
FF = 3072
BUCKETS = 32
MAXDIST = 128
DEC_LEN = 288
MEM_LEN = 1024
SEGS = 4
STEP = 10
ROWS_DEV = 4
ROWS = 64
PARAMS = 9439872


CLIP_NORM = 1.0


def rising(number, first_value, last_value):
    return first_value + (last_value - first_value) * jnp.arange(number, dtype=jnp.float32) / max(number - 1, 1)


def spread_log(key, array_shape, lowest, largest):
    return jnp.exp(jax.random.uniform(key, array_shape, jnp.float32, math.log(lowest), math.log(largest)))


def bounded_normal(key, array_shape):
    return jax.random.truncated_normal(key, -3.0, 3.0, array_shape, jnp.float32)


def entry_size(factor):
    return factor * CLIP_NORM / math.sqrt(PARAMS)


def first_moment(key, array_shape, factor):
    return bounded_normal(key, array_shape) * (0.1 / 0.9) * entry_size(factor)


def second_moment(key, array_shape, factor):
    return spread_log(key, array_shape, 1.0, 4.0) * (0.05 / 0.95) * entry_size(factor) ** 2


def packing(key):
    length_key, full_key, decoder_key, memory_key = jax.random.split(key, 4)
    half_memory = MEM_LEN // 2
    lengths = MEM_LEN - jax.random.randint(length_key, (ROWS,), 0, half_memory + 1)
    chosen = jax.random.randint(full_key, (ROWS // ROWS_DEV, 1), 0, ROWS_DEV)
    full_row = (jnp.arange(ROWS_DEV, dtype=jnp.int32)[None, :] == chosen).reshape(ROWS)
    lengths = jnp.where(full_row, MEM_LEN, lengths).astype(jnp.int32)
    decoder_cuts = 1 + jax.vmap(lambda row_key: jax.random.permutation(row_key, DEC_LEN - 1)[:SEGS - 1])(jax.random.split(decoder_key, ROWS))
    memory_marks = 1 + jax.vmap(lambda row_key: jax.random.permutation(row_key, half_memory - 1)[:SEGS - 1])(jax.random.split(memory_key, ROWS))
    memory_cuts = memory_marks * lengths[:, None] // half_memory
    decoder_places = jnp.arange(DEC_LEN, dtype=jnp.int32)
    memory_places = jnp.arange(MEM_LEN, dtype=jnp.int32)
    decoder_ids = jnp.sum((decoder_cuts[:, None, :] <= decoder_places[None, :, None]).astype(jnp.int32), axis=2)
    memory_ids = jnp.sum((memory_cuts[:, None, :] <= memory_places[None, :, None]).astype(jnp.int32), axis=2)
    return (decoder_ids.astype(jnp.int32), memory_ids.astype(jnp.int32), lengths)


def draw_dec_segments(key, part):
    shared = packing(key)
    return shared[0]


def draw_mem_segments(key, part):
    shared = packing(key)
    return shared[1]


def draw_mem_lengths(key, part):
    shared = packing(key)
    return shared[2]


def draw_inputs(key, part):
    key = jax.random.fold_in(key, 1)
    base_key, row_key, column_key, common_key = jax.random.split(key, 4)
    row_scale = spread_log(row_key, (ROWS, DEC_LEN, 1), 0.4, 4.0)
    column_scale = spread_log(column_key, (D,), 0.5, 2.0)
    base_draw = jax.random.truncated_normal(base_key, -4.0, 4.0, (ROWS, DEC_LEN, D), jnp.float32)
    return (base_draw * row_scale * column_scale).astype(jnp.bfloat16)


def draw_memory(key, part):
    key = jax.random.fold_in(key, 2)
    base_draw = jax.random.truncated_normal(key, -4.0, 4.0, (ROWS, MEM_LEN, D), jnp.float32) * rising(D, 0.6, 1.8)
    return base_draw.astype(jnp.bfloat16)


def draw_cotangent(key, part):
    key = jax.random.fold_in(key, 3)
    base_draw = jax.random.truncated_normal(key, -4.0, 4.0, (ROWS, DEC_LEN, D), jnp.float32) * rising(D, 0.6, 1.8)
    return base_draw.astype(jnp.bfloat16)


def draw_buckets(key, part):
    key = jax.random.fold_in(key, 4)
    half_buckets = BUCKETS // 2
    shuffled = jax.random.permutation(key, MAXDIST - half_buckets - 1)
    bounds = half_buckets + 1 + shuffled[:half_buckets - 1]
    distance = jnp.arange(DEC_LEN, dtype=jnp.int32)
    far_bucket = half_buckets + jnp.sum((bounds[None, :] <= distance[:, None]).astype(jnp.int32), axis=1)
    return jnp.where(distance < half_buckets, distance, far_bucket).astype(jnp.int32)


def draw_attention_in(key, part):
    key = jax.random.fold_in(key, 5)
    features = H * DH
    query_scale = (D * DH) ** (-0.5)
    other_scale = D ** (-0.5)
    scales = jnp.array([query_scale, other_scale, other_scale, query_scale, other_scale, other_scale], jnp.float32)
    ramp_factor = jnp.where((jnp.arange(6) % 3 == 2)[:, None], rising(features, 0.6, 1.6)[None, :], 1.0)
    return bounded_normal(key, (D, 6, features)) * scales[None, :, None] * ramp_factor[None]


def draw_attention_out(key, part):
    key = jax.random.fold_in(key, 6)
    features = H * DH
    scales = jnp.array([(features // 16) ** (-0.5), (features // 32) ** (-0.5)], jnp.float32)
    return bounded_normal(key, (D, 2, features)) * scales[None, :, None] * rising(features, 0.6, 1.6)[None, None, :]


def draw_expand_weight(key, part):
    key = jax.random.fold_in(key, 7)
    return bounded_normal(key, (D, FF)) * D ** (-0.5) * rising(FF, 0.6, 1.6)[None, :]


def draw_contract_weight(key, part):
    key = jax.random.fold_in(key, 8)
    return bounded_normal(key, (D, FF)) * FF ** (-0.5) * rising(FF, 0.6, 1.6)[None, :]


def draw_norm_gains(key, part):
    key = jax.random.fold_in(key, 9)
    noise = jax.random.truncated_normal(key, -2.0, 2.0, (D, 3), jnp.float32)
    return rising(D, 0.6, 1.8)[:, None] * (1.0 + 0.1 * noise)


def draw_moment_attention_in(key, part):
    key = jax.random.fold_in(key, 10)
    return first_moment(key, (D, 6, H * DH), 1.0)


def draw_square_attention_in(key, part):
    key = jax.random.fold_in(key, 11)
    return second_moment(key, (D, 6, H * DH), 1.0)


def draw_moment_attention_out(key, part):
    key = jax.random.fold_in(key, 12)
    return first_moment(key, (D, 2, H * DH), 0.1)


def draw_square_attention_out(key, part):
    key = jax.random.fold_in(key, 13)
    return second_moment(key, (D, 2, H * DH), 0.1)


def draw_moment_expand(key, part):
    key = jax.random.fold_in(key, 14)
    return first_moment(key, (D, FF), 0.06)


def draw_square_expand(key, part):
    key = jax.random.fold_in(key, 15)
    return second_moment(key, (D, FF), 0.06)


def draw_moment_contract(key, part):
    key = jax.random.fold_in(key, 16)
    return first_moment(key, (D, FF), 0.12)


def draw_square_contract(key, part):
    key = jax.random.fold_in(key, 17)
    return second_moment(key, (D, FF), 0.12)


def draw_moment_gains(key, part):
    key = jax.random.fold_in(key, 18)
    return first_moment(key, (D, 3), 0.3)


def draw_square_gains(key, part):
    key = jax.random.fold_in(key, 19)
    return second_moment(key, (D, 3), 0.3)


def draw_moment_bias(key, part):
    key = jax.random.fold_in(key, 20)
    return first_moment(key, (BUCKETS, H), 0.25)


def draw_square_bias(key, part):
    key = jax.random.fold_in(key, 21)
    return second_moment(key, (BUCKETS, H), 0.25)


def level_of(own_key, dims, cuts, low, high):
    factor_of = 1.0
    for dim, shards_of in cuts:
        heights = jax.random.uniform(jax.random.fold_in(jax.random.fold_in(own_key, 6), dim), (shards_of,), jnp.float32, low / len(cuts), high / len(cuts))
        factor_of = factor_of * jnp.repeat(jnp.exp(heights), dims[dim] // shards_of).reshape((-1,) + (1,) * (len(dims) - 1 - dim))
    return factor_of


def scatter_about(own_key, shape, width, reach, shards=(), kind=jnp.bfloat16):
    values = jax.random.normal(own_key, shape, jnp.float32) * width
    if len(shards) > 0:
        values = level_of(own_key, shape, shards, -0.22, 0.18) * values
    return jnp.clip(values, min=-reach, max=reach).astype(kind)


def setup_inputs(seed: int = 0) -> dict:
    streams_of = jax.random.split(jax.random.key(seed), 26)
    inputs = draw_inputs(jax.random.fold_in(streams_of[25], 71), 0)
    memory = draw_memory(jax.random.fold_in(streams_of[25], 71), 0)
    dec_segments = draw_dec_segments(jax.random.fold_in(streams_of[25], 71), 0)
    mem_segments = draw_mem_segments(jax.random.fold_in(streams_of[25], 71), 0)
    mem_lengths = draw_mem_lengths(jax.random.fold_in(streams_of[25], 71), 0)
    buckets = draw_buckets(jax.random.fold_in(streams_of[25], 71), 0)
    cotangent = draw_cotangent(jax.random.fold_in(streams_of[25], 71), 0)
    attention_in = draw_attention_in(jax.random.fold_in(streams_of[25], 71), 0)
    attention_out = draw_attention_out(jax.random.fold_in(streams_of[25], 71), 0)
    expand_weight = draw_expand_weight(jax.random.fold_in(streams_of[25], 71), 0)
    contract_weight = draw_contract_weight(jax.random.fold_in(streams_of[25], 71), 0)
    norm_gains = draw_norm_gains(jax.random.fold_in(streams_of[25], 71), 0)
    position_bias = scatter_about(streams_of[12], (BUCKETS, H), 1.0, 4.0, ((1, 2),), jnp.float32)
    moment_attention_in = draw_moment_attention_in(jax.random.fold_in(streams_of[25], 71), 0)
    square_attention_in = draw_square_attention_in(jax.random.fold_in(streams_of[25], 71), 0)
    moment_attention_out = draw_moment_attention_out(jax.random.fold_in(streams_of[25], 71), 0)
    square_attention_out = draw_square_attention_out(jax.random.fold_in(streams_of[25], 71), 0)
    moment_expand = draw_moment_expand(jax.random.fold_in(streams_of[25], 71), 0)
    square_expand = draw_square_expand(jax.random.fold_in(streams_of[25], 71), 0)
    moment_contract = draw_moment_contract(jax.random.fold_in(streams_of[25], 71), 0)
    square_contract = draw_square_contract(jax.random.fold_in(streams_of[25], 71), 0)
    moment_gains = draw_moment_gains(jax.random.fold_in(streams_of[25], 71), 0)
    square_gains = draw_square_gains(jax.random.fold_in(streams_of[25], 71), 0)
    moment_bias = draw_moment_bias(jax.random.fold_in(streams_of[25], 71), 0)
    square_bias = draw_square_bias(jax.random.fold_in(streams_of[25], 71), 0)
    return {"inputs": inputs, "memory": memory, "dec_segments": dec_segments, "mem_segments": mem_segments, "mem_lengths": mem_lengths, "buckets": buckets, "cotangent": cotangent, "attention_in": attention_in, "attention_out": attention_out, "expand_weight": expand_weight, "contract_weight": contract_weight, "norm_gains": norm_gains, "position_bias": position_bias, "moment_attention_in": moment_attention_in, "square_attention_in": square_attention_in, "moment_attention_out": moment_attention_out, "square_attention_out": square_attention_out, "moment_expand": moment_expand, "square_expand": square_expand, "moment_contract": moment_contract, "square_contract": square_contract, "moment_gains": moment_gains, "square_gains": square_gains, "moment_bias": moment_bias, "square_bias": square_bias}


NORM_EPS = 1e-06
MASKED = -1e+30
CLIP_NORM = 1.0
BETA_ONE = 0.9
BETA_TWO = 0.95
ADAM_EPS = 1e-08
MATRIX_RATE = 0.08
SMALL_RATE = 0.8
DECAY_RATE = 0.1
GELU_SCALE = 0.7978845608028654
GELU_CUBIC = 0.044715

@jax.custom_vjp
def lower_projection(v):
    return lax.optimization_barrier(v.astype(jnp.bfloat16)).astype(jnp.float32)

@jax.custom_vjp
def lower_projection_back(v):
    return v

def low_keep(v):
    return (lower_projection(v), None)

def low_pass(kept, grad):
    return (grad,)

def back_keep(v):
    return (v, None)

def back_low(kept, grad):
    return (lower_projection(grad),)
lower_projection.defvjp(low_keep, low_pass)
lower_projection_back.defvjp(back_keep, back_low)

def topmost_bucket(pattern, left_side, right_side):
    return jnp.einsum(pattern, left_side, right_side, precision=lax.Precision.HIGHEST, preferred_element_type=jnp.float32)

def gelu_tanh(values):
    return 0.5 * values * (1.0 + jnp.tanh(GELU_SCALE * (values + GELU_CUBIC * values * values * values)))

def normalize(hidden, gain_column):
    factor = lax.rsqrt(lax.optimization_barrier(jnp.mean(hidden * hidden, axis=-1, keepdims=True)) + NORM_EPS)
    return hidden * factor * gain_column

def attend(queries, keys_in, values_in, extra_bias, allowed):
    scores = lower_projection_back(topmost_bucket('rqhd,rkhd->rhqk', queries, keys_in) + extra_bias)
    scores = jnp.where(allowed, scores, MASKED)
    exponent = jnp.exp(scores - lax.optimization_barrier(jnp.max(scores, axis=-1, keepdims=True)))
    probabilities = exponent / lax.optimization_barrier(jnp.sum(exponent, axis=-1, keepdims=True))
    mixture = topmost_bucket('rhqk,rkhd->rqhd', lower_projection(probabilities), values_in)
    return lower_projection_back(lower_projection(mixture))

def layer(params, hidden_zero, memory_portion, decoder_ids, memory_ids, lengths_part, buckets):
    input_kernel_list, out_kernels, up_kernel, down_kernel, gains, position_bias = params
    block_rows, length = (hidden_zero.shape[0], hidden_zero.shape[1])
    positions = jnp.arange(length, dtype=jnp.int32)
    distance = positions[:, None] - positions[None, :]
    self_extra = jnp.transpose(position_bias[buckets[jnp.maximum(distance, 0)]], (2, 0, 1))[None]
    self_allowed = ((distance >= 0)[None] & (decoder_ids[:, :, None] == decoder_ids[:, None, :]))[:, None]
    first_normalized = lower_projection(normalize(hidden_zero, gains[:, 0]))
    self_head_split = lower_projection_back(lower_projection(topmost_bucket('nmq,qfw->fnmw', first_normalized, input_kernel_list[:, 0:3])))
    self_head_split = self_head_split.reshape(3, block_rows, length, H, DH)
    self_mixed = attend(self_head_split[0], self_head_split[1], self_head_split[2], self_extra, self_allowed)
    self_term = lower_projection_back(topmost_bucket('rle,de->rld', self_mixed.reshape(block_rows, length, H * DH), out_kernels[:, 0]))
    hidden_one = hidden_zero + self_term
    normed_one = lower_projection(normalize(hidden_one, gains[:, 1]))
    cross_query = lower_projection_back(lower_projection(topmost_bucket('rld,de->rle', normed_one, input_kernel_list[:, 3])))
    cross_query = cross_query.reshape(block_rows, length, H, DH)
    memory_head_split = lower_projection_back(lower_projection(topmost_bucket('oah,hjy->joay', memory_portion, input_kernel_list[:, 4:6])))
    memory_head_split = memory_head_split.reshape(2, block_rows, memory_portion.shape[1], H, DH)
    key_index = jnp.arange(memory_portion.shape[1], dtype=jnp.int32)
    same_doc = decoder_ids[:, :, None] == memory_ids[:, None, :]
    live_keys = key_index[None, None, :] < lengths_part[:, None, None]
    cross_allowed = (same_doc & live_keys)[:, None]
    cross_mixed = attend(cross_query, memory_head_split[0], memory_head_split[1], 0.0, cross_allowed)
    cross_term = lower_projection_back(topmost_bucket('rle,de->rld', cross_mixed.reshape(block_rows, length, H * DH), out_kernels[:, 1]))
    hidden_two = hidden_one + cross_term
    normed_two = lower_projection(normalize(hidden_two, gains[:, 2]))
    preactivation = lower_projection_back(topmost_bucket('rld,df->rlf', normed_two, up_kernel))
    activated = lower_projection(gelu_tanh(preactivation))
    return hidden_two + topmost_bucket('rlf,df->rld', activated, down_kernel)

def adam_update(weight, gradient, moment, square, learn_rate, weight_decay):
    new_moment = BETA_ONE * moment + (1.0 - BETA_ONE) * gradient
    new_square = BETA_TWO * square + (1.0 - BETA_TWO) * gradient * gradient
    direction = new_moment / (1.0 - BETA_ONE ** STEP) / (jnp.sqrt(new_square / (1.0 - BETA_TWO ** STEP)) + ADAM_EPS)
    return (new_moment, new_square, weight - learn_rate * (direction + weight_decay * weight))

def reference(inputs, memory, dec_segments, mem_segments, mem_lengths, buckets, cotangent, attention_in, attention_out, expand_weight, contract_weight, norm_gains, position_bias, moment_attention_in, square_attention_in, moment_attention_out, square_attention_out, moment_expand, square_expand, moment_contract, square_contract, moment_gains, square_gains, moment_bias, square_bias):
    params = (attention_in, attention_out, expand_weight, contract_weight, norm_gains, position_bias)

    def blocked(values):
        return values.reshape((values.shape[0] // ROWS_DEV, ROWS_DEV) + values.shape[1:])

    def forward(weights, hidden, memory_in):
        rounded = (lower_projection(weights[0]), lower_projection(weights[1]), lower_projection(weights[2]), lower_projection(weights[3]), weights[4], weights[5])

        def run_block(pieces):
            return layer(rounded, pieces[0], pieces[1], pieces[2], pieces[3], pieces[4], buckets)
        results = lax.map(jax.checkpoint(run_block), (blocked(hidden), blocked(memory_in), blocked(dec_segments), blocked(mem_segments), blocked(mem_lengths)))
        return results.reshape(hidden.shape)
    output, pullback = jax.vjp(forward, params, inputs.astype(jnp.float32), memory.astype(jnp.float32))
    slopes, input_grad, memory_grad = pullback(cotangent.astype(jnp.float32))
    square_sum = sum((jnp.sum(member * member) for member in slopes))
    grad_norm = jnp.sqrt(square_sum)
    clip_factor = jnp.minimum(1.0, CLIP_NORM / (grad_norm + 1e-06))
    new_moment_attention_in, new_square_attention_in, new_attention_in = adam_update(attention_in, slopes[0] * clip_factor, moment_attention_in, square_attention_in, MATRIX_RATE, DECAY_RATE)
    new_moment_attention_out, new_square_attention_out, new_attention_out = adam_update(attention_out, slopes[1] * clip_factor, moment_attention_out, square_attention_out, MATRIX_RATE, DECAY_RATE)
    new_moment_expand, new_square_expand, new_expand_weight = adam_update(expand_weight, slopes[2] * clip_factor, moment_expand, square_expand, MATRIX_RATE, DECAY_RATE)
    new_moment_contract, new_square_contract, new_contract_weight = adam_update(contract_weight, slopes[3] * clip_factor, moment_contract, square_contract, MATRIX_RATE, DECAY_RATE)
    new_moment_gains, new_square_gains, new_norm_gains = adam_update(norm_gains, slopes[4] * clip_factor, moment_gains, square_gains, SMALL_RATE, 0.0)
    new_moment_bias, new_square_bias, new_position_bias = adam_update(position_bias, slopes[5] * clip_factor, moment_bias, square_bias, SMALL_RATE, 0.0)
    return (output, input_grad, memory_grad, grad_norm, new_moment_attention_in, new_square_attention_in, new_attention_in, new_moment_attention_out, new_square_attention_out, new_attention_out, new_moment_expand, new_square_expand, new_expand_weight, new_moment_contract, new_square_contract, new_contract_weight, new_moment_gains, new_square_gains, new_norm_gains, new_moment_bias, new_square_bias, new_position_bias)
```

```python
import jax
import jax.numpy as jnp
from jax import lax
from jax.experimental import pallas as pl
from jax.experimental.pallas import tpu as pltpu
from jax.sharding import PartitionSpec as P

STEP = 10
NORM_EPS = 1e-06
CLIP_NORM = 1.0
BETA_ONE = 0.9
BETA_TWO = 0.95
ADAM_EPS = 1e-08
MATRIX_RATE = 0.08
SMALL_RATE = 0.8
DECAY_RATE = 0.1
GELU_SCALE = 0.7978845608028654
GELU_CUBIC = 0.044715
MASKED = -1e30
TABLE = 384
NT = (((1,), (1,)), ((), ()))
TN = (((0,), (0,)), ((), ()))


def dot(a, b, dims=(((1,), (0,)), ((), ()))):
    return lax.dot_general(a, b, dims, preferred_element_type=jnp.float32)


def lanes(shape):
    return lax.broadcasted_iota(jnp.int32, shape, len(shape) - 1)


def half_of(values, which):
    return jnp.where((lanes(values.shape) >= 64) == (which == 1), values, jnp.zeros_like(values))


def column(values, index):
    return jnp.sum(jnp.where(lanes(values.shape) == index, values, 0.0), axis=-1, keepdims=True)


def cross_forward_kernel(q_ref, k_ref, v_ref, dec_ref, mem_ref, o_ref, lse_ref):
    pair = pl.program_id(1)
    query, key, value = q_ref[0], k_ref[0], v_ref[0]
    allowed = dec_ref[0] == mem_ref[0]
    mixed, logs = forward_pair(query, key, value, [None, None], allowed)
    o_ref[0] = mixed.astype(o_ref.dtype)
    store_logs(lse_ref, logs, pair)


def store_logs(lse_ref, logs, pair):
    @pl.when(pair == 0)
    def _():
        lse_ref[0] = jnp.zeros(lse_ref.shape[1:], jnp.float32)

    lane = lanes(lse_ref.shape[1:])
    kept = lse_ref[0]
    for which in range(2):
        kept = jnp.where(lane == 2 * pair + which, logs[which], kept)
    lse_ref[0] = kept


def forward_pair(query, key, value, biases, allowed):
    mixed = jnp.zeros(query.shape, jnp.float32)
    logs = []
    for which in range(2):
        scores = dot(half_of(query, which), key, NT)
        if biases[which] is not None:
            scores = scores + biases[which]
        scores = jnp.where(allowed, scores, MASKED)
        top = jnp.max(scores, axis=-1, keepdims=True)
        weights = jnp.exp(scores - top)
        total = jnp.sum(weights, axis=-1, keepdims=True)
        logs.append(top + jnp.log(total))
        mixed = mixed + dot(weights.astype(jnp.bfloat16), half_of(value, which)) * (1.0 / total)
    return mixed, logs


def backward_pair(query, key, value, mixed, upstream, logs, biases, allowed):
    slope_q = jnp.zeros(query.shape, jnp.float32)
    slope_k = jnp.zeros(key.shape, jnp.float32)
    slope_v = jnp.zeros(key.shape, jnp.float32)
    grads = []
    product = upstream.astype(jnp.float32) * mixed.astype(jnp.float32)
    for which in range(2):
        query_half = half_of(query, which)
        up_half = half_of(upstream, which)
        scores = dot(query_half, key, NT)
        if biases[which] is not None:
            scores = scores + biases[which]
        prob = jnp.exp(jnp.where(allowed, scores - logs[which], MASKED))
        slope_p = dot(up_half, value, NT)
        inner = jnp.sum(half_of(product, which), axis=-1, keepdims=True)
        grad = (prob * (slope_p - inner)).astype(jnp.bfloat16)
        slope_q = slope_q + dot(grad, half_of(key, which))
        slope_k = slope_k + dot(grad, query_half, TN)
        slope_v = slope_v + dot(prob.astype(jnp.bfloat16), up_half, TN)
        grads.append(grad)
    return slope_q, slope_k, slope_v, grads


def cross_backward_kernel(
    q_ref, k_ref, v_ref, dec_ref, mem_ref, o_ref, lse_ref, up_ref, dq_ref, dk_ref, dv_ref
):
    pair = pl.program_id(1)
    allowed = dec_ref[0] == mem_ref[0]
    logs = [column(lse_ref[0], 2 * pair + which) for which in range(2)]
    slope_q, slope_k, slope_v, _ = backward_pair(
        q_ref[0], k_ref[0], v_ref[0], o_ref[0], up_ref[0], logs, [None, None], allowed
    )
    dq_ref[0] = slope_q.astype(jnp.bfloat16)
    dk_ref[0] = slope_k.astype(jnp.bfloat16)
    dv_ref[0] = slope_v.astype(jnp.bfloat16)


def pad_keys(values):
    extra = TABLE - values.shape[0]
    return jnp.concatenate([values, jnp.zeros((extra, values.shape[1]), values.dtype)], axis=0)


def self_allowed(dec_ref, decT_ref):
    length = dec_ref.shape[1]
    rows = lax.broadcasted_iota(jnp.int32, (length, TABLE), 0)
    return (dec_ref[0] == decT_ref[0]) & (lanes((length, TABLE)) <= rows)


def toeplitz(table_ref, which, length):
    spread = jnp.broadcast_to(table_ref[0, which : which + 1, :], (length, TABLE))
    return pltpu.roll(spread, 0, 1, stride=1, stride_axis=0)


def self_forward_kernel(q_ref, k_ref, v_ref, dec_ref, decT_ref, table_ref, o_ref, lse_ref):
    pair = pl.program_id(1)
    length = q_ref.shape[1]
    biases = [toeplitz(table_ref, which, length) for which in range(2)]
    mixed, logs = forward_pair(
        q_ref[0], pad_keys(k_ref[0]), pad_keys(v_ref[0]), biases, self_allowed(dec_ref, decT_ref)
    )
    o_ref[0] = mixed.astype(o_ref.dtype)
    store_logs(lse_ref, logs, pair)


def self_backward_kernel(
    q_ref, k_ref, v_ref, dec_ref, decT_ref, table_ref, o_ref, lse_ref, up_ref,
    dq_ref, dk_ref, dv_ref, diag_ref,
):
    pair, row = pl.program_id(0), pl.program_id(1)
    length = q_ref.shape[1]
    biases = [toeplitz(table_ref, which, length) for which in range(2)]
    logs = [column(lse_ref[0], 2 * pair + which) for which in range(2)]
    slope_q, slope_k, slope_v, grads = backward_pair(
        q_ref[0], pad_keys(k_ref[0]), pad_keys(v_ref[0]), o_ref[0], up_ref[0], logs, biases,
        self_allowed(dec_ref, decT_ref),
    )
    dq_ref[0] = slope_q.astype(jnp.bfloat16)
    dk_ref[0] = slope_k[:length].astype(jnp.bfloat16)
    dv_ref[0] = slope_v[:length].astype(jnp.bfloat16)

    @pl.when(row == 0)
    def _():
        diag_ref[...] = jnp.zeros(diag_ref.shape, jnp.float32)

    for which in range(2):
        diag_ref[0, which : which + 1, :] += diagonal_sums(grads[which].astype(jnp.float32))


def diagonal_sums(values):
    groups = jnp.zeros((8, TABLE), jnp.float32)
    for start in range(0, values.shape[0], 8):
        groups = groups + pltpu.roll(values[start : start + 8], (TABLE - start) % TABLE, 1)
    total = groups[0:1]
    for row in range(1, 8):
        total = total + pltpu.roll(groups, TABLE - row, 1)[row : row + 1]
    return total


def params(count):
    return pltpu.CompilerParams(
        dimension_semantics=("arbitrary",) * count, vmem_limit_bytes=48 * 1024 * 1024
    )


def cross_forward(q, kv, dec, mem):
    rows, length, width = q.shape
    keys = kv.shape[1]
    pairs = width // 128
    lanes_q = pl.BlockSpec((1, length, 128), lambda r, p: (r, 0, p))
    lanes_k = pl.BlockSpec((1, keys, 128), lambda r, p: (r, 0, p))
    lanes_v = pl.BlockSpec((1, keys, 128), lambda r, p: (r, 0, p + pairs))
    return pl.pallas_call(
        cross_forward_kernel,
        grid=(rows, width // 128),
        in_specs=[
            lanes_q, lanes_k, lanes_v,
            pl.BlockSpec((1, length, 1), lambda r, p: (r, 0, 0)),
            pl.BlockSpec((1, 1, keys), lambda r, p: (r, 0, 0)),
        ],
        out_specs=[lanes_q, pl.BlockSpec((1, length, 128), lambda r, p: (r, 0, 0))],
        out_shape=[
            jax.ShapeDtypeStruct((rows, length, width), jnp.bfloat16),
            jax.ShapeDtypeStruct((rows, length, 128), jnp.float32),
        ],
        compiler_params=params(2),
        cost_estimate=cost(4 * rows * length * keys * width, 2 * rows * width * (2 * length + 2 * keys), 2 * rows * length * keys * pairs),
        name="cross_forward",
    )(q, kv, kv, dec, mem)


def cross_backward(q, kv, dec, mem, mixed, logs, upstream):
    rows, length, width = q.shape
    keys = kv.shape[1]
    pairs = width // 128
    lanes_q = pl.BlockSpec((1, length, 128), lambda r, p: (r, 0, p))
    lanes_k = pl.BlockSpec((1, keys, 128), lambda r, p: (r, 0, p))
    lanes_v = pl.BlockSpec((1, keys, 128), lambda r, p: (r, 0, p + pairs))
    return pl.pallas_call(
        cross_backward_kernel,
        grid=(rows, width // 128),
        in_specs=[
            lanes_q, lanes_k, lanes_v,
            pl.BlockSpec((1, length, 1), lambda r, p: (r, 0, 0)),
            pl.BlockSpec((1, 1, keys), lambda r, p: (r, 0, 0)),
            lanes_q, pl.BlockSpec((1, length, 128), lambda r, p: (r, 0, 0)), lanes_q,
        ],
        out_specs=[lanes_q, lanes_k, lanes_k],
        out_shape=[
            jax.ShapeDtypeStruct((rows, length, width), jnp.bfloat16),
            jax.ShapeDtypeStruct((rows, keys, width), jnp.bfloat16),
            jax.ShapeDtypeStruct((rows, keys, width), jnp.bfloat16),
        ],
        compiler_params=params(2),
        cost_estimate=cost(10 * rows * length * keys * width, 2 * rows * width * (4 * length + 4 * keys), 2 * rows * length * keys * pairs),
        name="cross_backward",
    )(q, kv, kv, dec, mem, mixed, logs, upstream)


def self_forward(qkv, dec, decT, table):
    rows, length, width = qkv.shape
    width = width // 3
    pairs = width // 128
    spec = pl.BlockSpec((1, length, 128), lambda r, p: (r, 0, p))
    spec_k = pl.BlockSpec((1, length, 128), lambda r, p: (r, 0, p + pairs))
    spec_v = pl.BlockSpec((1, length, 128), lambda r, p: (r, 0, p + 2 * pairs))
    return pl.pallas_call(
        self_forward_kernel,
        grid=(rows, pairs),
        in_specs=[
            spec, spec_k, spec_v,
            pl.BlockSpec((1, length, 1), lambda r, p: (r, 0, 0)),
            pl.BlockSpec((1, 1, TABLE), lambda r, p: (r, 0, 0)),
            pl.BlockSpec((1, 2, TABLE), lambda r, p: (p, 0, 0)),
        ],
        out_specs=[spec, pl.BlockSpec((1, length, 128), lambda r, p: (r, 0, 0))],
        out_shape=[
            jax.ShapeDtypeStruct((rows, length, width), jnp.bfloat16),
            jax.ShapeDtypeStruct((rows, length, 128), jnp.float32),
        ],
        compiler_params=params(2),
        cost_estimate=cost(4 * rows * length * TABLE * width, 8 * rows * width * length, 2 * rows * length * TABLE * pairs),
        name="self_forward",
    )(qkv, qkv, qkv, dec, decT, table)


def self_backward(qkv, dec, decT, table, mixed, logs, upstream):
    rows, length, width = qkv.shape
    width = width // 3
    pairs = width // 128
    spec = pl.BlockSpec((1, length, 128), lambda p, r: (r, 0, p))
    spec_k = pl.BlockSpec((1, length, 128), lambda p, r: (r, 0, p + pairs))
    spec_v = pl.BlockSpec((1, length, 128), lambda p, r: (r, 0, p + 2 * pairs))
    table_spec = pl.BlockSpec((1, 2, TABLE), lambda p, r: (p, 0, 0))
    out = jax.ShapeDtypeStruct((rows, length, width), jnp.bfloat16)
    return pl.pallas_call(
        self_backward_kernel,
        grid=(pairs, rows),
        in_specs=[
            spec, spec_k, spec_v,
            pl.BlockSpec((1, length, 1), lambda p, r: (r, 0, 0)),
            pl.BlockSpec((1, 1, TABLE), lambda p, r: (r, 0, 0)),
            table_spec, spec,
            pl.BlockSpec((1, length, 128), lambda p, r: (r, 0, 0)), spec,
        ],
        out_specs=[spec, spec, spec, table_spec],
        out_shape=[out, out, out, jax.ShapeDtypeStruct((pairs, 2, TABLE), jnp.float32)],
        compiler_params=params(2),
        cost_estimate=cost(10 * rows * length * TABLE * width, 16 * rows * width * length, 2 * rows * length * TABLE * pairs),
        name="self_backward",
    )(qkv, qkv, qkv, dec, decT, table, mixed, logs, upstream)


SLOPE = GELU_SCALE * 3.0 * GELU_CUBIC
ROW_TILE = 16
FF_TILE = 256


def whole(shape):
    return pl.BlockSpec(shape, lambda *_: (0,) * len(shape))


def cost(flops, moved, exps=0):
    return pl.CostEstimate(flops=int(flops), bytes_accessed=int(moved), transcendentals=int(exps))


def row_scale(hidden):
    return lax.rsqrt(jnp.mean(hidden * hidden, axis=-1, keepdims=True) + NORM_EPS)


def row_back(hidden, gain, upstream):
    factor = row_scale(hidden)
    scaled = upstream * hidden
    inner = jnp.mean(scaled * gain, axis=-1, keepdims=True)
    slope = factor * (upstream * gain) - (factor * factor * factor * inner) * hidden
    return slope, jnp.sum(scaled * factor, axis=0, keepdims=True)


def emit(gradient, keep_ref, send_ref, start, upper):
    halves, blocks, rows, _ = keep_ref.shape
    columns = gradient.shape[1] // halves
    for half in range(halves):
        part = gradient[:, half * columns : (half + 1) * columns]
        part = part.reshape(blocks, 2, rows, columns)
        low, high = part[:, 0], part[:, 1]
        keep = jnp.where(upper, high, low).astype(jnp.bfloat16)
        send = jnp.where(upper, low, high).astype(jnp.bfloat16)
        keep_ref[half, :, :, start : start + columns] = keep
        send_ref[half, :, :, start : start + columns] = send


def call(kernel, name, grid, in_specs, out_specs, out_shape, work, scratch=(), scalars=1):
    return pl.pallas_call(
        kernel,
        grid_spec=pltpu.PrefetchScalarGridSpec(
            num_scalar_prefetch=scalars,
            grid=grid,
            in_specs=in_specs,
            out_specs=out_specs,
            scratch_shapes=scratch,
        ),
        out_shape=out_shape,
        compiler_params=pltpu.CompilerParams(
            dimension_semantics=("arbitrary",) * len(grid), vmem_limit_bytes=56 * 1024 * 1024
        ),
        cost_estimate=work,
        name=name,
    )


def shape_of(shape, kind=jnp.bfloat16):
    return jax.ShapeDtypeStruct(shape, kind)


def project_kernel(up_ref, x_ref, gain_ref, w_ref, n_ref, out_ref):
    @pl.when(pl.program_id(0) == 0)
    def _():
        hidden = x_ref[...].astype(jnp.float32)
        n_ref[...] = (hidden * row_scale(hidden) * gain_ref[0:1]).astype(jnp.bfloat16)

    out_ref[...] = dot(n_ref[...], w_ref[...]).astype(jnp.bfloat16)


def project(upper, hidden, gains, kernels):
    tokens, width = hidden.shape
    count = kernels.shape[1] // width
    return call(
        project_kernel, "project", (count,),
        [whole((tokens, width)), whole(gains.shape), pl.BlockSpec((width, width), lambda g, *_: (0, g))],
        [whole((tokens, width)), pl.BlockSpec((tokens, width), lambda g, *_: (0, g))],
        [shape_of((tokens, width)), shape_of((tokens, count * width))],
        cost(2 * tokens * width * width * count, 2 * width * (tokens * (count + 2) + count * width)),
    )(upper, hidden, gains, kernels)


def memory_project_kernel(up_ref, x_ref, w_ref, out_ref):
    out_ref[...] = dot(x_ref[...], w_ref[...]).astype(jnp.bfloat16)


def memory_project(upper, memory, kernels):
    tokens, width = memory.shape
    wide = kernels.shape[1]
    tile = 256
    return call(
        memory_project_kernel, "memory_project", (tokens // tile,),
        [pl.BlockSpec((tile, width), lambda g, *_: (g, 0)), whole(kernels.shape)],
        pl.BlockSpec((tile, wide), lambda g, *_: (g, 0)),
        shape_of((tokens, wide)),
        cost(2 * tokens * width * wide, 2 * (tokens * (width + wide) + width * wide)),
    )(upper, memory, kernels)


def after_self_kernel(up_ref, x_ref, a_ref, gain_ref, wo_ref, wq_ref, h_ref, n_ref, q_ref):
    hidden = x_ref[...].astype(jnp.float32) + dot(a_ref[...], wo_ref[...], NT)
    h_ref[...] = hidden
    normed = (hidden * row_scale(hidden) * gain_ref[1:2]).astype(jnp.bfloat16)
    n_ref[...] = normed
    q_ref[...] = dot(normed, wq_ref[...]).astype(jnp.bfloat16)


def after_self(upper, inputs, mixed, gains, kernel_o, kernel_q):
    tokens, width = inputs.shape
    tile = tokens // 2
    rows = pl.BlockSpec((tile, width), lambda g, *_: (g, 0))
    return call(
        after_self_kernel, "after_self", (2,),
        [rows, rows, whole(gains.shape), whole(kernel_o.shape), whole(kernel_q.shape)],
        [rows, rows, rows],
        [shape_of((tokens, width), jnp.float32), shape_of((tokens, width)), shape_of((tokens, width))],
        cost(4 * tokens * width * width, tokens * width * 12 + 4 * width * width),
    )(upper, inputs, mixed, gains, kernel_o, kernel_q)


def feed_kernel(
    up_ref, h1_ref, a_ref, gy_ref, gain_ref, wo_ref, w_ref,
    y_ref, g_ref, gh_ref, ga_ref, keep_ref, send_ref, gain_out_ref,
    n_ref, nT_ref, gyT_ref, acc_ref,
):
    step = pl.program_id(0)
    tile = FF_TILE
    width = y_ref.shape[1]

    @pl.when(step == 0)
    def _():
        hidden = h1_ref[...] + dot(a_ref[...], wo_ref[...], NT)
        gh_ref[...] = hidden
        y_ref[...] = hidden
        normed = (hidden * row_scale(hidden) * gain_ref[2:3]).astype(jnp.bfloat16)
        n_ref[...] = normed
        nT_ref[...] = normed.T
        gyT_ref[...] = gy_ref[...].T
        acc_ref[...] = jnp.zeros(acc_ref.shape, jnp.float32)

    wi = w_ref[:, 0, :, :tile].reshape(width, tile)
    wf = w_ref[:, 0, :, tile:].reshape(width, tile)
    u = dot(n_ref[...], wi)
    square = u * u
    bent = jnp.tanh(u * (GELU_SCALE + (GELU_SCALE * GELU_CUBIC) * square))
    half = 0.5 + 0.5 * bent
    act = (u * half).astype(jnp.bfloat16)
    slope = half + (0.5 * u) * (1.0 - bent * bent) * (GELU_SCALE + SLOPE * square)
    gu = (dot(gy_ref[...], wf) * slope).astype(jnp.bfloat16)
    y_ref[...] += dot(act, wf, NT)
    acc_ref[...] += dot(gu, wi, NT)
    g_ref[:, 0, :, :tile] = dot(nT_ref[...], gu).reshape(g_ref.shape[0], g_ref.shape[2], tile).astype(jnp.bfloat16)
    g_ref[:, 0, :, tile:] = dot(gyT_ref[...], act).reshape(g_ref.shape[0], g_ref.shape[2], tile).astype(jnp.bfloat16)

    @pl.when(step == pl.num_programs(0) - 1)
    def _():
        back, gain = row_back(gh_ref[...], gain_ref[2:3], acc_ref[...])
        gain_out_ref[...] = gain
        total = gy_ref[...].astype(jnp.float32) + back
        gh_ref[...] = total
        low = total.astype(jnp.bfloat16)
        ga_ref[...] = dot(low, wo_ref[...]).astype(jnp.bfloat16)
        emit(dot(low.T, a_ref[...]), keep_ref, send_ref, 0, up_ref[0] == 1)


def feed_forward(upper, hidden, mixed, cotangent, gains, kernel_o, weights, split):
    tokens, width = hidden.shape
    blocks, halves, rows, wide = weights.shape
    steps = wide // (2 * FF_TILE)
    spec = pl.BlockSpec((blocks, 1, rows, 2 * FF_TILE), lambda g, *_: (0, g // steps, 0, g % steps))
    full = whole((tokens, width))
    f32 = shape_of((tokens, width), jnp.float32)
    columns = width // halves
    return call(
        feed_kernel, "feed_forward", (halves * steps,),
        [full, full, full, whole(gains.shape), whole(kernel_o.shape), spec],
        [full, spec, full, full, whole(split + (columns,)), whole(split + (columns,)), whole((1, width))],
        [f32, shape_of(weights.shape), f32, shape_of((tokens, width)),
         shape_of(split + (columns,)), shape_of(split + (columns,)), shape_of((1, width), jnp.float32)],
        cost(6 * tokens * width * halves * wide, 40 * tokens * width, tokens * halves * wide / 2),
        scratch=[
            pltpu.VMEM((tokens, width), jnp.bfloat16), pltpu.VMEM((width, tokens), jnp.bfloat16),
            pltpu.VMEM((width, tokens), jnp.bfloat16), pltpu.VMEM((tokens, width), jnp.float32),
        ],
    )(upper, hidden, mixed, cotangent, gains, kernel_o, weights)


def after_cross_kernel(
    up_ref, gq_ref, n_ref, h_ref, gh_ref, a_ref, gain_ref, wq_ref, wo_ref,
    gh1_ref, ga_ref, keep_ref, send_ref, gain_out_ref,
):
    upper = up_ref[0] == 1
    columns = keep_ref.shape[3] // 2
    back, gain = row_back(h_ref[...], gain_ref[1:2], dot(gq_ref[...], wq_ref[...], NT))
    gain_out_ref[...] = gain
    total = gh_ref[...] + back
    gh1_ref[...] = total
    low = total.astype(jnp.bfloat16)
    ga_ref[...] = dot(low, wo_ref[...]).astype(jnp.bfloat16)
    emit(dot(n_ref[...].T, gq_ref[...]), keep_ref, send_ref, 0, upper)
    emit(dot(low.T, a_ref[...]), keep_ref, send_ref, columns, upper)


def after_cross(upper, slope_q, normed, hidden, slope_hidden, mixed, gains, kernel_q, kernel_o, split):
    tokens, width = hidden.shape
    full, square = whole((tokens, width)), whole((width, width))
    piece = split + (2 * (width // split[0]),)
    return call(
        after_cross_kernel, "after_cross", (1,),
        [full, full, full, full, full, whole(gains.shape), square, square],
        [full, full, whole(piece), whole(piece), whole((1, width))],
        [shape_of((tokens, width), jnp.float32), shape_of((tokens, width)),
         shape_of(piece), shape_of(piece), shape_of((1, width), jnp.float32)],
        cost(8 * tokens * width * width, tokens * width * 24 + 8 * width * width),
    )(upper, slope_q, normed, hidden, slope_hidden, mixed, gains, kernel_q, kernel_o)


def outer_kernel(up_ref, x_ref, *refs):
    slopes, keep_ref, send_ref = refs[:-2], refs[-2], refs[-1]
    upper = up_ref[0] == 1
    columns = keep_ref.shape[3] // len(slopes)
    across = x_ref[...].T
    for place, slope in enumerate(slopes):
        emit(dot(across, slope[...]), keep_ref, send_ref, place * columns, upper)


def outer(upper, rows, slopes, split, name):
    tokens, width = rows.shape
    piece = split + (len(slopes) * (width // split[0]),)
    return call(
        outer_kernel, name, (1,),
        [whole(rows.shape)] + [whole(slope.shape) for slope in slopes],
        [whole(piece), whole(piece)],
        [shape_of(piece), shape_of(piece)],
        cost(2 * tokens * width * width * len(slopes), 2 * width * (tokens + width) * (1 + len(slopes))),
    )(upper, rows, *slopes)


def memory_back_kernel(up_ref, gk_ref, gv_ref, w_ref, out_ref):
    width = gk_ref.shape[1]
    out_ref[...] = dot(gk_ref[...], w_ref[:, :width], NT) + dot(gv_ref[...], w_ref[:, width:], NT)


def memory_back(upper, slope_k, slope_v, kernels):
    tokens, width = slope_k.shape
    tile = 256
    rows = pl.BlockSpec((tile, width), lambda g, *_: (g, 0))
    return call(
        memory_back_kernel, "memory_back", (tokens // tile,),
        [rows, rows, whole(kernels.shape)], rows, shape_of((tokens, width), jnp.float32),
        cost(4 * tokens * width * width, 8 * tokens * width + 4 * width * width),
    )(upper, slope_k, slope_v, kernels)


def input_back_kernel(up_ref, gq_ref, gk_ref, gv_ref, x_ref, gh_ref, gain_ref, w_ref, out_ref, gain_out_ref):
    width = x_ref.shape[1]
    upstream = dot(gq_ref[...], w_ref[:, :width], NT)
    upstream += dot(gk_ref[...], w_ref[:, width : 2 * width], NT)
    upstream += dot(gv_ref[...], w_ref[:, 2 * width :], NT)
    back, gain = row_back(x_ref[...].astype(jnp.float32), gain_ref[0:1], upstream)
    out_ref[...] = (gh_ref[...] + back).astype(jnp.bfloat16)
    gain_out_ref[...] = gain


def input_back(upper, slopes, inputs, slope_hidden, gains, kernels):
    tokens, width = inputs.shape
    full = whole((tokens, width))
    return call(
        input_back_kernel, "input_back", (1,),
        [full] * 5 + [whole(gains.shape), whole(kernels.shape)],
        [full, whole((1, width))],
        [shape_of((tokens, width)), shape_of((1, width), jnp.float32)],
        cost(6 * tokens * width * width, 14 * tokens * width + 6 * width * width),
    )(upper, *slopes, inputs, slope_hidden, gains, kernels)


def assemble_kernel(layout, up_ref, *refs):
    pieces, outs = refs[: len(refs) - len(layout)], refs[len(refs) - len(layout) :]
    upper = up_ref[0] == 1
    for out, group in zip(outs, layout):
        rows = out.shape[0] // 2
        for place, (source, start, columns) in enumerate(group):
            for half in range(2):
                own = pieces[2 * source][half, 0, :, start : start + columns]
                other = pieces[2 * source + 1][half, 0, :, start : start + columns]
                at = (2 * place + half) * columns
                out[:rows, at : at + columns] = jnp.where(upper, other, own)
                out[rows:, at : at + columns] = jnp.where(upper, own, other)


def assemble(upper, pairs, layout):
    _, blocks, rows, _ = pairs[0][0].shape
    pieces = [piece for pair in pairs for piece in pair]
    wides = [sum(2 * columns for _, _, columns in group) for group in layout]
    if rows % ROW_TILE:
        return [
            jnp.concatenate([assemble_plain(upper, pairs[s], b, b + n) for s, b, n in group], axis=1)
            for group in layout
        ]
    spec = lambda piece: pl.BlockSpec((2, 1) + piece.shape[2:], lambda g, *_: (0, g, 0, 0))
    return call(
        lambda *refs: assemble_kernel(layout, *refs), "assemble", (blocks,),
        [spec(piece) for piece in pieces],
        [pl.BlockSpec((2 * rows, wide), lambda g, *_: (g, 0)) for wide in wides],
        [shape_of((2 * rows * blocks, wide)) for wide in wides],
        cost(0, sum(4 * piece.size for piece in pieces)),
    )(upper, *pieces)


def assemble_plain(upper, pair, start, stop):
    own, other = pair
    both = in_order(own[..., start:stop], other[..., start:stop], upper[0] == 1, 2)
    halves, blocks, _, rows, columns = both.shape
    return jnp.transpose(both, (1, 2, 3, 0, 4)).reshape(blocks * 2 * rows, halves * columns)


def axis_bits(size):
    return size.bit_length() - 1


def swap_dp(values, bit):
    count = lax.axis_size("dp")
    return lax.ppermute(values, "dp", [(i, i ^ (1 << bit)) for i in range(count)])


def swap_tensor(values):
    return lax.ppermute(values, "tensor", [(0, 1), (1, 0)])


def bit_set(index, bit):
    return lax.rem(lax.shift_right_logical(index, bit), 2) == 1


def in_order(own, other, upper, axis):
    return jnp.where(
        upper, jnp.stack([other, own], axis=axis), jnp.stack([own, other], axis=axis)
    )


def gather_bit(values, bit, index):
    both = in_order(values, swap_dp(values, bit), bit_set(index, bit), 2)
    return both.reshape((values.shape[0], 2 * values.shape[1]) + values.shape[2:])


def gather_tensor(values):
    return jnp.concatenate([values, swap_tensor(values)], axis=0)


def gather_rows(shard, index):
    bits = axis_bits(lax.axis_size("dp"))
    values = shard[None, None]
    for bit in range(bits - 1, 1, -1):
        values = gather_bit(values, bit, index)
    cut = values.shape[-1] // 2
    first = gather_tensor(gather_bit(values[..., :cut], 1, index))
    second = gather_bit(gather_tensor(values[..., cut:]), 1, index)
    return [(part, swap_dp(part, 0)) for part in (first, second)]


def pick(values, upper, axis):
    return jnp.where(
        upper,
        lax.index_in_dim(values, 1, axis, keepdims=False),
        lax.index_in_dim(values, 0, axis, keepdims=False),
    )


def add_low(left, right):
    return left.astype(jnp.float32) + right.astype(jnp.float32)


def reduce_bit(values, bit, index):
    shape = values.shape
    values = values.astype(jnp.bfloat16).reshape((shape[0], shape[1] // 2, 2) + shape[2:])
    upper = bit_set(index, bit)
    return add_low(pick(values, upper, 2), swap_dp(pick(values, ~upper, 2), bit))


def reduce_tensor(values):
    values = values.astype(jnp.bfloat16)
    return add_low(values[0:1], swap_tensor(values[1:2]))


def scatter_group(pieces, cut, index):
    bits = axis_bits(lax.axis_size("dp"))
    values = jnp.concatenate(
        [add_low(kept, swap_dp(sent, 0)) for kept, sent in pieces], axis=-1
    ).astype(jnp.bfloat16)
    first = reduce_bit(reduce_tensor(values[..., :cut]), 1, index)
    second = reduce_tensor(reduce_bit(values[..., cut:], 1, index))
    values = jnp.concatenate([first, second], axis=-1)
    for bit in range(2, bits):
        values = reduce_bit(values, bit, index)
    return values[0, 0]


def sum_everywhere(values):
    values = values + swap_tensor(values)
    for bit in range(axis_bits(lax.axis_size("dp"))):
        values = values + swap_dp(values, bit)
    return values


def reverse_distance(table):
    return jnp.roll(table[:, ::-1], 1, axis=1)


def adam_update(weight, gradient, moment, square, learn_rate, weight_decay):
    new_moment = BETA_ONE * moment + (1.0 - BETA_ONE) * gradient
    new_square = BETA_TWO * square + (1.0 - BETA_TWO) * gradient * gradient
    direction = (
        new_moment
        / (1.0 - BETA_ONE**STEP)
        / (jnp.sqrt(new_square / (1.0 - BETA_TWO**STEP)) + ADAM_EPS)
    )
    return (new_moment, new_square, weight - learn_rate * (direction + weight_decay * weight))


def interleave(left, right):
    rows = left.shape[0]
    parts = [part.reshape(rows, -1, 1, FF_TILE) for part in (left, right)]
    return jnp.concatenate(parts, axis=2).reshape(rows, -1)


def take_apart(values):
    parts = values.reshape(values.shape[0], -1, 2, FF_TILE)
    return (
        parts[:, :, 0].reshape(values.shape[0], -1),
        parts[:, :, 1].reshape(values.shape[0], -1),
    )


def on_device(
    inputs,
    memory,
    dec_segments,
    mem_segments,
    mem_lengths,
    buckets,
    cotangent,
    attention_in,
    attention_out,
    expand_weight,
    contract_weight,
    norm_gains,
    position_bias,
    moment_attention_in,
    square_attention_in,
    moment_attention_out,
    square_attention_out,
    moment_expand,
    square_expand,
    moment_contract,
    square_contract,
    moment_gains,
    square_gains,
    moment_bias,
    square_bias,
):
    low = jnp.bfloat16
    everywhere = ("dp", "tensor")
    tensor_count = lax.axis_size("tensor")
    tensor_index = lax.axis_index("tensor")
    index = lax.axis_index("dp")
    rows = inputs.shape[0] // tensor_count
    length, width = inputs.shape[1], inputs.shape[2]
    keys = memory.shape[1]
    shard_rows = attention_in.shape[0]
    shards = width // shard_rows
    columns = attention_in.shape[2]
    aligned = shard_rows % ROW_TILE == 0
    upper = bit_set(index, 0).astype(jnp.int32)[None]
    split = (tensor_count, shards // 2, shard_rows)

    def own_rows(values):
        return lax.dynamic_slice_in_dim(values, tensor_index * rows, rows, 0)

    def flat(values):
        return values.reshape(values.shape[0] * values.shape[1], values.shape[2])

    def in_rows(values, size):
        return values.reshape(rows, size, values.shape[-1])

    wa = attention_in.astype(low)
    wo = attention_out.astype(low)
    piece_self = gather_rows(
        jnp.concatenate([wa[:, 0], wa[:, 1], wa[:, 2], wo[:, 0]], axis=1), index
    )
    piece_cross = gather_rows(
        jnp.concatenate([wa[:, 4], wa[:, 5], wa[:, 3], wo[:, 1]], axis=1), index
    )
    feed_shard = interleave(expand_weight.astype(low), contract_weight.astype(low))
    feed_weights = lax.all_gather(feed_shard, everywhere, axis=0, tiled=True).reshape(
        shards, tensor_count, shard_rows, feed_shard.shape[1]
    )
    if not aligned:
        feed_weights = jnp.transpose(feed_weights, (1, 0, 2, 3)).reshape(
            1, tensor_count, width, feed_shard.shape[1]
        )
    kernel_qkv, kernel_so = assemble(
        upper, piece_self, [[(0, 0, columns), (0, columns, columns), (1, 0, columns)], [(1, columns, columns)]]
    )
    kernel_ckv, kernel_cq, kernel_co = assemble(
        upper, piece_cross, [[(0, 0, columns), (0, columns, columns)], [(1, 0, columns)], [(1, columns, columns)]]
    )

    decoder_ids = own_rows(dec_segments)
    key_index = jnp.arange(keys, dtype=jnp.int32)
    memory_ids = jnp.where(
        key_index[None, :] < own_rows(mem_lengths)[:, None], own_rows(mem_segments), -1
    )
    dec = decoder_ids[:, :, None]
    dec_across = jnp.pad(decoder_ids, ((0, 0), (0, TABLE - length)), constant_values=-1)[:, None]
    mem_across = memory_ids[:, None]
    own_heads = position_bias.shape[1]
    heads = own_heads * tensor_count
    both_bias = jnp.concatenate([position_bias, swap_tensor(position_bias)], axis=1)
    lookup = (
        buckets[None, :] == jnp.arange(position_bias.shape[0], dtype=jnp.int32)[:, None]
    ).astype(jnp.float32)
    lookup = jnp.pad(lookup, ((0, 0), (0, TABLE - length)))
    table = jnp.einsum(
        "gd,gm->md", lookup, both_bias, precision=lax.Precision.HIGHEST,
        preferred_element_type=jnp.float32,
    )
    table = reverse_distance(table).reshape(heads // 2, 2, TABLE)
    gains = norm_gains.T

    own_inputs = flat(own_rows(inputs))
    own_memory = flat(own_rows(memory))
    own_cotangent = flat(own_rows(cotangent))
    normed_zero, qkv = project(upper, own_inputs, gains, kernel_qkv)
    qkv = in_rows(qkv, length)
    cross_kv = in_rows(memory_project(upper, own_memory, kernel_ckv), keys)
    self_mixed, self_logs = self_forward(qkv, dec, dec_across, table)
    hidden_one, normed_one, cross_query = after_self(
        upper, own_inputs, flat(self_mixed), gains, kernel_so, kernel_cq
    )
    cross_query = in_rows(cross_query, length)
    cross_mixed, cross_logs = cross_forward(cross_query, cross_kv, dec, mem_across)
    split_or_whole = split if aligned else (tensor_count, 1, width // 2)
    output, feed_slopes, slope_two, slope_cm, keep_co, send_co, gain_two = feed_forward(
        upper, hidden_one, flat(cross_mixed), own_cotangent, gains, kernel_co, feed_weights, split_or_whole
    )
    output = in_rows(output, length)

    def halves_of(kept, sent):
        if aligned:
            return kept, sent
        low_half = jnp.where(upper[0] == 1, sent, kept)
        high_half = jnp.where(upper[0] == 1, kept, sent)
        both = jnp.concatenate([low_half, high_half], axis=2)
        both = both.reshape((tensor_count, shards // 2, 2, shard_rows, both.shape[-1]))
        return pick(both, upper[0] == 1, 2), pick(both, upper[0] == 0, 2)

    if not aligned:
        feed_slopes = jnp.transpose(
            feed_slopes.reshape(tensor_count, shards, shard_rows, feed_slopes.shape[-1]), (1, 0, 2, 3)
        )
    share_feed = lax.psum_scatter(
        feed_slopes.reshape(-1, feed_slopes.shape[-1]), everywhere, scatter_dimension=0, tiled=True
    ).astype(jnp.float32)

    slope_cq, slope_ck, slope_cv = cross_backward(
        cross_query, cross_kv, dec, mem_across, cross_mixed, cross_logs, in_rows(slope_cm, length)
    )
    slope_one, slope_sm, keep_qo, send_qo, gain_one = after_cross(
        upper, flat(slope_cq), normed_one, hidden_one, slope_two, flat(self_mixed), gains,
        kernel_cq, kernel_so, split_or_whole,
    )
    keep_kv, send_kv = outer(
        upper, own_memory, [flat(slope_ck), flat(slope_cv)], split_or_whole, "memory_outer"
    )
    share_cross = scatter_group(
        [halves_of(keep_co, send_co), halves_of(keep_qo, send_qo), halves_of(keep_kv, send_kv)],
        1024, index,
    )
    slope_q, slope_k, slope_v, diagonals = self_backward(
        qkv, dec, dec_across, table, self_mixed, self_logs, in_rows(slope_sm, length)
    )
    slopes_self = [flat(slope_q), flat(slope_k), flat(slope_v)]
    share_self = scatter_group(
        [halves_of(*outer(upper, normed_zero, slopes_self, split_or_whole, "self_outer"))], 512, index
    )
    memory_grad = in_rows(
        memory_back(upper, flat(slope_ck), flat(slope_cv), kernel_ckv), keys
    )
    input_slope, gain_zero = input_back(
        upper, slopes_self, own_inputs, slope_one, gains, kernel_qkv
    )
    input_slope = in_rows(input_slope, length)
    input_grad = (
        in_order(input_slope, swap_tensor(input_slope), tensor_index == 1, 0)
        .reshape(inputs.shape)
        .astype(jnp.float32)
    )

    bias_local = jnp.einsum(
        "gd,md->gm", lookup, reverse_distance(diagonals.reshape(heads, TABLE)),
        precision=lax.Precision.HIGHEST, preferred_element_type=jnp.float32,
    )
    bias_local = jnp.where(
        tensor_index == 1, jnp.roll(bias_local, own_heads, axis=1), bias_local
    )
    small = jnp.concatenate([gain_zero[0], gain_one[0], gain_two[0], bias_local.reshape(-1)])
    small = sum_everywhere(small)
    gain_sums = small[: 3 * width].reshape(3, width)
    bias_sums = small[3 * width :].reshape(bias_local.shape)
    square_sum = sum_everywhere(
        sum(jnp.sum(share * share) for share in (share_self, share_cross, share_feed))
    )
    grad_norm = jnp.sqrt(square_sum + jnp.sum(small * small))
    clip_factor = jnp.minimum(1.0, CLIP_NORM / (grad_norm + 1e-06))

    parts_self = [share_self[:, i * columns : (i + 1) * columns] for i in range(3)]
    parts_cross = [share_cross[:, i * columns : (i + 1) * columns] for i in range(5)]
    slope_in = jnp.stack(parts_self + [parts_cross[1], parts_cross[3], parts_cross[4]], axis=1)
    slope_out = jnp.stack([parts_cross[2], parts_cross[0]], axis=1)
    slope_up, slope_down = take_apart(share_feed)
    shared_gains = lax.dynamic_slice_in_dim(gain_sums, index * shard_rows, shard_rows, 1).T
    old_gains = lax.dynamic_slice_in_dim(norm_gains, index * shard_rows, shard_rows, 0)
    bias_share = lax.dynamic_slice_in_dim(bias_sums, tensor_index * own_heads, own_heads, 1)
    new_in = adam_update(
        attention_in, slope_in * clip_factor, moment_attention_in, square_attention_in,
        MATRIX_RATE, DECAY_RATE,
    )
    new_out = adam_update(
        attention_out, slope_out * clip_factor, moment_attention_out, square_attention_out,
        MATRIX_RATE, DECAY_RATE,
    )
    new_up = adam_update(
        expand_weight, slope_up * clip_factor, moment_expand, square_expand,
        MATRIX_RATE, DECAY_RATE,
    )
    new_down = adam_update(
        contract_weight, slope_down * clip_factor, moment_contract, square_contract,
        MATRIX_RATE, DECAY_RATE,
    )
    new_gains = adam_update(
        old_gains, shared_gains * clip_factor, moment_gains, square_gains, SMALL_RATE, 0.0
    )
    new_bias = adam_update(
        position_bias, bias_share * clip_factor, moment_bias, square_bias, SMALL_RATE, 0.0
    )
    return (
        (output, input_grad, memory_grad, grad_norm)
        + new_in + new_out + new_up + new_down + new_gains + new_bias
    )


def solution(mesh):
    return jax.shard_map(
        on_device,
        mesh=mesh,
        in_specs=(
            P("dp", None, None),
            P("dp", None, None),
            P("dp", None),
            P("dp", None),
            P("dp"),
            P(),
            P("dp", None, None),
            P("dp", None, "tensor"),
            P("dp", None, "tensor"),
            P("dp", "tensor"),
            P("dp", "tensor"),
            P(),
            P(None, "tensor"),
            P("dp", None, "tensor"),
            P("dp", None, "tensor"),
            P("dp", None, "tensor"),
            P("dp", None, "tensor"),
            P("dp", "tensor"),
            P("dp", "tensor"),
            P("dp", "tensor"),
            P("dp", "tensor"),
            P("dp", None),
            P("dp", None),
            P(None, "tensor"),
            P(None, "tensor"),
        ),
        out_specs=(
            P(("dp", "tensor"), None, None),
            P("dp", None, None),
            P(("dp", "tensor"), None, None),
            P(),
            P("dp", None, "tensor"),
            P("dp", None, "tensor"),
            P("dp", None, "tensor"),
            P("dp", None, "tensor"),
            P("dp", None, "tensor"),
            P("dp", None, "tensor"),
            P("dp", "tensor"),
            P("dp", "tensor"),
            P("dp", "tensor"),
            P("dp", "tensor"),
            P("dp", "tensor"),
            P("dp", "tensor"),
            P("dp", None),
            P("dp", None),
            P("dp", None),
            P(None, "tensor"),
            P(None, "tensor"),
            P(None, "tensor"),
        ),
        check_vma=False,
    )
```

```python
import functools

import jax
import jax.numpy as jnp
from jax import lax
from jax.experimental import pallas as pl
from jax.experimental.pallas import tpu as pltpu
from jax.sharding import PartitionSpec as P

STEP = 10
NORM_EPS = 1e-06
CLIP_NORM = 1.0
BETA_ONE = 0.9
BETA_TWO = 0.95
ADAM_EPS = 1e-08
MATRIX_RATE = 0.08
SMALL_RATE = 0.8
DECAY_RATE = 0.1
GELU_SCALE = 0.7978845608028654
GELU_CUBIC = 0.044715
MASKED = -1e30
TABLE = 384
NT = (((1,), (1,)), ((), ()))
TN = (((0,), (0,)), ((), ()))


def dot(a, b, dims=(((1,), (0,)), ((), ()))):
    return lax.dot_general(a, b, dims, preferred_element_type=jnp.float32)


def lanes(shape):
    return lax.broadcasted_iota(jnp.int32, shape, len(shape) - 1)


def half_of(values, which):
    return jnp.where((lanes(values.shape) >= 64) == (which == 1), values, jnp.zeros_like(values))


def column(values, index):
    return jnp.sum(jnp.where(lanes(values.shape) == index, values, 0.0), axis=-1, keepdims=True)


def cross_forward_kernel(q_ref, k_ref, v_ref, dec_ref, mem_ref, o_ref, lse_ref):
    pair = pl.program_id(1)
    query, key, value = q_ref[0], k_ref[0], v_ref[0]
    allowed = dec_ref[0] == mem_ref[0]
    mixed, logs = forward_pair(query, key, value, [None, None], allowed)
    o_ref[0] = mixed.astype(o_ref.dtype)
    store_logs(lse_ref, logs, pair)


def store_logs(lse_ref, logs, pair):
    @pl.when(pair == 0)
    def _():
        lse_ref[0] = jnp.zeros(lse_ref.shape[1:], jnp.float32)

    lane = lanes(lse_ref.shape[1:])
    kept = lse_ref[0]
    for which in range(2):
        kept = jnp.where(lane == 2 * pair + which, logs[which], kept)
    lse_ref[0] = kept


def forward_pair(query, key, value, biases, allowed):
    mixed = jnp.zeros(query.shape, jnp.float32)
    logs = []
    for which in range(2):
        scores = dot(half_of(query, which), key, NT)
        if biases[which] is not None:
            scores = scores + biases[which]
        scores = jnp.where(allowed, scores, MASKED)
        top = jnp.max(scores, axis=-1, keepdims=True)
        weights = jnp.exp(scores - top)
        total = jnp.sum(weights, axis=-1, keepdims=True)
        logs.append(top + jnp.log(total))
        mixed = mixed + dot(weights.astype(jnp.bfloat16), half_of(value, which)) * (1.0 / total)
    return mixed, logs


def backward_pair(query, key, value, mixed, upstream, logs, biases, allowed):
    slope_q = jnp.zeros(query.shape, jnp.float32)
    slope_k = jnp.zeros(key.shape, jnp.float32)
    slope_v = jnp.zeros(key.shape, jnp.float32)
    grads = []
    product = upstream.astype(jnp.float32) * mixed.astype(jnp.float32)
    for which in range(2):
        query_half = half_of(query, which)
        up_half = half_of(upstream, which)
        scores = dot(query_half, key, NT)
        if biases[which] is not None:
            scores = scores + biases[which]
        prob = jnp.exp(jnp.where(allowed, scores - logs[which], MASKED))
        slope_p = dot(up_half, value, NT)
        inner = jnp.sum(half_of(product, which), axis=-1, keepdims=True)
        grad = (prob * (slope_p - inner)).astype(jnp.bfloat16)
        slope_q = slope_q + dot(grad, half_of(key, which))
        slope_k = slope_k + dot(grad, query_half, TN)
        slope_v = slope_v + dot(prob.astype(jnp.bfloat16), up_half, TN)
        grads.append(grad)
    return slope_q, slope_k, slope_v, grads


def cross_backward_kernel(
    q_ref, k_ref, v_ref, dec_ref, mem_ref, o_ref, lse_ref, up_ref, dq_ref, dk_ref, dv_ref
):
    pair = pl.program_id(1)
    allowed = dec_ref[0] == mem_ref[0]
    logs = [column(lse_ref[0], 2 * pair + which) for which in range(2)]
    slope_q, slope_k, slope_v, _ = backward_pair(
        q_ref[0], k_ref[0], v_ref[0], o_ref[0], up_ref[0], logs, [None, None], allowed
    )
    dq_ref[0] = slope_q.astype(jnp.bfloat16)
    dk_ref[0] = slope_k.astype(jnp.bfloat16)
    dv_ref[0] = slope_v.astype(jnp.bfloat16)


def pad_keys(values):
    extra = TABLE - values.shape[0]
    return jnp.concatenate([values, jnp.zeros((extra, values.shape[1]), values.dtype)], axis=0)


def self_allowed(dec_ref, decT_ref):
    length = dec_ref.shape[1]
    rows = lax.broadcasted_iota(jnp.int32, (length, TABLE), 0)
    return (dec_ref[0] == decT_ref[0]) & (lanes((length, TABLE)) <= rows)


def toeplitz(table_ref, which, length):
    spread = jnp.broadcast_to(table_ref[0, which : which + 1, :], (length, TABLE))
    return pltpu.roll(spread, 0, 1, stride=1, stride_axis=0)


def self_forward_kernel(q_ref, k_ref, v_ref, dec_ref, decT_ref, table_ref, o_ref, lse_ref):
    pair = pl.program_id(1)
    length = q_ref.shape[1]
    biases = [toeplitz(table_ref, which, length) for which in range(2)]
    mixed, logs = forward_pair(
        q_ref[0], pad_keys(k_ref[0]), pad_keys(v_ref[0]), biases, self_allowed(dec_ref, decT_ref)
    )
    o_ref[0] = mixed.astype(o_ref.dtype)
    store_logs(lse_ref, logs, pair)


def self_backward_kernel(ties, *refs):
    q_ref, k_ref, v_ref, dec_ref, decT_ref, table_ref, o_ref, lse_ref, up_ref = refs[:9]
    dq_ref, dk_ref, dv_ref, diag_ref = refs[9 + ties :]
    pair, row = pl.program_id(0), pl.program_id(1)
    length = q_ref.shape[1]
    biases = [toeplitz(table_ref, which, length) for which in range(2)]
    logs = [column(lse_ref[0], 2 * pair + which) for which in range(2)]
    slope_q, slope_k, slope_v, grads = backward_pair(
        q_ref[0], pad_keys(k_ref[0]), pad_keys(v_ref[0]), o_ref[0], up_ref[0], logs, biases,
        self_allowed(dec_ref, decT_ref),
    )
    dq_ref[0] = slope_q.astype(jnp.bfloat16)
    dk_ref[0] = slope_k[:length].astype(jnp.bfloat16)
    dv_ref[0] = slope_v[:length].astype(jnp.bfloat16)

    @pl.when(row == 0)
    def _():
        diag_ref[...] = jnp.zeros(diag_ref.shape, jnp.float32)

    for which in range(2):
        diag_ref[0, which : which + 1, :] += diagonal_sums(grads[which].astype(jnp.float32))


def diagonal_sums(values):
    groups = jnp.zeros((8, TABLE), jnp.float32)
    for start in range(0, values.shape[0], 8):
        groups = groups + pltpu.roll(values[start : start + 8], (TABLE - start) % TABLE, 1)
    total = groups[0:1]
    for row in range(1, 8):
        total = total + pltpu.roll(groups, TABLE - row, 1)[row : row + 1]
    return total


def params(count):
    return pltpu.CompilerParams(
        dimension_semantics=("arbitrary",) * count, vmem_limit_bytes=48 * 1024 * 1024
    )


def cross_forward(q, kv, dec, mem):
    rows, length, width = q.shape
    keys = kv.shape[1]
    pairs = width // 128
    lanes_q = pl.BlockSpec((1, length, 128), lambda r, p: (r, 0, p))
    lanes_k = pl.BlockSpec((1, keys, 128), lambda r, p: (r, 0, p))
    lanes_v = pl.BlockSpec((1, keys, 128), lambda r, p: (r, 0, p + pairs))
    return pl.pallas_call(
        cross_forward_kernel,
        grid=(rows, width // 128),
        in_specs=[
            lanes_q, lanes_k, lanes_v,
            pl.BlockSpec((1, length, 1), lambda r, p: (r, 0, 0)),
            pl.BlockSpec((1, 1, keys), lambda r, p: (r, 0, 0)),
        ],
        out_specs=[lanes_q, pl.BlockSpec((1, length, 128), lambda r, p: (r, 0, 0))],
        out_shape=[
            jax.ShapeDtypeStruct((rows, length, width), jnp.bfloat16),
            jax.ShapeDtypeStruct((rows, length, 128), jnp.float32),
        ],
        compiler_params=params(2),
        cost_estimate=cost(4 * rows * length * keys * width, 2 * rows * width * (2 * length + 2 * keys), 2 * rows * length * keys * pairs),
        name="cross_forward",
    )(q, kv, kv, dec, mem)


def cross_backward(q, kv, dec, mem, mixed, logs, upstream):
    rows, length, width = q.shape
    keys = kv.shape[1]
    pairs = width // 128
    lanes_q = pl.BlockSpec((1, length, 128), lambda r, p: (r, 0, p))
    lanes_k = pl.BlockSpec((1, keys, 128), lambda r, p: (r, 0, p))
    lanes_v = pl.BlockSpec((1, keys, 128), lambda r, p: (r, 0, p + pairs))
    return pl.pallas_call(
        cross_backward_kernel,
        grid=(rows, width // 128),
        in_specs=[
            lanes_q, lanes_k, lanes_v,
            pl.BlockSpec((1, length, 1), lambda r, p: (r, 0, 0)),
            pl.BlockSpec((1, 1, keys), lambda r, p: (r, 0, 0)),
            lanes_q, pl.BlockSpec((1, length, 128), lambda r, p: (r, 0, 0)), lanes_q,
        ],
        out_specs=[lanes_q, lanes_k, lanes_k],
        out_shape=[
            jax.ShapeDtypeStruct((rows, length, width), jnp.bfloat16),
            jax.ShapeDtypeStruct((rows, keys, width), jnp.bfloat16),
            jax.ShapeDtypeStruct((rows, keys, width), jnp.bfloat16),
        ],
        compiler_params=params(2),
        cost_estimate=cost(10 * rows * length * keys * width, 2 * rows * width * (4 * length + 4 * keys), 2 * rows * length * keys * pairs),
        name="cross_backward",
    )(q, kv, kv, dec, mem, mixed, logs, upstream)


def self_forward(qkv, dec, decT, table, half):
    rows, length, width = qkv.shape
    width = width // 3
    pairs = width // 128
    count = pairs // 2
    first = half * count
    spec = pl.BlockSpec((1, length, 128), lambda r, p: (r, 0, p + first))
    spec_k = pl.BlockSpec((1, length, 128), lambda r, p: (r, 0, p + first + pairs))
    spec_v = pl.BlockSpec((1, length, 128), lambda r, p: (r, 0, p + first + 2 * pairs))
    return pl.pallas_call(
        self_forward_kernel,
        grid=(rows, count),
        in_specs=[
            spec, spec_k, spec_v,
            pl.BlockSpec((1, length, 1), lambda r, p: (r, 0, 0)),
            pl.BlockSpec((1, 1, TABLE), lambda r, p: (r, 0, 0)),
            pl.BlockSpec((1, 2, TABLE), lambda r, p: (p + first, 0, 0)),
        ],
        out_specs=[
            pl.BlockSpec((1, length, 128), lambda r, p: (r, 0, p)),
            pl.BlockSpec((1, length, 128), lambda r, p: (r, 0, 0)),
        ],
        out_shape=[
            jax.ShapeDtypeStruct((rows, length, width // 2), jnp.bfloat16),
            jax.ShapeDtypeStruct((rows, length, 128), jnp.float32),
        ],
        compiler_params=params(2),
        name="self_forward",
    )(qkv, qkv, qkv, dec, decT, table)


def self_backward(qkv, dec, decT, table, mixed, logs, upstream, half, after):
    rows, length, width = qkv.shape
    width = width // 3
    pairs = width // 128
    count = pairs // 2
    first = half * count
    spec = pl.BlockSpec((1, length, 128), lambda p, r: (r, 0, p + first))
    spec_k = pl.BlockSpec((1, length, 128), lambda p, r: (r, 0, p + first + pairs))
    spec_v = pl.BlockSpec((1, length, 128), lambda p, r: (r, 0, p + first + 2 * pairs))
    spec_out = pl.BlockSpec((1, length, 128), lambda p, r: (r, 0, p))
    out = jax.ShapeDtypeStruct((rows, length, width // 2), jnp.bfloat16)
    return pl.pallas_call(
        functools.partial(self_backward_kernel, len(after)),
        grid=(count, rows),
        in_specs=[
            spec, spec_k, spec_v,
            pl.BlockSpec((1, length, 1), lambda p, r: (r, 0, 0)),
            pl.BlockSpec((1, 1, TABLE), lambda p, r: (r, 0, 0)),
            pl.BlockSpec((1, 2, TABLE), lambda p, r: (p + first, 0, 0)), spec_out,
            pl.BlockSpec((1, length, 128), lambda p, r: (r, 0, 0)), spec,
        ] + [pl.BlockSpec(memory_space=pl.ANY)] * len(after),
        out_specs=[spec_out, spec_out, spec_out, pl.BlockSpec((1, 2, TABLE), lambda p, r: (p, 0, 0))],
        out_shape=[out, out, out, jax.ShapeDtypeStruct((count, 2, TABLE), jnp.float32)],
        compiler_params=params(2),
        cost_estimate=cost(5 * rows * length * TABLE * width, 8 * rows * width * length, rows * length * TABLE * pairs),
        name="self_backward",
    )(qkv, qkv, qkv, dec, decT, table, mixed, logs, upstream, *after)


SLOPE = GELU_SCALE * 3.0 * GELU_CUBIC
ROW_TILE = 16
FF_TILE = 256
MEMORY_TILE = 512


def whole(shape):
    return pl.BlockSpec(shape, lambda *_: (0,) * len(shape))


def cost(*_):
    return None


def row_scale(hidden):
    return lax.rsqrt(jnp.mean(hidden * hidden, axis=-1, keepdims=True) + NORM_EPS)


def row_back(hidden, gain, upstream):
    factor = row_scale(hidden)
    scaled = upstream * hidden
    inner = jnp.mean(scaled * gain, axis=-1, keepdims=True)
    slope = factor * (upstream * gain) - (factor * factor * factor * inner) * hidden
    return slope


def emit(gradient, keep_ref, send_ref, start, upper):
    halves, blocks, rows, _ = keep_ref.shape
    columns = gradient.shape[1] // halves
    for half in range(halves):
        part = gradient[:, half * columns : (half + 1) * columns]
        part = part.reshape(blocks, 2, rows, columns)
        low, high = part[:, 0], part[:, 1]
        keep = jnp.where(upper, high, low).astype(jnp.bfloat16)
        send = jnp.where(upper, low, high).astype(jnp.bfloat16)
        keep_ref[half, :, :, start : start + columns] = keep
        send_ref[half, :, :, start : start + columns] = send


def call(kernel, name, grid, in_specs, out_specs, out_shape, work, scratch=(), weights=(), after=(), aliases=None):
    count, loaded = len(in_specs), 2 * len(weights)
    outs = len(out_specs) if isinstance(out_specs, list) else 1

    def run(up_ref, *refs):
        ins = refs[:count]
        pieces = refs[count : count + loaded]
        kernel(up_ref, *ins, pieces, *refs[count + loaded + len(after) :])

    anywhere = pl.BlockSpec(memory_space=pl.ANY)
    return lambda upper, *operands: pl.pallas_call(
        run if weights else lambda up_ref, *refs: kernel(up_ref, *refs[:count], *refs[count + len(after) :]),
        grid_spec=pltpu.PrefetchScalarGridSpec(
            num_scalar_prefetch=1,
            grid=grid,
            in_specs=in_specs + [anywhere] * (loaded + len(after)),
            out_specs=out_specs,
            scratch_shapes=scratch,
        ),
        out_shape=out_shape,
        input_output_aliases=aliases or {},
        compiler_params=pltpu.CompilerParams(
            dimension_semantics=("arbitrary",) * len(grid), vmem_limit_bytes=56 * 1024 * 1024
        ),
        cost_estimate=work,
        name=name,
    )(upper, *operands, *[piece for pair in weights for piece in pair], *after)


def fetch(pieces, store, sems, mats, upper):
    copies = []
    columns = store.shape[3] // (2 * len(mats))
    for place, (source, start) in enumerate(mats):
        group = []
        for half in range(2):
            for other in range(2):
                copy = pltpu.make_async_copy(
                    pieces[2 * source + other].at[half, :, :, pl.ds(start, columns)],
                    store.at[:, (upper + other) % 2, :, pl.ds((2 * place + half) * columns, columns)],
                    sems.at[place * 4 + half * 2 + other],
                )
                group.append(copy)
        copies.append(group)
    return copies


def start(copies):
    for group in copies:
        for copy in group:
            copy.start()


def wait(group):
    for copy in group:
        copy.wait()


def kernel_of(store, place, width):
    return store[:, :, :, place * width : (place + 1) * width].reshape(width, width)


def room(weights, count):
    _, blocks, rows, _ = weights[0][0].shape
    wide = 2 * count * (weights[0][0].shape[3] // 2)
    return [pltpu.VMEM((blocks, 2, rows, wide), jnp.bfloat16), pltpu.SemaphoreType.DMA((4 * count,))]


def shape_of(shape, kind=jnp.bfloat16):
    return jax.ShapeDtypeStruct(shape, kind)


QKV = ((0, 0), (0, 1), (1, 0))
SO = ((1, 1),)
CKV = ((0, 0), (0, 1))
CQ = ((1, 0),)
CO = ((1, 1),)


def placed(mats, pieces):
    columns = pieces[0].shape[3] // 2
    return [(source, which * columns) for source, which in mats]


def project_kernel(up_ref, x_ref, gain_ref, pieces, n_ref, out_ref, store, sems):
    copies = fetch(pieces, store, sems, placed(QKV, pieces), up_ref[0])

    @pl.when(pl.program_id(0) == 0)
    def _():
        start(copies)
        hidden = x_ref[...].astype(jnp.float32)
        n_ref[...] = (hidden * row_scale(hidden) * gain_ref[0:1]).astype(jnp.bfloat16)

    width = n_ref.shape[1]
    for place in range(3):
        @pl.when(pl.program_id(0) == place)
        def _():
            wait(copies[place])
            out_ref[...] = dot(n_ref[...], kernel_of(store, place, width)).astype(jnp.bfloat16)


def project(upper, hidden, gains, pieces):
    tokens, width = hidden.shape
    return call(
        project_kernel, "project", (3,),
        [whole((tokens, width)), whole(gains.shape)],
        [whole((tokens, width)), pl.BlockSpec((tokens, width), lambda g, *_: (0, g))],
        [shape_of((tokens, width)), shape_of((tokens, 3 * width))],
        cost(6 * tokens * width * width, 2 * width * (tokens * 5 + 3 * width)),
        scratch=room(pieces, 3), weights=pieces,
    )(upper, hidden, gains)


def memory_project_kernel(up_ref, x_ref, pieces, out_ref, store, sems):
    copies = fetch(pieces, store, sems, placed(CKV, pieces), up_ref[0])

    @pl.when(pl.program_id(0) == 0)
    def _():
        start(copies)
        wait(copies[0])
        wait(copies[1])

    width = x_ref.shape[1]
    out_ref[...] = dot(x_ref[...], store[...].reshape(width, 2 * width)).astype(jnp.bfloat16)


def memory_project(upper, memory, pieces):
    tokens, width = memory.shape
    tile = MEMORY_TILE
    return call(
        memory_project_kernel, "memory_project", (tokens // tile,),
        [pl.BlockSpec((tile, width), lambda g, *_: (g, 0))],
        pl.BlockSpec((tile, 2 * width), lambda g, *_: (g, 0)),
        shape_of((tokens, 2 * width)),
        cost(4 * tokens * width * width, 2 * (3 * tokens * width + 2 * width * width)),
        scratch=room(pieces, 2), weights=pieces,
    )(upper, memory)


def after_self_kernel(up_ref, x_ref, a_ref, b_ref, gain_ref, pieces, h_ref, n_ref, q_ref, store, sems):
    copies = fetch(pieces, store, sems, [placed(SO, pieces[:4])[0], (2 + CQ[0][0], 0)], up_ref[0])

    @pl.when(pl.program_id(0) == 0)
    def _():
        start(copies)
        wait(copies[0])
        wait(copies[1])

    width = x_ref.shape[1]
    weight = kernel_of(store, 0, width)
    hidden = x_ref[...].astype(jnp.float32) + dot(a_ref[...], weight[:, : width // 2], NT)
    hidden += dot(b_ref[...], weight[:, width // 2 :], NT)
    h_ref[...] = hidden
    normed = (hidden * row_scale(hidden) * gain_ref[1:2]).astype(jnp.bfloat16)
    n_ref[...] = normed
    q_ref[...] = dot(normed, kernel_of(store, 1, width)).astype(jnp.bfloat16)


def after_self(upper, inputs, mixed, gains, pieces):
    half = pl.BlockSpec((inputs.shape[0] // 2, inputs.shape[1] // 2), lambda g, *_: (g, 0))
    tokens, width = inputs.shape
    tile = tokens // 2
    rows = pl.BlockSpec((tile, width), lambda g, *_: (g, 0))
    return call(
        after_self_kernel, "after_self", (2,),
        [rows, half, half, whole(gains.shape)],
        [rows, rows, rows],
        [shape_of((tokens, width), jnp.float32), shape_of((tokens, width)), shape_of((tokens, width))],
        cost(4 * tokens * width * width, tokens * width * 12 + 4 * width * width),
        scratch=room(pieces, 2), weights=pieces,
    )(upper, inputs, *mixed, gains)


def feed_kernel(
    up_ref, h1_ref, a_ref, gy_ref, gain_ref, w_ref, pieces,
    y_ref, g_ref, gh_ref, ga_ref, keep_ref, send_ref,
    n_ref, nT_ref, gyT_ref, acc_ref, store, sems,
):
    step = pl.program_id(0)
    tile = FF_TILE
    width = y_ref.shape[1]
    copies = fetch(pieces, store, sems, placed(CO, pieces), up_ref[0])

    @pl.when(step == 0)
    def _():
        start(copies)
        gyT_ref[...] = gy_ref[...].T
        wait(copies[0])
        hidden = h1_ref[...] + dot(a_ref[...], kernel_of(store, 0, width), NT)
        gh_ref[...] = hidden
        y_ref[...] = hidden
        normed = (hidden * row_scale(hidden) * gain_ref[2:3]).astype(jnp.bfloat16)
        n_ref[...] = normed
        nT_ref[...] = normed.T
        acc_ref[...] = jnp.zeros(acc_ref.shape, jnp.float32)

    wi = w_ref[:, 0, :, :tile].reshape(width, tile)
    wf = w_ref[:, 0, :, tile:].reshape(width, tile)
    u = dot(n_ref[...], wi)
    square = u * u
    bent = jnp.tanh(u * (GELU_SCALE + (GELU_SCALE * GELU_CUBIC) * square))
    half = 0.5 + 0.5 * bent
    act = (u * half).astype(jnp.bfloat16)
    slope = half + (0.5 * u) * (1.0 - bent * bent) * (GELU_SCALE + SLOPE * square)
    gu = (dot(gy_ref[...], wf) * slope).astype(jnp.bfloat16)
    y_ref[...] += dot(act, wf, NT)
    acc_ref[...] += dot(gu, wi, NT)
    g_ref[:, 0, :, :tile] = dot(nT_ref[...], gu).reshape(g_ref.shape[0], g_ref.shape[2], tile).astype(jnp.bfloat16)
    g_ref[:, 0, :, tile:] = dot(gyT_ref[...], act).reshape(g_ref.shape[0], g_ref.shape[2], tile).astype(jnp.bfloat16)

    @pl.when(step == pl.num_programs(0) - 1)
    def _():
        back = row_back(gh_ref[...], gain_ref[2:3], acc_ref[...])
        total = gy_ref[...].astype(jnp.float32) + back
        gh_ref[...] = total
        low = total.astype(jnp.bfloat16)
        ga_ref[...] = dot(low, kernel_of(store, 0, width)).astype(jnp.bfloat16)
        emit(dot(low.T, a_ref[...]), keep_ref, send_ref, 0, up_ref[0] == 1)


def feed_forward(upper, hidden, mixed, cotangent, gains, pieces, weights, split):
    tokens, width = hidden.shape
    blocks, halves, rows, wide = weights.shape
    steps = wide // (2 * FF_TILE)
    spec = pl.BlockSpec((blocks, 1, rows, 2 * FF_TILE), lambda g, *_: (0, g // steps, 0, g % steps))
    full = whole((tokens, width))
    f32 = shape_of((tokens, width), jnp.float32)
    columns = width // halves
    return call(
        feed_kernel, "feed_forward", (halves * steps,),
        [full, full, full, whole(gains.shape), spec],
        [full, spec, full, full, whole(split + (columns,)), whole(split + (columns,))],
        [f32, shape_of(weights.shape), f32, shape_of((tokens, width)),
         shape_of(split + (columns,)), shape_of(split + (columns,))],
        cost(6 * tokens * width * halves * wide, 40 * tokens * width, tokens * halves * wide / 2),
        scratch=[
            pltpu.VMEM((tokens, width), jnp.bfloat16), pltpu.VMEM((width, tokens), jnp.bfloat16),
            pltpu.VMEM((width, tokens), jnp.bfloat16), pltpu.VMEM((tokens, width), jnp.float32),
        ] + room(pieces, 1), weights=pieces,
    )(upper, hidden, mixed, cotangent, gains, weights)


def after_cross_kernel(
    up_ref, gq_ref, n_ref, h_ref, gh_ref, a_ref, b_ref, gain_ref, pieces,
    gh1_ref, ga_ref, keep_ref, send_ref, store, sems,
):
    copies = fetch(pieces, store, sems, [placed(SO, pieces[:4])[0], (2 + CQ[0][0], 0)], up_ref[0])
    start(copies)
    upper = up_ref[0] == 1
    columns = keep_ref.shape[3] // 2
    width = h_ref.shape[1]
    emit(dot(n_ref[...].T, gq_ref[...]), keep_ref, send_ref, 0, upper)
    wait(copies[1])
    back = row_back(h_ref[...], gain_ref[1:2], dot(gq_ref[...], kernel_of(store, 1, width), NT))
    total = gh_ref[...] + back
    gh1_ref[...] = total
    low = total.astype(jnp.bfloat16)
    wait(copies[0])
    ga_ref[...] = dot(low, kernel_of(store, 0, width)).astype(jnp.bfloat16)
    across = low.T
    emit(dot(across, a_ref[...]), keep_ref.at[0:1], send_ref.at[0:1], columns, upper)
    emit(dot(across, b_ref[...]), keep_ref.at[1:2], send_ref.at[1:2], columns, upper)


def after_cross(upper, slope_q, normed, hidden, slope_hidden, mixed, gains, pieces, split, after):
    tokens, width = hidden.shape
    full = whole((tokens, width))
    piece = split + (2 * (width // split[0]),)
    return call(
        after_cross_kernel, "after_cross", (1,),
        [full, full, full, full, whole((tokens, width // 2)), whole((tokens, width // 2)), whole(gains.shape)],
        [full, full, whole(piece), whole(piece)],
        [shape_of((tokens, width), jnp.float32), shape_of((tokens, width)),
         shape_of(piece), shape_of(piece)],
        cost(8 * tokens * width * width, tokens * width * 24 + 8 * width * width),
        scratch=room(pieces, 2), weights=pieces, after=after,
    )(upper, slope_q, normed, hidden, slope_hidden, *mixed, gains)


def outer_kernel(up_ref, x_ref, *refs):
    slopes, keep_ref, send_ref = refs[:-2], refs[-2], refs[-1]
    upper = up_ref[0] == 1
    columns = keep_ref.shape[3] // len(slopes)
    across = x_ref[...].T
    for place, slope in enumerate(slopes):
        emit(dot(across, slope[...]), keep_ref, send_ref, place * columns, upper)


def outer(upper, rows, slopes, split, name, after=()):
    tokens, width = rows.shape
    wide = slopes[0].shape[1]
    piece = split + (len(slopes) * (wide // split[0]),)
    return call(
        outer_kernel, name, (1,),
        [whole(rows.shape)] + [whole(slope.shape) for slope in slopes],
        [whole(piece), whole(piece)],
        [shape_of(piece), shape_of(piece)],
        cost(2 * tokens * width * wide * len(slopes), 2 * (tokens + width) * (width + wide * len(slopes))),
        after=after,
    )(upper, rows, *slopes)


def memory_back_kernel(up_ref, gk_ref, gv_ref, pieces, out_ref, store, sems):
    copies = fetch(pieces, store, sems, placed(CKV, pieces), up_ref[0])

    @pl.when(pl.program_id(0) == 0)
    def _():
        start(copies)
        wait(copies[0])
        wait(copies[1])

    width = gk_ref.shape[1]
    out_ref[...] = dot(gk_ref[...], kernel_of(store, 0, width), NT) + dot(gv_ref[...], kernel_of(store, 1, width), NT)


def memory_back(upper, slope_k, slope_v, pieces, part, earlier):
    tokens, width = slope_k.shape
    tile = MEMORY_TILE
    first = part * (tokens // 2 // tile)
    rows = pl.BlockSpec((tile, width), lambda g, *_: (g + first, 0))
    in_specs = [rows, rows] + [pl.BlockSpec(memory_space=pl.ANY)] * len(earlier)
    return call(
        lambda up_ref, gk_ref, gv_ref, *refs: memory_back_kernel(up_ref, gk_ref, gv_ref, *refs[len(earlier) :]),
        "memory_back", (tokens // 2 // tile,),
        in_specs, rows, shape_of((tokens, width), jnp.float32),
        cost(2 * tokens * width * width, 4 * tokens * width + 4 * width * width),
        scratch=room(pieces, 2), weights=pieces, aliases={3: 0} if earlier else {},
    )(upper, slope_k, slope_v, *earlier)


def input_back_kernel(up_ref, *refs):
    slopes, (x_ref, gh_ref, gain_ref, pieces, out_ref, store, sems) = refs[:6], refs[6:]
    copies = fetch(pieces, store, sems, placed(QKV, pieces), up_ref[0])
    start(copies)
    width = x_ref.shape[1]
    half = width // 2
    upstream = 0.0
    for place in range(3):
        wait(copies[place])
        weight = kernel_of(store, place, width)
        upstream += dot(slopes[2 * place][...], weight[:, :half], NT)
        upstream += dot(slopes[2 * place + 1][...], weight[:, half:], NT)
    back = row_back(x_ref[...].astype(jnp.float32), gain_ref[0:1], upstream)
    out_ref[...] = (gh_ref[...] + back).astype(jnp.bfloat16)


def input_back(upper, slopes, inputs, slope_hidden, gains, pieces, after):
    tokens, width = inputs.shape
    full = whole((tokens, width))
    return call(
        input_back_kernel, "input_back", (1,),
        [whole((tokens, width // 2))] * 6 + [full, full, whole(gains.shape)],
        [full],
        [shape_of((tokens, width))],
        cost(6 * tokens * width * width, 14 * tokens * width + 6 * width * width),
        scratch=room(pieces, 3), weights=pieces, after=after,
    )(upper, *slopes, inputs, slope_hidden, gains)


def in_blocks(pairs, upper):
    if pairs[0][0].shape[2] % ROW_TILE == 0:
        return pairs
    result = []
    for own, other in pairs:
        both = in_order(own, other, upper[0] == 1, 2)
        halves, blocks, _, rows, columns = both.shape
        both = both.reshape(halves, 2, 1, blocks * rows, columns)
        result.append((pick(both, upper[0] == 1, 1), pick(both, upper[0] == 0, 1)))
    return result


def axis_bits(size):
    return size.bit_length() - 1


def swap_mask(values, mask):
    count = lax.axis_size("dp")
    return lax.ppermute(values, "dp", [(i, i ^ mask) for i in range(count)])


def swap_dp(values, bit):
    return swap_mask(values, 1 << bit)


def swap_tensor(values):
    return lax.ppermute(values, "tensor", [(0, 1), (1, 0)])


def bit_set(index, bit):
    return lax.rem(lax.shift_right_logical(index, bit), 2) == 1


def hold(values, *before):
    return lax.optimization_barrier((values,) + before)[0]


def in_order(own, other, upper, axis):
    return jnp.where(
        upper, jnp.stack([other, own], axis=axis), jnp.stack([own, other], axis=axis)
    )


def gather_bit(values, bit, index):
    both = in_order(values, swap_dp(values, bit), bit_set(index, bit), 2)
    return both.reshape((values.shape[0], 2 * values.shape[1]) + values.shape[2:])


def gather_tensor(values):
    return jnp.concatenate([values, swap_tensor(values)], axis=0)


def gather_far(shard, index, before):
    bits = axis_bits(lax.axis_size("dp"))
    values = hold(shard[None, None], *before)
    for bit in range(bits - 1, 1, -1):
        values = gather_bit(values, bit, index)
    return values


def gather_near(values, index, before):
    cut = values.shape[-1] // 2
    first, second = values[..., :cut], values[..., cut:]
    first, second = gather_bit(first, 1, index), gather_tensor(second)
    if before:
        first, second = hold(first, *before), hold(second, *before)
    return gather_tensor(first), gather_bit(second, 1, index)


def gather_core(first, second, before):
    if before:
        first, second = hold(first, *before), hold(second, *before)
    return [(part, swap_dp(part, 0)) for part in (first, second)]


def pick(values, upper, axis):
    return jnp.where(
        upper,
        lax.index_in_dim(values, 1, axis, keepdims=False),
        lax.index_in_dim(values, 0, axis, keepdims=False),
    )


def add_low(left, right):
    return left.astype(jnp.float32) + right.astype(jnp.float32)


def send_bit(values, bit, index):
    shape = values.shape
    values = values.reshape((shape[0], shape[1] // 2, 2) + shape[2:])
    return swap_dp(pick(values, ~bit_set(index, bit), 2), bit)


def keep_bit(values, received, bit, index):
    shape = values.shape
    values = values.reshape((shape[0], shape[1] // 2, 2) + shape[2:])
    return add_low(pick(values, bit_set(index, bit), 2), received)


def reduce_bit(values, bit, index):
    values = values.astype(jnp.bfloat16)
    return keep_bit(values, send_bit(values, bit, index), bit, index)


def joined(pieces):
    return jnp.concatenate([add_low(*pair) for pair in pieces], axis=-1).astype(jnp.bfloat16)


def sum_everywhere(values):
    values = values + swap_tensor(values)
    for bit in range(axis_bits(lax.axis_size("dp"))):
        values = values + swap_dp(values, bit)
    return values


def reverse_distance(table):
    return jnp.roll(table[:, ::-1], 1, axis=1)


def statistics_kernel(up_ref, self_ref, cross_ref, feed_ref, in_ref, wide_ref, bias_ref, out_ref):
    own, cross, feed = self_ref[...], cross_ref[...], feed_ref[...]
    columns = in_ref.shape[2]
    rows = own.shape[0]
    lane = lanes((rows, 128))
    squares = sum(jnp.sum(x * x, axis=-1, keepdims=True) for x in (own, cross, feed))

    def along(gradient, weight):
        weight = weight.astype(jnp.bfloat16).astype(jnp.float32)
        return jnp.sum(gradient * weight, axis=-1, keepdims=True)

    zero = sum(along(own[:, i * columns : (i + 1) * columns], in_ref[i]) for i in range(3))
    one = along(cross[:, 3 * columns : 4 * columns], in_ref[3])
    two = 0.0
    for tile in range(wide_ref.shape[1] // FF_TILE):
        two += along(
            feed[:, 2 * tile * FF_TILE : (2 * tile + 1) * FF_TILE],
            wide_ref[:, tile * FF_TILE : (tile + 1) * FF_TILE],
        )
    out = jnp.where(lane == 0, zero, 0.0)
    for place, column in ((1, one), (2, two), (3, squares)):
        out = jnp.where(lane == place, column, out)
    out_ref[:rows] = out
    out_ref[rows:] = bias_ref[...]


def statistics(upper, own, cross, feed, attention_in, expand_weight, bias):
    operands = (own, cross, feed, attention_in, expand_weight, bias)
    rows = own.shape[0] + bias.shape[0]
    return call(
        statistics_kernel, "statistics", (1,), [whole(x.shape) for x in operands],
        whole((rows, 128)), shape_of((rows, 128), jnp.float32),
        cost(4 * own.size, 4 * sum(x.size for x in operands)),
    )(upper, *operands)


def adam_update(weight, gradient, moment, square, learn_rate, weight_decay):
    new_moment = BETA_ONE * moment + (1.0 - BETA_ONE) * gradient
    new_square = BETA_TWO * square + (1.0 - BETA_TWO) * gradient * gradient
    direction = (
        new_moment
        / (1.0 - BETA_ONE**STEP)
        / (jnp.sqrt(new_square / (1.0 - BETA_TWO**STEP)) + ADAM_EPS)
    )
    return (new_moment, new_square, weight - learn_rate * (direction + weight_decay * weight))


def update_kernel(up_ref, clip_ref, own_ref, cross_ref, feed_ref, *refs):
    ins, outs = refs[:12], refs[12:]
    clip = clip_ref[0]
    columns = ins[0].shape[2]

    def step(group, at, gradient):
        weight, moment, square = (ins[3 * group + i][at] for i in range(3))
        new = adam_update(weight, gradient * clip, moment, square, MATRIX_RATE, DECAY_RATE)
        for i in range(3):
            outs[3 * group + i][at] = new[i]

    every = slice(None)
    for place in range(3):
        step(0, place, own_ref[:, place * columns : (place + 1) * columns])
    for place, source in ((3, 3), (4, 1), (5, 2)):
        step(0, place, cross_ref[:, source * columns : (source + 1) * columns])
    for place, source in ((0, 4), (1, 0)):
        step(1, place, cross_ref[:, source * columns : (source + 1) * columns])
    for tile in range(ins[6].shape[1] // FF_TILE):
        for group in (2, 3):
            first = (2 * tile + group - 2) * FF_TILE
            step(group, (every, slice(tile * FF_TILE, (tile + 1) * FF_TILE)), feed_ref[:, first : first + FF_TILE])


def update(upper, clip, own, cross, feed, states):
    operands = (own, cross, feed) + tuple(states)
    out = [shape_of(states[i].shape, jnp.float32) for i in range(12)]
    return call(
        update_kernel, "update", (1,),
        [pl.BlockSpec(memory_space=pltpu.SMEM)] + [whole(x.shape) for x in operands],
        [whole(x.shape) for x in out], out,
        cost(20 * own.size, 8 * sum(x.size for x in operands)),
    )(upper, clip, *operands)


def interleave(left, right):
    rows = left.shape[0]
    parts = [part.reshape(rows, -1, 1, FF_TILE) for part in (left, right)]
    return jnp.concatenate(parts, axis=2).reshape(rows, -1)


def on_device(
    inputs,
    memory,
    dec_segments,
    mem_segments,
    mem_lengths,
    buckets,
    cotangent,
    attention_in,
    attention_out,
    expand_weight,
    contract_weight,
    norm_gains,
    position_bias,
    moment_attention_in,
    square_attention_in,
    moment_attention_out,
    square_attention_out,
    moment_expand,
    square_expand,
    moment_contract,
    square_contract,
    moment_gains,
    square_gains,
    moment_bias,
    square_bias,
):
    low = jnp.bfloat16
    everywhere = ("dp", "tensor")
    tensor_count = lax.axis_size("tensor")
    tensor_index = lax.axis_index("tensor")
    index = lax.axis_index("dp")
    rows = inputs.shape[0] // tensor_count
    length, width = inputs.shape[1], inputs.shape[2]
    keys = memory.shape[1]
    shard_rows = attention_in.shape[0]
    shards = width // shard_rows
    columns = attention_in.shape[2]
    aligned = shard_rows % ROW_TILE == 0
    upper = bit_set(index, 0).astype(jnp.int32)[None]
    split = (tensor_count, shards // 2, shard_rows)

    def own_rows(values):
        return lax.dynamic_slice_in_dim(values, tensor_index * rows, rows, 0)

    def flat(values):
        return values.reshape(values.shape[0] * values.shape[1], values.shape[2])

    def in_rows(values, size):
        return values.reshape(rows, size, values.shape[-1])

    wa = attention_in.astype(low)
    wo = attention_out.astype(low)
    shard_self = jnp.concatenate([wa[:, 0], wa[:, 1], wa[:, 2], wo[:, 0]], axis=1)
    shard_cross = jnp.concatenate([wa[:, 4], wa[:, 5], wa[:, 3], wo[:, 1]], axis=1)
    far_self = gather_far(shard_self, index, [])
    far_cross = gather_far(shard_cross, index, [far_self])
    piece_self = gather_core(*gather_near(far_self, index, []), [])
    feed_shard = interleave(expand_weight.astype(low), contract_weight.astype(low))
    feed_shard = hold(feed_shard, far_self)
    feed_weights = lax.all_gather(feed_shard, everywhere, axis=0, tiled=True).reshape(
        shards, tensor_count, shard_rows, feed_shard.shape[1]
    )
    if not aligned:
        feed_weights = jnp.transpose(feed_weights, (1, 0, 2, 3)).reshape(
            1, tensor_count, width, feed_shard.shape[1]
        )
    near_cross = gather_near(far_cross, index, [piece_self[0][1], piece_self[1][1]])
    piece_self = in_blocks(piece_self, upper)

    decoder_ids = own_rows(dec_segments)
    key_index = jnp.arange(keys, dtype=jnp.int32)
    memory_ids = jnp.where(
        key_index[None, :] < own_rows(mem_lengths)[:, None], own_rows(mem_segments), -1
    )
    dec = decoder_ids[:, :, None]
    dec_across = jnp.pad(decoder_ids, ((0, 0), (0, TABLE - length)), constant_values=-1)[:, None]
    mem_across = memory_ids[:, None]
    own_heads = position_bias.shape[1]
    heads = own_heads * tensor_count
    both_bias = jnp.concatenate([position_bias, swap_tensor(position_bias)], axis=1)
    lookup = (
        buckets[None, :] == jnp.arange(position_bias.shape[0], dtype=jnp.int32)[:, None]
    ).astype(jnp.float32)
    lookup = jnp.pad(lookup, ((0, 0), (0, TABLE - length)))
    table = jnp.einsum(
        "gd,gm->md", lookup, both_bias, precision=lax.Precision.HIGHEST,
        preferred_element_type=jnp.float32,
    )
    table = reverse_distance(table).reshape(heads // 2, 2, TABLE)
    gains = norm_gains.T

    own_inputs = flat(own_rows(inputs))
    own_memory = flat(own_rows(memory))
    own_cotangent = flat(own_rows(cotangent))
    normed_zero, qkv = project(upper, own_inputs, gains, piece_self)
    qkv = in_rows(qkv, length)
    mixed_own, logs_own = self_forward(qkv, dec, dec_across, table, 0)
    piece_cross = in_blocks(gather_core(*near_cross, [mixed_own]), upper)
    mixed_other, logs_other = self_forward(qkv, dec, dec_across, table, 1)
    self_mixed = [flat(mixed_own), flat(mixed_other)]
    hidden_one, normed_one, cross_query = after_self(
        upper, own_inputs, self_mixed, gains, piece_self + piece_cross
    )
    cross_kv = in_rows(memory_project(upper, own_memory, piece_cross), keys)
    cross_query = in_rows(cross_query, length)
    cross_mixed, cross_logs = cross_forward(cross_query, cross_kv, dec, mem_across)
    split_or_whole = split if aligned else (tensor_count, 1, width // 2)
    output, feed_slopes, slope_two, slope_cm, keep_co, send_co = feed_forward(
        upper, hidden_one, flat(cross_mixed), own_cotangent, gains, piece_cross, feed_weights, split_or_whole
    )
    output = in_rows(output, length)

    def halves_of(kept, sent):
        if aligned:
            return kept, sent
        low_half = jnp.where(upper[0] == 1, sent, kept)
        high_half = jnp.where(upper[0] == 1, kept, sent)
        both = jnp.concatenate([low_half, high_half], axis=2)
        both = both.reshape((both.shape[0], shards // 2, 2, shard_rows, both.shape[-1]))
        return pick(both, upper[0] == 1, 2), pick(both, upper[0] == 0, 2)

    if not aligned:
        feed_slopes = jnp.transpose(
            feed_slopes.reshape(tensor_count, shards, shard_rows, feed_slopes.shape[-1]), (1, 0, 2, 3)
        )
    share_feed = lax.psum_scatter(
        feed_slopes.reshape(-1, feed_slopes.shape[-1]), everywhere, scatter_dimension=0, tiled=True
    ).astype(jnp.float32)

    slope_cq, slope_ck, slope_cv = cross_backward(
        cross_query, cross_kv, dec, mem_across, cross_mixed, cross_logs, in_rows(slope_cm, length)
    )
    keep_co, send_co = halves_of(keep_co, send_co)
    got_co = swap_dp(send_co, 0)
    keep_kv, send_kv = halves_of(*outer(
        upper, own_memory, [flat(slope_ck), flat(slope_cv)], split_or_whole, "memory_outer", [got_co]
    ))
    got_kv = swap_dp(send_kv, 0)
    slope_one, slope_sm, keep_qo, send_qo = after_cross(
        upper, flat(slope_cq), normed_one, hidden_one, slope_two, self_mixed, gains,
        piece_self + piece_cross, split_or_whole, [keep_kv],
    )
    keep_qo, send_qo = halves_of(keep_qo, send_qo)
    got_qo = swap_dp(send_qo, 0)
    cross_sum = joined([(keep_co, got_co), (keep_kv, got_kv), (keep_qo, got_qo)])
    first, second = cross_sum[..., :1024], cross_sum[..., 1024:]
    first_got, second_got = swap_tensor(first[1:2]), send_bit(second, 1, index)
    slope_sm = in_rows(slope_sm, length)

    def self_half(half, mixed, logs, after):
        *slopes, diagonals = self_backward(
            qkv, dec, dec_across, table, mixed, logs, slope_sm, half, after
        )
        return [flat(slope) for slope in slopes], diagonals

    one_half = (1,) + split_or_whole[1:]
    slopes_other, diagonals_other = self_half(1, mixed_other, logs_other, [got_qo])
    first = hold(add_low(first[0:1], first_got).astype(low), slopes_other[0])
    second = hold(keep_bit(second, second_got, 1, index).astype(low), slopes_other[0])
    first_got, second_got = send_bit(first, 1, index), swap_tensor(second[1:2])
    keep_other, send_other = halves_of(
        *outer(upper, normed_zero, slopes_other, one_half, "self_outer")
    )
    got_other = swap_dp(send_other, 0)
    other_sum = add_low(keep_other, got_other).astype(low)
    cross_sum = jnp.concatenate(
        [keep_bit(first, first_got, 1, index), add_low(second[0:1], second_got)], axis=-1
    ).astype(low)
    cross_sum = hold(cross_sum, keep_other)
    cross_got = send_bit(cross_sum, 2, index)
    other_got = swap_tensor(other_sum)
    slopes_own, diagonals_own = self_half(0, mixed_own, logs_own, [other_sum])
    cross_sum = hold(keep_bit(cross_sum, cross_got, 2, index), slopes_own[0])
    bits = axis_bits(lax.axis_size("dp"))
    for bit in range(3, bits):
        cross_sum = reduce_bit(cross_sum, bit, index)
    keep_own, send_own = halves_of(
        *outer(upper, normed_zero, slopes_own, one_half, "self_outer")
    )
    got_own = swap_dp(send_own, 0)
    self_sum = (add_low(keep_own, got_own) + other_got.astype(jnp.float32)).astype(low)
    self_got = send_bit(self_sum, 1, index)
    slopes_self = [part for pair in zip(slopes_own, slopes_other) for part in pair]
    diagonals = jnp.concatenate([diagonals_own, diagonals_other], axis=0)
    (input_slope,) = input_back(
        upper, slopes_self, own_inputs, slope_one, gains, piece_self, [got_own]
    )
    self_sum = hold(keep_bit(self_sum, self_got, 1, index), input_slope)
    memory_slopes = [flat(slope_ck), flat(slope_cv)]
    memory_slopes[0] = hold(memory_slopes[0], input_slope)
    memory_grad = memory_back(upper, *memory_slopes, piece_cross, 0, [])
    for bit in range(2, bits):
        self_sum = reduce_bit(self_sum, bit, index)
        if bit == 2:
            self_sum = hold(self_sum, memory_grad)
    memory_grad = in_rows(memory_back(upper, *memory_slopes, piece_cross, 1, [memory_grad]), keys)
    share_cross, share_self = cross_sum[0, 0], self_sum[0, 0]
    input_slope = in_rows(input_slope, length)
    input_grad = (
        in_order(input_slope, swap_tensor(input_slope), tensor_index == 1, 0)
        .reshape(inputs.shape)
        .astype(jnp.float32)
    )

    bias_local = jnp.einsum(
        "gd,md->gm", lookup, reverse_distance(diagonals.reshape(heads, TABLE)),
        precision=lax.Precision.HIGHEST, preferred_element_type=jnp.float32,
    )
    bias_local = jnp.where(
        tensor_index == 1, jnp.roll(bias_local, own_heads, axis=1), bias_local
    )
    bias_rows = bias_local.size // 128
    bias_tile = jnp.pad(bias_local.reshape(bias_rows, 128), ((0, 8 - bias_rows), (0, 0)))
    table_rows = statistics(
        upper, share_self, share_cross, share_feed, jnp.swapaxes(attention_in, 0, 1), expand_weight, bias_tile
    )
    table_rows = table_rows + swap_tensor(table_rows)
    totals = table_rows[shard_rows:]
    table_rows = table_rows[:shard_rows]
    old_gains = lax.dynamic_slice_in_dim(norm_gains, index * shard_rows, shard_rows, 0)
    shared_gains = table_rows[:, :3] / old_gains
    square_sum = jnp.sum(table_rows[:, 3]) + jnp.sum(shared_gains * shared_gains)
    totals = totals + jnp.where(
        lax.broadcasted_iota(jnp.int32, totals.shape, 0) == bias_rows, square_sum, 0.0
    )
    for bit in range(bits):
        totals = totals + swap_dp(totals, bit)
    bias_sums = totals[:bias_rows].reshape(bias_local.shape)
    grad_norm = jnp.sqrt(totals[bias_rows, 0] + jnp.sum(bias_sums * bias_sums))
    clip_factor = jnp.minimum(1.0, CLIP_NORM / (grad_norm + 1e-06))

    bias_share = lax.dynamic_slice_in_dim(bias_sums, tensor_index * own_heads, own_heads, 1)
    new = update(
        upper, clip_factor[None], share_self, share_cross, share_feed,
        tuple(
            jnp.swapaxes(state, 0, 1)
            for state in (
                attention_in, moment_attention_in, square_attention_in,
                attention_out, moment_attention_out, square_attention_out,
            )
        )
        + (
            expand_weight, moment_expand, square_expand,
            contract_weight, moment_contract, square_contract,
        ),
    )
    new = [jnp.swapaxes(state, 0, 1) for state in new[:6]] + list(new[6:])
    new_gains = adam_update(
        old_gains, shared_gains * clip_factor, moment_gains, square_gains, SMALL_RATE, 0.0
    )
    new_bias = adam_update(
        position_bias, bias_share * clip_factor, moment_bias, square_bias, SMALL_RATE, 0.0
    )
    return (
        (output, input_grad, memory_grad, grad_norm)
        + tuple(new) + new_gains + new_bias
    )


def solution(mesh):
    return jax.shard_map(
        on_device,
        mesh=mesh,
        in_specs=(
            P("dp", None, None),
            P("dp", None, None),
            P("dp", None),
            P("dp", None),
            P("dp"),
            P(),
            P("dp", None, None),
            P("dp", None, "tensor"),
            P("dp", None, "tensor"),
            P("dp", "tensor"),
            P("dp", "tensor"),
            P(),
            P(None, "tensor"),
            P("dp", None, "tensor"),
            P("dp", None, "tensor"),
            P("dp", None, "tensor"),
            P("dp", None, "tensor"),
            P("dp", "tensor"),
            P("dp", "tensor"),
            P("dp", "tensor"),
            P("dp", "tensor"),
            P("dp", None),
            P("dp", None),
            P(None, "tensor"),
            P(None, "tensor"),
        ),
        out_specs=(
            P(("dp", "tensor"), None, None),
            P("dp", None, None),
            P(("dp", "tensor"), None, None),
            P(),
            P("dp", None, "tensor"),
            P("dp", None, "tensor"),
            P("dp", None, "tensor"),
            P("dp", None, "tensor"),
            P("dp", None, "tensor"),
            P("dp", None, "tensor"),
            P("dp", "tensor"),
            P("dp", "tensor"),
            P("dp", "tensor"),
            P("dp", "tensor"),
            P("dp", "tensor"),
            P("dp", "tensor"),
            P("dp", None),
            P("dp", None),
            P("dp", None),
            P(None, "tensor"),
            P(None, "tensor"),
            P(None, "tensor"),
        ),
        check_vma=False,
    )
```

```python
import functools

import jax
import jax.numpy as jnp
from jax import lax
from jax.experimental import pallas as pl
from jax.experimental.pallas import tpu as pltpu
from jax.sharding import PartitionSpec as P

STEP = 10
NORM_EPS = 1e-06
CLIP_NORM = 1.0
BETA_ONE = 0.9
BETA_TWO = 0.95
ADAM_EPS = 1e-08
MATRIX_RATE = 0.08
SMALL_RATE = 0.8
DECAY_RATE = 0.1
GELU_SCALE = 0.7978845608028654
GELU_CUBIC = 0.044715
MASKED = -1e30
TABLE = 384
NT = (((1,), (1,)), ((), ()))
TN = (((0,), (0,)), ((), ()))


def dot(a, b, dims=(((1,), (0,)), ((), ()))):
    return lax.dot_general(a, b, dims, preferred_element_type=jnp.float32)


def lanes(shape):
    return lax.broadcasted_iota(jnp.int32, shape, len(shape) - 1)


def half_of(values, which):
    return jnp.where((lanes(values.shape) >= 64) == (which == 1), values, jnp.zeros_like(values))


def column(values, index):
    return jnp.sum(jnp.where(lanes(values.shape) == index, values, 0.0), axis=-1, keepdims=True)


def cross_forward_kernel(q_ref, k_ref, v_ref, dec_ref, mem_ref, o_ref, lse_ref):
    pair = pl.program_id(1)
    query, key, value = q_ref[0], k_ref[0], v_ref[0]
    allowed = dec_ref[0] == mem_ref[0]
    mixed, logs = forward_pair(query, key, value, [None, None], allowed)
    o_ref[0] = mixed.astype(o_ref.dtype)
    store_logs(lse_ref, logs, pair)


def store_logs(lse_ref, logs, pair):
    @pl.when(pair == 0)
    def _():
        lse_ref[0] = jnp.zeros(lse_ref.shape[1:], jnp.float32)

    lane = lanes(lse_ref.shape[1:])
    kept = lse_ref[0]
    for which in range(2):
        kept = jnp.where(lane == 2 * pair + which, logs[which], kept)
    lse_ref[0] = kept


def forward_pair(query, key, value, biases, allowed):
    mixed = jnp.zeros(query.shape, jnp.float32)
    logs = []
    for which in range(2):
        scores = dot(half_of(query, which), key, NT)
        if biases[which] is not None:
            scores = scores + biases[which]
        scores = jnp.where(allowed, scores, MASKED)
        top = jnp.max(scores, axis=-1, keepdims=True)
        weights = jnp.exp(scores - top)
        total = jnp.sum(weights, axis=-1, keepdims=True)
        logs.append(top + jnp.log(total))
        mixed = mixed + dot(weights.astype(jnp.bfloat16), half_of(value, which)) * (1.0 / total)
    return mixed, logs


def backward_pair(query, key, value, mixed, upstream, logs, biases, allowed):
    slope_q = jnp.zeros(query.shape, jnp.float32)
    slope_k = jnp.zeros(key.shape, jnp.float32)
    slope_v = jnp.zeros(key.shape, jnp.float32)
    grads = []
    product = upstream.astype(jnp.float32) * mixed.astype(jnp.float32)
    for which in range(2):
        query_half = half_of(query, which)
        up_half = half_of(upstream, which)
        scores = dot(query_half, key, NT)
        if biases[which] is not None:
            scores = scores + biases[which]
        prob = jnp.exp(jnp.where(allowed, scores - logs[which], MASKED))
        slope_p = dot(up_half, value, NT)
        inner = jnp.sum(half_of(product, which), axis=-1, keepdims=True)
        grad = (prob * (slope_p - inner)).astype(jnp.bfloat16)
        slope_q = slope_q + dot(grad, half_of(key, which))
        slope_k = slope_k + dot(grad, query_half, TN)
        slope_v = slope_v + dot(prob.astype(jnp.bfloat16), up_half, TN)
        grads.append(grad)
    return slope_q, slope_k, slope_v, grads


def cross_backward_kernel(
    q_ref, k_ref, v_ref, dec_ref, mem_ref, o_ref, lse_ref, up_ref, dq_ref, dk_ref, dv_ref
):
    pair = pl.program_id(1)
    allowed = dec_ref[0] == mem_ref[0]
    logs = [column(lse_ref[0], 2 * pair + which) for which in range(2)]
    slope_q, slope_k, slope_v, _ = backward_pair(
        q_ref[0], k_ref[0], v_ref[0], o_ref[0], up_ref[0], logs, [None, None], allowed
    )
    dq_ref[0] = slope_q.astype(jnp.bfloat16)
    dk_ref[0] = slope_k.astype(jnp.bfloat16)
    dv_ref[0] = slope_v.astype(jnp.bfloat16)


def pad_keys(values):
    extra = TABLE - values.shape[0]
    return jnp.concatenate([values, jnp.zeros((extra, values.shape[1]), values.dtype)], axis=0)


def self_allowed(dec_ref, decT_ref):
    length = dec_ref.shape[1]
    rows = lax.broadcasted_iota(jnp.int32, (length, TABLE), 0)
    return (dec_ref[0] == decT_ref[0]) & (lanes((length, TABLE)) <= rows)


def toeplitz(table_ref, which, length):
    spread = jnp.broadcast_to(table_ref[0, which : which + 1, :], (length, TABLE))
    return pltpu.roll(spread, 0, 1, stride=1, stride_axis=0)


def self_forward_kernel(q_ref, k_ref, v_ref, dec_ref, decT_ref, table_ref, o_ref, lse_ref):
    pair = pl.program_id(1)
    length = q_ref.shape[1]
    biases = [toeplitz(table_ref, which, length) for which in range(2)]
    mixed, logs = forward_pair(
        q_ref[0], pad_keys(k_ref[0]), pad_keys(v_ref[0]), biases, self_allowed(dec_ref, decT_ref)
    )
    o_ref[0] = mixed.astype(o_ref.dtype)
    store_logs(lse_ref, logs, pair)


def self_backward_kernel(ties, *refs):
    q_ref, k_ref, v_ref, dec_ref, decT_ref, table_ref, o_ref, lse_ref, up_ref = refs[:9]
    dq_ref, dk_ref, dv_ref, diag_ref = refs[9 + ties :]
    pair, row = pl.program_id(0), pl.program_id(1)
    length = q_ref.shape[1]
    biases = [toeplitz(table_ref, which, length) for which in range(2)]
    logs = [column(lse_ref[0], 2 * pair + which) for which in range(2)]
    slope_q, slope_k, slope_v, grads = backward_pair(
        q_ref[0], pad_keys(k_ref[0]), pad_keys(v_ref[0]), o_ref[0], up_ref[0], logs, biases,
        self_allowed(dec_ref, decT_ref),
    )
    dq_ref[0] = slope_q.astype(jnp.bfloat16)
    dk_ref[0] = slope_k[:length].astype(jnp.bfloat16)
    dv_ref[0] = slope_v[:length].astype(jnp.bfloat16)

    @pl.when(row == 0)
    def _():
        diag_ref[...] = jnp.zeros(diag_ref.shape, jnp.float32)

    for which in range(2):
        diag_ref[0, which : which + 1, :] += diagonal_sums(grads[which].astype(jnp.float32))


def diagonal_sums(values):
    groups = jnp.zeros((8, TABLE), jnp.float32)
    for start in range(0, values.shape[0], 8):
        groups = groups + pltpu.roll(values[start : start + 8], (TABLE - start) % TABLE, 1)
    total = groups[0:1]
    for row in range(1, 8):
        total = total + pltpu.roll(groups, TABLE - row, 1)[row : row + 1]
    return total


def params(count):
    return pltpu.CompilerParams(
        dimension_semantics=("arbitrary",) * count, vmem_limit_bytes=48 * 1024 * 1024
    )


def cross_forward(q, kv, dec, mem):
    rows, length, width = q.shape
    keys = kv.shape[1]
    pairs = width // 128
    lanes_q = pl.BlockSpec((1, length, 128), lambda r, p: (r, 0, p))
    lanes_k = pl.BlockSpec((1, keys, 128), lambda r, p: (r, 0, p))
    lanes_v = pl.BlockSpec((1, keys, 128), lambda r, p: (r, 0, p + pairs))
    return pl.pallas_call(
        cross_forward_kernel,
        grid=(rows, width // 128),
        in_specs=[
            lanes_q, lanes_k, lanes_v,
            pl.BlockSpec((1, length, 1), lambda r, p: (r, 0, 0)),
            pl.BlockSpec((1, 1, keys), lambda r, p: (r, 0, 0)),
        ],
        out_specs=[lanes_q, pl.BlockSpec((1, length, 128), lambda r, p: (r, 0, 0))],
        out_shape=[
            jax.ShapeDtypeStruct((rows, length, width), jnp.bfloat16),
            jax.ShapeDtypeStruct((rows, length, 128), jnp.float32),
        ],
        compiler_params=params(2),
        cost_estimate=cost(4 * rows * length * keys * width, 2 * rows * width * (2 * length + 2 * keys), 2 * rows * length * keys * pairs),
        name="cross_forward",
    )(q, kv, kv, dec, mem)


def cross_backward(q, kv, dec, mem, mixed, logs, upstream):
    rows, length, width = q.shape
    keys = kv.shape[1]
    pairs = width // 128
    lanes_q = pl.BlockSpec((1, length, 128), lambda r, p: (r, 0, p))
    lanes_k = pl.BlockSpec((1, keys, 128), lambda r, p: (r, 0, p))
    lanes_v = pl.BlockSpec((1, keys, 128), lambda r, p: (r, 0, p + pairs))
    return pl.pallas_call(
        cross_backward_kernel,
        grid=(rows, width // 128),
        in_specs=[
            lanes_q, lanes_k, lanes_v,
            pl.BlockSpec((1, length, 1), lambda r, p: (r, 0, 0)),
            pl.BlockSpec((1, 1, keys), lambda r, p: (r, 0, 0)),
            lanes_q, pl.BlockSpec((1, length, 128), lambda r, p: (r, 0, 0)), lanes_q,
        ],
        out_specs=[lanes_q, lanes_k, lanes_k],
        out_shape=[
            jax.ShapeDtypeStruct((rows, length, width), jnp.bfloat16),
            jax.ShapeDtypeStruct((rows, keys, width), jnp.bfloat16),
            jax.ShapeDtypeStruct((rows, keys, width), jnp.bfloat16),
        ],
        compiler_params=params(2),
        cost_estimate=cost(10 * rows * length * keys * width, 2 * rows * width * (4 * length + 4 * keys), 2 * rows * length * keys * pairs),
        name="cross_backward",
    )(q, kv, kv, dec, mem, mixed, logs, upstream)


def self_forward(qkv, dec, decT, table, half):
    rows, length, width = qkv.shape
    count = width // 384
    first = half * count
    spec = pl.BlockSpec((1, length, 128), lambda r, p: (r, 0, p))
    spec_k = pl.BlockSpec((1, length, 128), lambda r, p: (r, 0, p + count))
    spec_v = pl.BlockSpec((1, length, 128), lambda r, p: (r, 0, p + 2 * count))
    return pl.pallas_call(
        self_forward_kernel,
        grid=(rows, count),
        in_specs=[
            spec, spec_k, spec_v,
            pl.BlockSpec((1, length, 1), lambda r, p: (r, 0, 0)),
            pl.BlockSpec((1, 1, TABLE), lambda r, p: (r, 0, 0)),
            pl.BlockSpec((1, 2, TABLE), lambda r, p: (p + first, 0, 0)),
        ],
        out_specs=[
            pl.BlockSpec((1, length, 128), lambda r, p: (r, 0, p)),
            pl.BlockSpec((1, length, 128), lambda r, p: (r, 0, 0)),
        ],
        out_shape=[
            jax.ShapeDtypeStruct((rows, length, width // 3), jnp.bfloat16),
            jax.ShapeDtypeStruct((rows, length, 128), jnp.float32),
        ],
        compiler_params=params(2),
        cost_estimate=cost(2 * rows * length * TABLE * width // 3, 8 * rows * width * length // 3, 2 * rows * length * TABLE * count),
        name="self_forward",
    )(qkv, qkv, qkv, dec, decT, table)


def self_backward(qkv, dec, decT, table, mixed, logs, upstream, half, after):
    rows, length, width = qkv.shape
    count = width // 384
    first = half * count
    spec = pl.BlockSpec((1, length, 128), lambda p, r: (r, 0, p))
    spec_k = pl.BlockSpec((1, length, 128), lambda p, r: (r, 0, p + count))
    spec_v = pl.BlockSpec((1, length, 128), lambda p, r: (r, 0, p + 2 * count))
    spec_up = pl.BlockSpec((1, length, 128), lambda p, r: (r, 0, p + first))
    out = jax.ShapeDtypeStruct((rows, length, width // 3), jnp.bfloat16)
    return pl.pallas_call(
        functools.partial(self_backward_kernel, len(after)),
        grid=(count, rows),
        in_specs=[
            spec, spec_k, spec_v,
            pl.BlockSpec((1, length, 1), lambda p, r: (r, 0, 0)),
            pl.BlockSpec((1, 1, TABLE), lambda p, r: (r, 0, 0)),
            pl.BlockSpec((1, 2, TABLE), lambda p, r: (p + first, 0, 0)), spec,
            pl.BlockSpec((1, length, 128), lambda p, r: (r, 0, 0)), spec_up,
        ] + [pl.BlockSpec(memory_space=pl.ANY)] * len(after),
        out_specs=[spec, spec, spec, pl.BlockSpec((1, 2, TABLE), lambda p, r: (p, 0, 0))],
        out_shape=[out, out, out, jax.ShapeDtypeStruct((count, 2, TABLE), jnp.float32)],
        compiler_params=params(2),
        cost_estimate=cost(5 * rows * length * TABLE * width // 3, 16 * rows * width * length // 3, 2 * rows * length * TABLE * count),
        name="self_backward",
    )(qkv, qkv, qkv, dec, decT, table, mixed, logs, upstream, *after)


SLOPE = GELU_SCALE * 3.0 * GELU_CUBIC
ROW_TILE = 16
FF_TILE = 512
MEMORY_TILE = 512


def whole(shape):
    return pl.BlockSpec(shape, lambda *_: (0,) * len(shape))


def cost(flops, moved, exps=0):
    return pl.CostEstimate(flops=int(flops), bytes_accessed=int(moved), transcendentals=int(exps))


def row_scale(hidden):
    return lax.rsqrt(jnp.mean(hidden * hidden, axis=-1, keepdims=True) + NORM_EPS)


def row_back(hidden, gain, upstream):
    factor = row_scale(hidden)
    scaled = upstream * hidden
    inner = jnp.mean(scaled * gain, axis=-1, keepdims=True)
    slope = factor * (upstream * gain) - (factor * factor * factor * inner) * hidden
    return slope


def emit(gradient, keep_ref, send_ref, start, upper):
    halves, blocks, rows, _ = keep_ref.shape
    columns = gradient.shape[1] // halves
    for half in range(halves):
        part = gradient[:, half * columns : (half + 1) * columns]
        part = part.reshape(blocks, 2, rows, columns)
        low, high = part[:, 0], part[:, 1]
        keep = jnp.where(upper, high, low).astype(jnp.bfloat16)
        send = jnp.where(upper, low, high).astype(jnp.bfloat16)
        keep_ref[half, :, :, start : start + columns] = keep
        send_ref[half, :, :, start : start + columns] = send


def call(kernel, name, grid, in_specs, out_specs, out_shape, work, scratch=(), weights=(), after=(), aliases=None):
    count, loaded = len(in_specs), 2 * len(weights)
    outs = len(out_specs) if isinstance(out_specs, list) else 1

    def run(up_ref, *refs):
        ins = refs[:count]
        pieces = refs[count : count + loaded]
        kernel(up_ref, *ins, pieces, *refs[count + loaded + len(after) :])

    anywhere = pl.BlockSpec(memory_space=pl.ANY)
    return lambda upper, *operands: pl.pallas_call(
        run if weights else lambda up_ref, *refs: kernel(up_ref, *refs[:count], *refs[count + len(after) :]),
        grid_spec=pltpu.PrefetchScalarGridSpec(
            num_scalar_prefetch=1,
            grid=grid,
            in_specs=in_specs + [anywhere] * (loaded + len(after)),
            out_specs=out_specs,
            scratch_shapes=scratch,
        ),
        out_shape=out_shape,
        input_output_aliases=aliases or {},
        compiler_params=pltpu.CompilerParams(
            dimension_semantics=("arbitrary",) * len(grid), vmem_limit_bytes=56 * 1024 * 1024
        ),
        cost_estimate=work,
        name=name,
    )(upper, *operands, *[piece for pair in weights for piece in pair], *after)


def fetch(pieces, store, sems, mats, upper):
    copies = []
    columns = store.shape[3] // len(mats)
    for place, (source, begin, half) in enumerate(mats):
        group = []
        for other in range(2):
            piece = pieces[4 * source + 2 * half + other]
            copy = pltpu.make_async_copy(
                piece.at[half % piece.shape[0], :, :, pl.ds(begin, columns)],
                store.at[:, (upper + other) % 2, :, pl.ds(place * columns, columns)],
                sems.at[place * 2 + other],
            )
            group.append(copy)
        copies.append(group)
    return copies


def start(copies):
    for group in copies:
        for copy in group:
            copy.start()


def wait(group):
    for copy in group:
        copy.wait()


def shape_of(shape, kind=jnp.bfloat16):
    return jax.ShapeDtypeStruct(shape, kind)


def kernel_of(store, place, width):
    return store[:, :, :, place * width : (place + 1) * width].reshape(store.shape[0] * 2 * store.shape[2], width)


def room(weights, count):
    _, blocks, rows, columns = weights[0][0].shape
    wide = count * (columns // 4)
    return [pltpu.VMEM((blocks, 2, rows, wide), jnp.bfloat16), pltpu.SemaphoreType.DMA((2 * count,))]


QKV, SO = (0, 1, 2), 3
CKV, CQ, CO = (0, 1), 2, 3


def placed(mats, pieces, source=0, halves=(0, 1)):
    columns = pieces[0].shape[3] // 4
    return [(source, which * columns, half) for which in mats for half in halves]


def project_kernel(half, up_ref, x_ref, gain_ref, pieces, n_ref, out_ref, store, sems):
    copies = fetch(pieces, store, sems, placed(QKV, pieces, 0, (half,)), up_ref[0])

    @pl.when(pl.program_id(0) == 0)
    def _():
        start(copies)
        hidden = x_ref[...].astype(jnp.float32)
        n_ref[...] = (hidden * row_scale(hidden) * gain_ref[0:1]).astype(jnp.bfloat16)

    width = out_ref.shape[1]
    for place in range(3):
        @pl.when(pl.program_id(0) == place)
        def _():
            wait(copies[place])
            out_ref[...] = dot(n_ref[...], kernel_of(store, place, width)).astype(jnp.bfloat16)


def own_spec(tokens, width):
    return pl.BlockSpec((tokens, width), lambda g, up: (up[1], 0))


def project(upper, inputs, gains, pieces, half):
    tokens, width = inputs.shape[0] // 2, inputs.shape[1]
    wide = width // 2
    return call(
        functools.partial(project_kernel, half), "project", (3,),
        [own_spec(tokens, width), whole(gains.shape)],
        [whole((tokens, width)), pl.BlockSpec((tokens, wide), lambda g, *_: (0, g))],
        [shape_of((tokens, width)), shape_of((tokens, 3 * wide))],
        cost(3 * tokens * width * width, 2 * width * (3 * tokens + 2 * width)), scratch=room(pieces, 3), weights=pieces,
    )(upper, inputs, gains)


def memory_project_kernel(up_ref, x_ref, pieces, out_ref, store, sems):
    copies = fetch(pieces, store, sems, placed(CKV, pieces), up_ref[0])

    @pl.when(pl.program_id(0) == 0)
    def _():
        start(copies)
        for group in copies:
            wait(group)

    width = x_ref.shape[1]
    out_ref[...] = dot(x_ref[...], kernel_of(store, 0, 2 * width)).astype(jnp.bfloat16)


def memory_project(upper, memory, pieces):
    tokens, width = memory.shape[0] // 2, memory.shape[1]
    tile = MEMORY_TILE
    steps = tokens // tile
    return call(
        memory_project_kernel, "memory_project", (steps,),
        [pl.BlockSpec((tile, width), lambda g, up: (up[1] * steps + g, 0))],
        pl.BlockSpec((tile, 2 * width), lambda g, *_: (g, 0)),
        shape_of((tokens, 2 * width)),
        cost(4 * tokens * width * width, 2 * width * (3 * tokens + 2 * width)), scratch=room(pieces, 4), weights=pieces,
    )(upper, memory)


def after_self_kernel(up_ref, x_ref, a_ref, b_ref, gain_ref, pieces, h_ref, n_ref, q_ref, store, sems):
    copies = fetch(pieces, store, sems, placed([SO], pieces) + placed([CQ], pieces, 1), up_ref[0])

    @pl.when(pl.program_id(0) == 0)
    def _():
        start(copies)
        for group in copies:
            wait(group)

    width = x_ref.shape[1]
    weight = kernel_of(store, 0, width)
    hidden = x_ref[...].astype(jnp.float32) + dot(a_ref[...], weight[:, : width // 2], NT)
    hidden += dot(b_ref[...], weight[:, width // 2 :], NT)
    h_ref[...] = hidden
    normed = (hidden * row_scale(hidden) * gain_ref[1:2]).astype(jnp.bfloat16)
    n_ref[...] = normed
    q_ref[...] = dot(normed, kernel_of(store, 1, width)).astype(jnp.bfloat16)


def after_self(upper, inputs, mixed, gains, pieces):
    tokens, width = inputs.shape[0] // 2, inputs.shape[1]
    tile = tokens // 2
    rows = pl.BlockSpec((tile, width), lambda g, *_: (g, 0))
    half = pl.BlockSpec((tile, width // 2), lambda g, *_: (g, 0))
    return call(
        after_self_kernel, "after_self", (2,),
        [pl.BlockSpec((tile, width), lambda g, up: (2 * up[1] + g, 0)), half, half, whole(gains.shape)],
        [rows, rows, rows],
        [shape_of((tokens, width), jnp.float32), shape_of((tokens, width)), shape_of((tokens, width))],
        cost(4 * tokens * width * width, width * (12 * tokens + 4 * width)), scratch=room(pieces, 4), weights=pieces,
    )(upper, inputs, *mixed, gains)


def feed_kernel(
    up_ref, h1_ref, a_ref, gy_ref, gain_ref, w_ref, pieces,
    y_ref, g_ref, gh_ref, ga_ref, keep_ref, send_ref,
    n_ref, nT_ref, gyT_ref, acc_ref, store, sems,
):
    step = pl.program_id(0)
    tile = FF_TILE
    width = y_ref.shape[1]
    copies = fetch(pieces, store, sems, placed([CO], pieces), up_ref[0])

    @pl.when(step == 0)
    def _():
        start(copies)
        gyT_ref[...] = gy_ref[...].T
        wait(copies[0])
        wait(copies[1])
        hidden = h1_ref[...] + dot(a_ref[...], kernel_of(store, 0, width), NT)
        gh_ref[...] = hidden
        y_ref[...] = hidden
        normed = (hidden * row_scale(hidden) * gain_ref[2:3]).astype(jnp.bfloat16)
        n_ref[...] = normed
        nT_ref[...] = normed.T
        acc_ref[...] = jnp.zeros(acc_ref.shape, jnp.float32)

    wi = w_ref[:, 0, :, :tile].reshape(width, tile)
    wf = w_ref[:, 0, :, tile:].reshape(width, tile)
    u = dot(n_ref[...], wi)
    square = u * u
    bent = jnp.tanh(u * (GELU_SCALE + (GELU_SCALE * GELU_CUBIC) * square))
    half = 0.5 + 0.5 * bent
    act = (u * half).astype(jnp.bfloat16)
    slope = half + (0.5 * u) * (1.0 - bent * bent) * (GELU_SCALE + SLOPE * square)
    gu = (dot(gy_ref[...], wf) * slope).astype(jnp.bfloat16)
    y_ref[...] += dot(act, wf, NT)
    acc_ref[...] += dot(gu, wi, NT)
    g_ref[:, 0, :, :tile] = dot(nT_ref[...], gu).reshape(g_ref.shape[0], g_ref.shape[2], tile).astype(jnp.bfloat16)
    g_ref[:, 0, :, tile:] = dot(gyT_ref[...], act).reshape(g_ref.shape[0], g_ref.shape[2], tile).astype(jnp.bfloat16)

    @pl.when(step == pl.num_programs(0) - 1)
    def _():
        back = row_back(gh_ref[...], gain_ref[2:3], acc_ref[...])
        total = gy_ref[...].astype(jnp.float32) + back
        gh_ref[...] = total
        low = total.astype(jnp.bfloat16)
        ga_ref[...] = dot(low, kernel_of(store, 0, width)).astype(jnp.bfloat16)
        emit(dot(low.T, a_ref[...]), keep_ref, send_ref, 0, up_ref[0] == 1)


def feed_forward(upper, hidden, mixed, cotangent, gains, pieces, weights, split):
    tokens, width = hidden.shape
    blocks, halves, rows, wide = weights.shape
    steps = wide // (2 * FF_TILE)
    spec = pl.BlockSpec((blocks, 1, rows, 2 * FF_TILE), lambda g, *_: (0, g // steps, 0, g % steps))
    full = whole((tokens, width))
    f32 = shape_of((tokens, width), jnp.float32)
    columns = width // halves
    return call(
        feed_kernel, "feed_forward", (halves * steps,),
        [full, full, own_spec(tokens, width), whole(gains.shape), spec],
        [full, spec, full, full, whole(split + (columns,)), whole(split + (columns,))],
        [f32, shape_of(weights.shape), f32, shape_of((tokens, width)),
         shape_of(split + (columns,)), shape_of(split + (columns,))],
        cost(6 * tokens * width * halves * wide, 40 * tokens * width, tokens * halves * wide / 2),
        scratch=[
            pltpu.VMEM((tokens, width), jnp.bfloat16), pltpu.VMEM((width, tokens), jnp.bfloat16),
            pltpu.VMEM((width, tokens), jnp.bfloat16), pltpu.VMEM((tokens, width), jnp.float32),
        ] + room(pieces, 2), weights=pieces,
    )(upper, hidden, mixed, cotangent, gains, weights)


def after_cross_kernel(
    up_ref, gq_ref, n_ref, h_ref, gh_ref, a_ref, b_ref, gain_ref, pieces,
    gh1_ref, ga_ref, keep_ref, send_ref, store, sems,
):
    copies = fetch(pieces, store, sems, placed([SO], pieces) + placed([CQ], pieces, 1), up_ref[0])
    start(copies)
    upper = up_ref[0] == 1
    columns = keep_ref.shape[3] // 2
    width = h_ref.shape[1]
    emit(dot(n_ref[...].T, gq_ref[...]), keep_ref, send_ref, 0, upper)
    wait(copies[2])
    wait(copies[3])
    back = row_back(h_ref[...], gain_ref[1:2], dot(gq_ref[...], kernel_of(store, 1, width), NT))
    total = gh_ref[...] + back
    gh1_ref[...] = total
    low = total.astype(jnp.bfloat16)
    wait(copies[0])
    wait(copies[1])
    ga_ref[...] = dot(low, kernel_of(store, 0, width)).astype(jnp.bfloat16)
    across = low.T
    emit(dot(across, a_ref[...]), keep_ref.at[0:1], send_ref.at[0:1], columns, upper)
    emit(dot(across, b_ref[...]), keep_ref.at[1:2], send_ref.at[1:2], columns, upper)


def after_cross(upper, slope_q, normed, hidden, slope_hidden, mixed, gains, pieces, split, after):
    tokens, width = hidden.shape
    full = whole((tokens, width))
    piece = split + (2 * (width // split[0]),)
    return call(
        after_cross_kernel, "after_cross", (1,),
        [full, full, full, full, whole((tokens, width // 2)), whole((tokens, width // 2)), whole(gains.shape)],
        [full, full, whole(piece), whole(piece)],
        [shape_of((tokens, width), jnp.float32), shape_of((tokens, width)),
         shape_of(piece), shape_of(piece)],
        cost(8 * tokens * width * width, tokens * width * 24 + 8 * width * width),
        scratch=room(pieces, 4), weights=pieces, after=after,
    )(upper, slope_q, normed, hidden, slope_hidden, *mixed, gains)


def outer_kernel(up_ref, x_ref, *refs):
    slopes, keep_ref, send_ref = refs[:-2], refs[-2], refs[-1]
    upper = up_ref[0] == 1
    columns = keep_ref.shape[3] // len(slopes)
    across = x_ref[...].T
    for place, slope in enumerate(slopes):
        emit(dot(across, slope[...]), keep_ref, send_ref, place * columns, upper)


def outer(upper, rows, slopes, split, name, after=()):
    tokens, width = slopes[0].shape[0], rows.shape[1]
    wide = slopes[0].shape[1]
    piece = split + (len(slopes) * (wide // split[0]),)
    return call(
        outer_kernel, name, (1,),
        [whole(rows.shape) if rows.shape[0] == tokens else own_spec(tokens, width)]
        + [whole(slope.shape) for slope in slopes],
        [whole(piece), whole(piece)],
        [shape_of(piece), shape_of(piece)],
        cost(2 * tokens * width * wide * len(slopes), 2 * (tokens + width) * (width + wide * len(slopes))),
        after=after,
    )(upper, rows, *slopes)


def memory_back_kernel(up_ref, gk_ref, gv_ref, pieces, out_ref, store, sems):
    copies = fetch(pieces, store, sems, placed(CKV, pieces), up_ref[0])

    @pl.when(pl.program_id(0) == 0)
    def _():
        start(copies)
        for group in copies:
            wait(group)

    width = gk_ref.shape[1]
    out_ref[...] = dot(gk_ref[...], kernel_of(store, 0, width), NT) + dot(gv_ref[...], kernel_of(store, 1, width), NT)


def memory_back(upper, slope_k, slope_v, pieces, part, earlier):
    tokens, width = slope_k.shape
    tile = MEMORY_TILE
    first = part * (tokens // 2 // tile)
    rows = pl.BlockSpec((tile, width), lambda g, *_: (g + first, 0))
    in_specs = [rows, rows] + [pl.BlockSpec(memory_space=pl.ANY)] * len(earlier)
    return call(
        lambda up_ref, gk_ref, gv_ref, *refs: memory_back_kernel(up_ref, gk_ref, gv_ref, *refs[len(earlier) :]),
        "memory_back", (tokens // 2 // tile,),
        in_specs, rows, shape_of((tokens, width), jnp.float32),
        cost(2 * tokens * width * width, width * (4 * tokens + 4 * width)),
        scratch=room(pieces, 4), weights=pieces, aliases={3: 0} if earlier else {},
    )(upper, slope_k, slope_v, *earlier)


def input_back_kernel(up_ref, *refs):
    slopes, (x_ref, gh_ref, gain_ref, pieces, out_ref, store, sems) = refs[:6], refs[6:]
    copies = fetch(pieces, store, sems, placed(QKV, pieces), up_ref[0])
    start(copies)
    width = x_ref.shape[1]
    half = width // 2
    upstream = 0.0
    for place in range(6):
        wait(copies[place])
        upstream += dot(slopes[place][...], kernel_of(store, place, half), NT)
    back = row_back(x_ref[...].astype(jnp.float32), gain_ref[0:1], upstream)
    out_ref[...] = (gh_ref[...] + back).astype(jnp.bfloat16)


def input_back(upper, slopes, inputs, slope_hidden, gains, pieces, after):
    tokens, width = inputs.shape[0] // 2, inputs.shape[1]
    full = whole((tokens, width))
    return call(
        input_back_kernel, "input_back", (1,),
        [whole((tokens, width // 2))] * 6 + [own_spec(tokens, width), full, whole(gains.shape)],
        [full],
        [shape_of((tokens, width))],
        cost(6 * tokens * width * width, width * (14 * tokens + 6 * width)),
        scratch=room(pieces, 6), weights=pieces, after=after,
    )(upper, *slopes, inputs, slope_hidden, gains)


def in_blocks(pairs, upper):
    if pairs[0][0].shape[2] % ROW_TILE == 0:
        return pairs
    result = []
    for own, other in pairs:
        both = in_order(own, other, upper[0] == 1, 2)
        halves, blocks, _, rows, columns = both.shape
        both = both.reshape(halves, 2, 1, blocks * rows, columns)
        result.append((pick(both, upper[0] == 1, 1), pick(both, upper[0] == 0, 1)))
    return result


def axis_bits(size):
    return size.bit_length() - 1


def swap_mask(values, mask):
    count = lax.axis_size("dp")
    return lax.ppermute(values, "dp", [(i, i ^ mask) for i in range(count)])


def swap_dp(values, bit):
    return swap_mask(values, 1 << bit)


def swap_tensor(values):
    return lax.ppermute(values, "tensor", [(0, 1), (1, 0)])


def bit_set(index, bit):
    return lax.rem(lax.shift_right_logical(index, bit), 2) == 1


def hold(values, *before):
    return lax.optimization_barrier((values,) + before)[0]


def in_order(own, other, upper, axis):
    return jnp.where(
        upper, jnp.stack([other, own], axis=axis), jnp.stack([own, other], axis=axis)
    )


def gather_bit(values, bit, index):
    return place_bit(values, swap_dp(values, bit), bit, index)


def place_bit(values, received, bit, index):
    both = in_order(values, received, bit_set(index, bit), 2)
    return both.reshape((values.shape[0], 2 * values.shape[1]) + values.shape[2:])


def gather_tensor(values):
    return jnp.concatenate([values, swap_tensor(values)], axis=0)


def gather_far(shard, index, before):
    bits = axis_bits(lax.axis_size("dp"))
    values = shard[None, None]
    for bit in range(bits - 1, 1, -1):
        values = gather_bit(values, bit, index)
        if bit == bits - 1:
            values = hold(values, *before)
    return values


def gather_near(values, index):
    cut = values.shape[-1] // 2
    return gather_bit(values[..., :cut], 1, index), gather_tensor(values[..., cut:])


def gather_rest(first, second, index):
    return gather_tensor(first), gather_bit(second, 1, index)


def gather_core(first, second, before):
    if before:
        first, second = hold(first, *before), hold(second, *before)
    return [(part, swap_dp(part, 0)) for part in (first, second)]


def pick(values, upper, axis):
    return jnp.where(
        upper,
        lax.index_in_dim(values, 1, axis, keepdims=False),
        lax.index_in_dim(values, 0, axis, keepdims=False),
    )


def add_low(left, right):
    return left.astype(jnp.float32) + right.astype(jnp.float32)


def send_bit(values, bit, index):
    shape = values.shape
    values = values.reshape((shape[0], shape[1] // 2, 2) + shape[2:])
    return swap_dp(pick(values, ~bit_set(index, bit), 2), bit)


def keep_bit(values, received, bit, index):
    shape = values.shape
    values = values.reshape((shape[0], shape[1] // 2, 2) + shape[2:])
    return add_low(pick(values, bit_set(index, bit), 2), received)


def reduce_bit(values, bit, index):
    values = values.astype(jnp.bfloat16)
    return keep_bit(values, send_bit(values, bit, index), bit, index)


def joined(pieces):
    return jnp.concatenate([add_low(*pair) for pair in pieces], axis=-1).astype(jnp.bfloat16)


def sum_everywhere(values):
    values = values + swap_tensor(values)
    for bit in range(axis_bits(lax.axis_size("dp"))):
        values = values + swap_dp(values, bit)
    return values


def reverse_distance(table):
    return jnp.roll(table[:, ::-1], 1, axis=1)


def statistics_kernel(up_ref, self_ref, cross_ref, feed_ref, in_ref, wide_ref, bias_ref, out_ref):
    own, cross, feed = self_ref[...], cross_ref[...], feed_ref[...].astype(jnp.float32)
    columns = in_ref.shape[2]
    rows = own.shape[0]
    lane = lanes((rows, 128))
    squares = sum(jnp.sum(x * x, axis=-1, keepdims=True) for x in (own, cross, feed))

    def along(gradient, weight):
        weight = weight.astype(jnp.bfloat16).astype(jnp.float32)
        return jnp.sum(gradient * weight, axis=-1, keepdims=True)

    zero = sum(along(own[:, i * columns : (i + 1) * columns], in_ref[i]) for i in range(3))
    one = along(cross[:, 3 * columns : 4 * columns], in_ref[3])
    two = 0.0
    for tile in range(wide_ref.shape[1] // FF_TILE):
        two += along(
            feed[:, 2 * tile * FF_TILE : (2 * tile + 1) * FF_TILE],
            wide_ref[:, tile * FF_TILE : (tile + 1) * FF_TILE],
        )
    out = jnp.where(lane == 0, zero, 0.0)
    for place, column in ((1, one), (2, two), (3, squares)):
        out = jnp.where(lane == place, column, out)
    out_ref[:rows] = out
    out_ref[rows:] = bias_ref[...]


def statistics(upper, own, cross, feed, attention_in, expand_weight, bias):
    operands = (own, cross, feed, attention_in, expand_weight, bias)
    rows = own.shape[0] + bias.shape[0]
    return call(
        statistics_kernel, "statistics", (1,), [whole(x.shape) for x in operands],
        whole((rows, 128)), shape_of((rows, 128), jnp.float32),
        cost(4 * own.size, 4 * sum(x.size for x in operands)),
    )(upper, *operands)


def adam_update(weight, gradient, moment, square, learn_rate, weight_decay):
    new_moment = BETA_ONE * moment + (1.0 - BETA_ONE) * gradient
    new_square = BETA_TWO * square + (1.0 - BETA_TWO) * gradient * gradient
    direction = (
        new_moment
        / (1.0 - BETA_ONE**STEP)
        / (jnp.sqrt(new_square / (1.0 - BETA_TWO**STEP)) + ADAM_EPS)
    )
    return (new_moment, new_square, weight - learn_rate * (direction + weight_decay * weight))


def update_kernel(up_ref, clip_ref, own_ref, cross_ref, feed_ref, *refs):
    ins, outs = refs[:12], refs[12:]
    clip = clip_ref[0]
    columns = ins[0].shape[2]

    def step(group, at, gradient):
        weight, moment, square = (ins[3 * group + i][at] for i in range(3))
        new = adam_update(weight, gradient * clip, moment, square, MATRIX_RATE, DECAY_RATE)
        for i in range(3):
            outs[3 * group + i][at] = new[i]

    every = slice(None)
    for place in range(3):
        step(0, place, own_ref[:, place * columns : (place + 1) * columns])
    for place, source in ((3, 3), (4, 1), (5, 2)):
        step(0, place, cross_ref[:, source * columns : (source + 1) * columns])
    for place, source in ((0, 4), (1, 0)):
        step(1, (every, place), cross_ref[:, source * columns : (source + 1) * columns])
    for tile in range(ins[6].shape[1] // FF_TILE):
        for group in (2, 3):
            first = (2 * tile + group - 2) * FF_TILE
            step(group, (every, slice(tile * FF_TILE, (tile + 1) * FF_TILE)), feed_ref[:, first : first + FF_TILE].astype(jnp.float32))


def update(upper, clip, own, cross, feed, states):
    operands = (own, cross, feed) + tuple(states)
    out = [shape_of(states[i].shape, jnp.float32) for i in range(12)]
    return call(
        update_kernel, "update", (1,),
        [pl.BlockSpec(memory_space=pltpu.SMEM)] + [whole(x.shape) for x in operands],
        [whole(x.shape) for x in out], out,
        cost(20 * own.size, 8 * sum(x.size for x in operands)),
    )(upper, clip, *operands)


def interleave(left, right):
    rows = left.shape[0]
    parts = [part.reshape(rows, -1, 1, FF_TILE) for part in (left, right)]
    return jnp.concatenate(parts, axis=2).reshape(rows, -1)


def on_device(
    inputs,
    memory,
    dec_segments,
    mem_segments,
    mem_lengths,
    buckets,
    cotangent,
    attention_in,
    attention_out,
    expand_weight,
    contract_weight,
    norm_gains,
    position_bias,
    moment_attention_in,
    square_attention_in,
    moment_attention_out,
    square_attention_out,
    moment_expand,
    square_expand,
    moment_contract,
    square_contract,
    moment_gains,
    square_gains,
    moment_bias,
    square_bias,
):
    low = jnp.bfloat16
    everywhere = ("dp", "tensor")
    tensor_count = lax.axis_size("tensor")
    tensor_index = lax.axis_index("tensor")
    index = lax.axis_index("dp")
    rows = inputs.shape[0] // tensor_count
    length, width = inputs.shape[1], inputs.shape[2]
    keys = memory.shape[1]
    shard_rows = attention_in.shape[0]
    shards = width // shard_rows
    columns = attention_in.shape[2]
    aligned = shard_rows % ROW_TILE == 0
    upper = jnp.stack([bit_set(index, 0).astype(jnp.int32), tensor_index])
    split = (tensor_count, shards // 2, shard_rows)

    def own_rows(values):
        return lax.dynamic_slice_in_dim(values, tensor_index * rows, rows, 0)

    def flat(values):
        return values.reshape(values.shape[0] * values.shape[1], values.shape[2])

    def in_rows(values, size):
        return values.reshape(rows, size, values.shape[-1])

    wa = attention_in.astype(low)
    wo = attention_out.astype(low)
    shard = jnp.concatenate([wa[:, i] for i in (0, 1, 2)] + [wo[:, 0]] + [wa[:, i] for i in (4, 5, 3)] + [wo[:, 1]], axis=1)
    other_bias = swap_tensor(position_bias)
    far = gather_far(shard, index, [other_bias])
    halves = gather_near(far, index)
    first, second = halves
    pair_own = (first, swap_dp(first, 0))
    pair_own = in_blocks([pair_own], upper)[0]
    first = swap_tensor(first)
    second_got = swap_dp(second, 1)
    feed_shard = interleave(expand_weight.astype(low), contract_weight.astype(low))
    feed_shard = hold(feed_shard, far)
    feed_weights = lax.all_gather(feed_shard, everywhere, axis=0, tiled=True).reshape(
        shards, tensor_count, shard_rows, feed_shard.shape[1]
    )
    if not aligned:
        feed_weights = jnp.transpose(feed_weights, (1, 0, 2, 3)).reshape(
            1, tensor_count, width, feed_shard.shape[1]
        )

    decoder_ids = own_rows(dec_segments)
    key_index = jnp.arange(keys, dtype=jnp.int32)
    memory_ids = jnp.where(
        key_index[None, :] < own_rows(mem_lengths)[:, None], own_rows(mem_segments), -1
    )
    dec = decoder_ids[:, :, None]
    dec_across = jnp.pad(decoder_ids, ((0, 0), (0, TABLE - length)), constant_values=-1)[:, None]
    mem_across = memory_ids[:, None]
    own_heads = position_bias.shape[1]
    heads = own_heads * tensor_count
    both_bias = jnp.concatenate([position_bias, other_bias], axis=1)
    lookup = (
        buckets[None, :] == jnp.arange(position_bias.shape[0], dtype=jnp.int32)[:, None]
    ).astype(jnp.float32)
    lookup = jnp.pad(lookup, ((0, 0), (0, TABLE - length)))
    table = jnp.einsum(
        "gd,gm->md", lookup, both_bias, precision=lax.Precision.HIGHEST,
        preferred_element_type=jnp.float32,
    )
    table = reverse_distance(table).reshape(heads // 2, 2, TABLE)
    gains = norm_gains.T

    all_inputs, all_memory, all_cotangent = flat(inputs), flat(memory), flat(cotangent)
    normed_zero, qkv_own = project(upper, all_inputs, gains, [pair_own, pair_own], 0)
    qkv_own = in_rows(qkv_own, length)
    mixed_own, logs_own = self_forward(qkv_own, dec, dec_across, table, 0)
    first, second_got = hold(first, mixed_own), hold(second_got, mixed_own)
    second = place_bit(second, second_got, 1, index)
    pair_other, piece_cross = in_blocks(gather_core(first, second, []), upper)
    piece_self, piece_cross = [pair_own, pair_other], [piece_cross, piece_cross]
    qkv_other = in_rows(project(upper, all_inputs, gains, piece_self, 1)[1], length)
    mixed_other, logs_other = self_forward(qkv_other, dec, dec_across, table, 1)
    self_mixed = [flat(mixed_own), flat(mixed_other)]
    hidden_one, normed_one, cross_query = after_self(
        upper, all_inputs, self_mixed, gains, piece_self + piece_cross
    )
    cross_kv = in_rows(memory_project(upper, all_memory, piece_cross), keys)
    cross_query = in_rows(cross_query, length)
    cross_mixed, cross_logs = cross_forward(cross_query, cross_kv, dec, mem_across)
    split_or_whole = split if aligned else (tensor_count, 1, width // 2)
    output, feed_slopes, slope_two, slope_cm, keep_co, send_co = feed_forward(
        upper, hidden_one, flat(cross_mixed), all_cotangent, gains, piece_cross, feed_weights, split_or_whole
    )
    output = in_rows(output, length)

    def halves_of(kept, sent):
        if aligned:
            return kept, sent
        low_half = jnp.where(upper[0] == 1, sent, kept)
        high_half = jnp.where(upper[0] == 1, kept, sent)
        both = jnp.concatenate([low_half, high_half], axis=2)
        both = both.reshape((both.shape[0], shards // 2, 2, shard_rows, both.shape[-1]))
        return pick(both, upper[0] == 1, 2), pick(both, upper[0] == 0, 2)

    if not aligned:
        feed_slopes = jnp.transpose(
            feed_slopes.reshape(tensor_count, shards, shard_rows, feed_slopes.shape[-1]), (1, 0, 2, 3)
        )
    share_feed = lax.psum_scatter(
        feed_slopes.reshape(-1, feed_slopes.shape[-1]), everywhere, scatter_dimension=0, tiled=True
    )

    slope_cq, slope_ck, slope_cv = cross_backward(
        cross_query, cross_kv, dec, mem_across, cross_mixed, cross_logs, in_rows(slope_cm, length)
    )
    keep_co, send_co = halves_of(keep_co, send_co)
    got_co = swap_dp(send_co, 0)
    keep_kv, send_kv = halves_of(*outer(
        upper, all_memory, [flat(slope_ck), flat(slope_cv)], split_or_whole, "memory_outer", [got_co]
    ))
    got_kv = swap_dp(send_kv, 0)
    slope_one, slope_sm, keep_qo, send_qo = after_cross(
        upper, flat(slope_cq), normed_one, hidden_one, slope_two, self_mixed, gains,
        piece_self + piece_cross, split_or_whole, [keep_kv],
    )
    keep_qo, send_qo = halves_of(keep_qo, send_qo)
    got_qo = swap_dp(send_qo, 0)
    cross_sum = joined([(keep_co, got_co), (keep_kv, got_kv), (keep_qo, got_qo)])
    first, second = cross_sum[..., :1024], cross_sum[..., 1024:]
    first_got, second_got = swap_tensor(first[1:2]), send_bit(second, 1, index)
    slope_sm = in_rows(slope_sm, length)

    def self_half(half, qkv, mixed, logs, after):
        *slopes, diagonals = self_backward(
            qkv, dec, dec_across, table, mixed, logs, slope_sm, half, after
        )
        return [flat(slope) for slope in slopes], diagonals

    one_half = (1,) + split_or_whole[1:]
    slopes_other, diagonals_other = self_half(1, qkv_other, mixed_other, logs_other, [got_qo])
    first = hold(add_low(first[0:1], first_got).astype(low), slopes_other[0])
    second = hold(keep_bit(second, second_got, 1, index).astype(low), slopes_other[0])
    first_got, second_got = send_bit(first, 1, index), swap_tensor(second[1:2])
    keep_other, send_other = halves_of(
        *outer(upper, normed_zero, slopes_other, one_half, "self_outer")
    )
    got_other = swap_dp(send_other, 0)
    other_sum = add_low(keep_other, got_other).astype(low)
    cross_sum = jnp.concatenate(
        [keep_bit(first, first_got, 1, index), add_low(second[0:1], second_got)], axis=-1
    ).astype(low)
    cross_sum = hold(cross_sum, keep_other)
    cross_got = send_bit(cross_sum, 2, index)
    other_got = swap_tensor(other_sum)
    slopes_own, diagonals_own = self_half(0, qkv_own, mixed_own, logs_own, [other_sum])
    cross_sum = hold(keep_bit(cross_sum, cross_got, 2, index), slopes_own[0])
    bits = axis_bits(lax.axis_size("dp"))
    for bit in range(3, bits):
        cross_sum = reduce_bit(cross_sum, bit, index)
    keep_own, send_own = halves_of(
        *outer(upper, normed_zero, slopes_own, one_half, "self_outer")
    )
    got_own = swap_dp(send_own, 0)
    memory_slopes = [hold(flat(slope_ck), keep_own), flat(slope_cv)]
    memory_grad = memory_back(upper, *memory_slopes, piece_cross, 0, [])
    other_got = hold(other_got, memory_grad)
    self_sum = (add_low(keep_own, got_own) + other_got.astype(jnp.float32)).astype(low)
    self_got = send_bit(self_sum, 1, index)
    slopes_self = [part for pair in zip(slopes_own, slopes_other) for part in pair]
    diagonals = jnp.concatenate([diagonals_own, diagonals_other], axis=0)
    (input_slope,) = input_back(
        upper, slopes_self, all_inputs, slope_one, gains, piece_self, [got_own]
    )
    input_got = swap_tensor(input_slope)
    self_sum = hold(keep_bit(self_sum, self_got, 1, index), input_slope)
    for bit in range(2, bits):
        if bit == 2:
            self_got = send_bit(self_sum.astype(low), bit, index)
            memory_slopes[0] = hold(memory_slopes[0], input_slope)
            memory_grad = memory_back(upper, *memory_slopes, piece_cross, 1, [memory_grad])
            self_sum = keep_bit(self_sum.astype(low), hold(self_got, memory_grad), bit, index)
        else:
            self_got = send_bit(self_sum.astype(low), bit, index)
            if bit == bits - 1 and False:
                self_got = hold(self_got, input_got)
            self_sum = keep_bit(self_sum.astype(low), self_got, bit, index)
    memory_grad = in_rows(memory_grad, keys)
    share_cross, share_self = cross_sum[0, 0], self_sum[0, 0]
    input_grad = (
        in_order(in_rows(input_slope, length), in_rows(input_got, length), tensor_index == 1, 0)
        .reshape(inputs.shape)
        .astype(jnp.float32)
    )

    bias_local = jnp.einsum(
        "gd,md->gm", lookup, reverse_distance(diagonals.reshape(heads, TABLE)),
        precision=lax.Precision.HIGHEST, preferred_element_type=jnp.float32,
    )
    bias_local = jnp.where(
        tensor_index == 1, jnp.roll(bias_local, own_heads, axis=1), bias_local
    )
    bias_rows = bias_local.size // 128
    bias_tile = jnp.pad(bias_local.reshape(bias_rows, 128), ((0, 8 - bias_rows), (0, 0)))
    table_rows = statistics(
        upper, share_self, share_cross, share_feed, jnp.swapaxes(attention_in, 0, 1), expand_weight, bias_tile
    )
    table_rows = table_rows + hold(swap_tensor(table_rows), input_got)
    totals = table_rows[shard_rows:]
    table_rows = table_rows[:shard_rows]
    old_gains = lax.dynamic_slice_in_dim(norm_gains, index * shard_rows, shard_rows, 0)
    shared_gains = table_rows[:, :3] / old_gains
    square_sum = jnp.sum(table_rows[:, 3]) + jnp.sum(shared_gains * shared_gains)
    totals = totals + jnp.where(
        lax.broadcasted_iota(jnp.int32, totals.shape, 0) == bias_rows, square_sum, 0.0
    )
    for bit in range(bits):
        totals = totals + swap_dp(totals, bit)
    bias_sums = totals[:bias_rows].reshape(bias_local.shape)
    grad_norm = jnp.sqrt(totals[bias_rows, 0] + jnp.sum(bias_sums * bias_sums))
    clip_factor = jnp.minimum(1.0, CLIP_NORM / (grad_norm + 1e-06))

    bias_share = lax.dynamic_slice_in_dim(bias_sums, tensor_index * own_heads, own_heads, 1)
    new = update(
        upper, clip_factor[None], share_self, share_cross, share_feed,
        tuple(
            jnp.swapaxes(state, 0, 1)
            for state in (attention_in, moment_attention_in, square_attention_in)
        )
        + (
            attention_out, moment_attention_out, square_attention_out,
            expand_weight, moment_expand, square_expand,
            contract_weight, moment_contract, square_contract,
        ),
    )
    new = [jnp.swapaxes(state, 0, 1) for state in new[:3]] + list(new[3:])
    new_gains = adam_update(
        old_gains, shared_gains * clip_factor, moment_gains, square_gains, SMALL_RATE, 0.0
    )
    new_bias = adam_update(
        position_bias, bias_share * clip_factor, moment_bias, square_bias, SMALL_RATE, 0.0
    )
    return (
        (output, input_grad, memory_grad, grad_norm)
        + tuple(new) + new_gains + new_bias
    )


def solution(mesh):
    return jax.shard_map(
        on_device,
        mesh=mesh,
        in_specs=(
            P("dp", None, None),
            P("dp", None, None),
            P("dp", None),
            P("dp", None),
            P("dp"),
            P(),
            P("dp", None, None),
            P("dp", None, "tensor"),
            P("dp", None, "tensor"),
            P("dp", "tensor"),
            P("dp", "tensor"),
            P(),
            P(None, "tensor"),
            P("dp", None, "tensor"),
            P("dp", None, "tensor"),
            P("dp", None, "tensor"),
            P("dp", None, "tensor"),
            P("dp", "tensor"),
            P("dp", "tensor"),
            P("dp", "tensor"),
            P("dp", "tensor"),
            P("dp", None),
            P("dp", None),
            P(None, "tensor"),
            P(None, "tensor"),
        ),
        out_specs=(
            P(("dp", "tensor"), None, None),
            P("dp", None, None),
            P(("dp", "tensor"), None, None),
            P(),
            P("dp", None, "tensor"),
            P("dp", None, "tensor"),
            P("dp", None, "tensor"),
            P("dp", None, "tensor"),
            P("dp", None, "tensor"),
            P("dp", None, "tensor"),
            P("dp", "tensor"),
            P("dp", "tensor"),
            P("dp", "tensor"),
            P("dp", "tensor"),
            P("dp", "tensor"),
            P("dp", "tensor"),
            P("dp", None),
            P("dp", None),
            P("dp", None),
            P(None, "tensor"),
            P(None, "tensor"),
            P(None, "tensor"),
        ),
        check_vma=False,
    )
```

```python
import functools

import jax
import jax.numpy as jnp
from jax import lax
from jax.experimental import pallas as pl
from jax.experimental.pallas import tpu as pltpu
from jax.sharding import PartitionSpec as P

STEP = 10
NORM_EPS = 1e-06
CLIP_NORM = 1.0
BETA_ONE = 0.9
BETA_TWO = 0.95
ADAM_EPS = 1e-08
MATRIX_RATE = 0.08
SMALL_RATE = 0.8
DECAY_RATE = 0.1
GELU_SCALE = 0.7978845608028654
GELU_CUBIC = 0.044715
MASKED = -1e30
TABLE = 384
NT = (((1,), (1,)), ((), ()))
TN = (((0,), (0,)), ((), ()))


def dot(a, b, dims=(((1,), (0,)), ((), ()))):
    return lax.dot_general(a, b, dims, preferred_element_type=jnp.float32)


def lanes(shape):
    return lax.broadcasted_iota(jnp.int32, shape, len(shape) - 1)


def half_of(values, which):
    return jnp.where((lanes(values.shape) >= 64) == (which == 1), values, jnp.zeros_like(values))


def column(values, index):
    return jnp.sum(jnp.where(lanes(values.shape) == index, values, 0.0), axis=-1, keepdims=True)


def cross_forward_kernel(q_ref, k_ref, v_ref, dec_ref, mem_ref, o_ref, lse_ref):
    pair = pl.program_id(1)
    query, key, value = q_ref[0], k_ref[0], v_ref[0]
    allowed = dec_ref[0] == mem_ref[0]
    mixed, logs = forward_pair(query, key, value, [None, None], allowed)
    o_ref[0] = mixed.astype(o_ref.dtype)
    store_logs(lse_ref, logs, pair)


def store_logs(lse_ref, logs, pair):
    @pl.when(pair == 0)
    def _():
        lse_ref[0] = jnp.zeros(lse_ref.shape[1:], jnp.float32)

    lane = lanes(lse_ref.shape[1:])
    kept = lse_ref[0]
    for which in range(2):
        kept = jnp.where(lane == 2 * pair + which, logs[which], kept)
    lse_ref[0] = kept


def forward_pair(query, key, value, biases, allowed):
    mixed = jnp.zeros(query.shape, jnp.float32)
    logs = []
    for which in range(2):
        scores = dot(half_of(query, which), key, NT)
        if biases[which] is not None:
            scores = scores + biases[which]
        scores = jnp.where(allowed, scores, MASKED)
        top = jnp.max(scores, axis=-1, keepdims=True)
        weights = jnp.exp(scores - top)
        total = jnp.sum(weights, axis=-1, keepdims=True)
        logs.append(top + jnp.log(total))
        mixed = mixed + dot(weights.astype(jnp.bfloat16), half_of(value, which)) * (1.0 / total)
    return mixed, logs


def backward_pair(query, key, value, mixed, upstream, logs, biases, allowed):
    slope_q = jnp.zeros(query.shape, jnp.float32)
    slope_k = jnp.zeros(key.shape, jnp.float32)
    slope_v = jnp.zeros(key.shape, jnp.float32)
    grads = []
    product = upstream.astype(jnp.float32) * mixed.astype(jnp.float32)
    for which in range(2):
        query_half = half_of(query, which)
        up_half = half_of(upstream, which)
        scores = dot(query_half, key, NT)
        if biases[which] is not None:
            scores = scores + biases[which]
        prob = jnp.exp(jnp.where(allowed, scores - logs[which], MASKED))
        slope_p = dot(up_half, value, NT)
        inner = jnp.sum(half_of(product, which), axis=-1, keepdims=True)
        grad = (prob * (slope_p - inner)).astype(jnp.bfloat16)
        slope_q = slope_q + dot(grad, half_of(key, which))
        slope_k = slope_k + dot(grad, query_half, TN)
        slope_v = slope_v + dot(prob.astype(jnp.bfloat16), up_half, TN)
        grads.append(grad)
    return slope_q, slope_k, slope_v, grads


def cross_backward_kernel(
    q_ref, k_ref, v_ref, dec_ref, mem_ref, o_ref, lse_ref, up_ref, dq_ref, dk_ref, dv_ref
):
    pair = pl.program_id(1)
    allowed = dec_ref[0] == mem_ref[0]
    logs = [column(lse_ref[0], 2 * pair + which) for which in range(2)]
    slope_q, slope_k, slope_v, _ = backward_pair(
        q_ref[0], k_ref[0], v_ref[0], o_ref[0], up_ref[0], logs, [None, None], allowed
    )
    dq_ref[0] = slope_q.astype(jnp.bfloat16)
    dk_ref[0] = slope_k.astype(jnp.bfloat16)
    dv_ref[0] = slope_v.astype(jnp.bfloat16)


def pad_keys(values):
    extra = TABLE - values.shape[0]
    return jnp.concatenate([values, jnp.zeros((extra, values.shape[1]), values.dtype)], axis=0)


def self_allowed(dec_ref, decT_ref):
    length = dec_ref.shape[1]
    rows = lax.broadcasted_iota(jnp.int32, (length, TABLE), 0)
    return (dec_ref[0] == decT_ref[0]) & (lanes((length, TABLE)) <= rows)


def toeplitz(table_ref, which, length):
    spread = jnp.broadcast_to(table_ref[0, which : which + 1, :], (length, TABLE))
    return pltpu.roll(spread, 0, 1, stride=1, stride_axis=0)


def self_forward_kernel(q_ref, k_ref, v_ref, dec_ref, decT_ref, table_ref, o_ref, lse_ref):
    pair = pl.program_id(1)
    length = q_ref.shape[1]
    biases = [toeplitz(table_ref, which, length) for which in range(2)]
    mixed, logs = forward_pair(
        q_ref[0], pad_keys(k_ref[0]), pad_keys(v_ref[0]), biases, self_allowed(dec_ref, decT_ref)
    )
    o_ref[0] = mixed.astype(o_ref.dtype)
    store_logs(lse_ref, logs, pair)


def self_backward_kernel(ties, *refs):
    q_ref, k_ref, v_ref, dec_ref, decT_ref, table_ref, o_ref, lse_ref, up_ref = refs[:9]
    dq_ref, dk_ref, dv_ref, diag_ref = refs[9 + ties :]
    pair, row = pl.program_id(0), pl.program_id(1)
    length = q_ref.shape[1]
    biases = [toeplitz(table_ref, which, length) for which in range(2)]
    logs = [column(lse_ref[0], 2 * pair + which) for which in range(2)]
    slope_q, slope_k, slope_v, grads = backward_pair(
        q_ref[0], pad_keys(k_ref[0]), pad_keys(v_ref[0]), o_ref[0], up_ref[0], logs, biases,
        self_allowed(dec_ref, decT_ref),
    )
    dq_ref[0] = slope_q.astype(jnp.bfloat16)
    dk_ref[0] = slope_k[:length].astype(jnp.bfloat16)
    dv_ref[0] = slope_v[:length].astype(jnp.bfloat16)

    @pl.when(row == 0)
    def _():
        diag_ref[...] = jnp.zeros(diag_ref.shape, jnp.float32)

    for which in range(2):
        diag_ref[0, which : which + 1, :] += diagonal_sums(grads[which].astype(jnp.float32))


def diagonal_sums(values):
    groups = jnp.zeros((8, TABLE), jnp.float32)
    for start in range(0, values.shape[0], 8):
        groups = groups + pltpu.roll(values[start : start + 8], (TABLE - start) % TABLE, 1)
    total = groups[0:1]
    for row in range(1, 8):
        total = total + pltpu.roll(groups, TABLE - row, 1)[row : row + 1]
    return total


def params(count):
    return pltpu.CompilerParams(
        dimension_semantics=("arbitrary",) * count, vmem_limit_bytes=48 * 1024 * 1024
    )


def cross_forward(q, kv, dec, mem):
    rows, length, width = q.shape
    keys = kv.shape[1]
    pairs = width // 128
    lanes_q = pl.BlockSpec((1, length, 128), lambda r, p: (r, 0, p))
    lanes_k = pl.BlockSpec((1, keys, 128), lambda r, p: (r, 0, p))
    lanes_v = pl.BlockSpec((1, keys, 128), lambda r, p: (r, 0, p + pairs))
    return pl.pallas_call(
        cross_forward_kernel,
        grid=(rows, width // 128),
        in_specs=[
            lanes_q, lanes_k, lanes_v,
            pl.BlockSpec((1, length, 1), lambda r, p: (r, 0, 0)),
            pl.BlockSpec((1, 1, keys), lambda r, p: (r, 0, 0)),
        ],
        out_specs=[lanes_q, pl.BlockSpec((1, length, 128), lambda r, p: (r, 0, 0))],
        out_shape=[
            jax.ShapeDtypeStruct((rows, length, width), jnp.bfloat16),
            jax.ShapeDtypeStruct((rows, length, 128), jnp.float32),
        ],
        compiler_params=params(2),
        cost_estimate=cost(4 * rows * length * keys * width, 2 * rows * width * (2 * length + 2 * keys), 2 * rows * length * keys * pairs),
        name="cross_forward",
    )(q, kv, kv, dec, mem)


def cross_backward(q, kv, dec, mem, mixed, logs, upstream):
    rows, length, width = q.shape
    keys = kv.shape[1]
    pairs = width // 128
    lanes_q = pl.BlockSpec((1, length, 128), lambda r, p: (r, 0, p))
    lanes_k = pl.BlockSpec((1, keys, 128), lambda r, p: (r, 0, p))
    lanes_v = pl.BlockSpec((1, keys, 128), lambda r, p: (r, 0, p + pairs))
    return pl.pallas_call(
        cross_backward_kernel,
        grid=(rows, width // 128),
        in_specs=[
            lanes_q, lanes_k, lanes_v,
            pl.BlockSpec((1, length, 1), lambda r, p: (r, 0, 0)),
            pl.BlockSpec((1, 1, keys), lambda r, p: (r, 0, 0)),
            lanes_q, pl.BlockSpec((1, length, 128), lambda r, p: (r, 0, 0)), lanes_q,
        ],
        out_specs=[lanes_q, lanes_k, lanes_k],
        out_shape=[
            jax.ShapeDtypeStruct((rows, length, width), jnp.bfloat16),
            jax.ShapeDtypeStruct((rows, keys, width), jnp.bfloat16),
            jax.ShapeDtypeStruct((rows, keys, width), jnp.bfloat16),
        ],
        compiler_params=params(2),
        cost_estimate=cost(10 * rows * length * keys * width, 2 * rows * width * (4 * length + 4 * keys), 2 * rows * length * keys * pairs),
        name="cross_backward",
    )(q, kv, kv, dec, mem, mixed, logs, upstream)


def self_forward(qkv, dec, decT, table, half):
    rows, length, width = qkv.shape
    count = width // 384
    first = half * count
    spec = pl.BlockSpec((1, length, 128), lambda r, p: (r, 0, p))
    spec_k = pl.BlockSpec((1, length, 128), lambda r, p: (r, 0, p + count))
    spec_v = pl.BlockSpec((1, length, 128), lambda r, p: (r, 0, p + 2 * count))
    return pl.pallas_call(
        self_forward_kernel,
        grid=(rows, count),
        in_specs=[
            spec, spec_k, spec_v,
            pl.BlockSpec((1, length, 1), lambda r, p: (r, 0, 0)),
            pl.BlockSpec((1, 1, TABLE), lambda r, p: (r, 0, 0)),
            pl.BlockSpec((1, 2, TABLE), lambda r, p: (p + first, 0, 0)),
        ],
        out_specs=[
            pl.BlockSpec((1, length, 128), lambda r, p: (r, 0, p)),
            pl.BlockSpec((1, length, 128), lambda r, p: (r, 0, 0)),
        ],
        out_shape=[
            jax.ShapeDtypeStruct((rows, length, width // 3), jnp.bfloat16),
            jax.ShapeDtypeStruct((rows, length, 128), jnp.float32),
        ],
        compiler_params=params(2),
        cost_estimate=cost(2 * rows * length * TABLE * width // 3, 8 * rows * width * length // 3, 2 * rows * length * TABLE * count),
        name="self_forward",
    )(qkv, qkv, qkv, dec, decT, table)


def self_backward(qkv, dec, decT, table, mixed, logs, upstream, half, after):
    rows, length, width = qkv.shape
    count = width // 384
    first = half * count
    spec = pl.BlockSpec((1, length, 128), lambda p, r: (r, 0, p))
    spec_k = pl.BlockSpec((1, length, 128), lambda p, r: (r, 0, p + count))
    spec_v = pl.BlockSpec((1, length, 128), lambda p, r: (r, 0, p + 2 * count))
    spec_up = pl.BlockSpec((1, length, 128), lambda p, r: (r, 0, p + first))
    out = jax.ShapeDtypeStruct((rows, length, width // 3), jnp.bfloat16)
    return pl.pallas_call(
        functools.partial(self_backward_kernel, len(after)),
        grid=(count, rows),
        in_specs=[
            spec, spec_k, spec_v,
            pl.BlockSpec((1, length, 1), lambda p, r: (r, 0, 0)),
            pl.BlockSpec((1, 1, TABLE), lambda p, r: (r, 0, 0)),
            pl.BlockSpec((1, 2, TABLE), lambda p, r: (p + first, 0, 0)), spec,
            pl.BlockSpec((1, length, 128), lambda p, r: (r, 0, 0)), spec_up,
        ] + [pl.BlockSpec(memory_space=pl.ANY)] * len(after),
        out_specs=[spec, spec, spec, pl.BlockSpec((1, 2, TABLE), lambda p, r: (p, 0, 0))],
        out_shape=[out, out, out, jax.ShapeDtypeStruct((count, 2, TABLE), jnp.float32)],
        compiler_params=params(2),
        cost_estimate=cost(5 * rows * length * TABLE * width // 3, 16 * rows * width * length // 3, 2 * rows * length * TABLE * count),
        name="self_backward",
    )(qkv, qkv, qkv, dec, decT, table, mixed, logs, upstream, *after)


SLOPE = GELU_SCALE * 3.0 * GELU_CUBIC
ROW_TILE = 16
FF_TILE = 512
MEMORY_TILE = 512


def whole(shape):
    return pl.BlockSpec(shape, lambda *_: (0,) * len(shape))


def cost(flops, moved, exps=0):
    return pl.CostEstimate(flops=int(flops), bytes_accessed=int(moved), transcendentals=int(exps))


def row_scale(hidden):
    return lax.rsqrt(jnp.mean(hidden * hidden, axis=-1, keepdims=True) + NORM_EPS)


def row_back(hidden, gain, upstream):
    factor = row_scale(hidden)
    scaled = upstream * hidden
    inner = jnp.mean(scaled * gain, axis=-1, keepdims=True)
    slope = factor * (upstream * gain) - (factor * factor * factor * inner) * hidden
    return slope


def emit(gradient, keep_ref, send_ref, start, upper):
    halves, blocks, rows, _ = keep_ref.shape
    columns = gradient.shape[1] // halves
    for half in range(halves):
        part = gradient[:, half * columns : (half + 1) * columns]
        part = part.reshape(blocks, 2, rows, columns)
        low, high = part[:, 0], part[:, 1]
        keep = jnp.where(upper, high, low).astype(jnp.bfloat16)
        send = jnp.where(upper, low, high).astype(jnp.bfloat16)
        keep_ref[half, :, :, start : start + columns] = keep
        send_ref[half, :, :, start : start + columns] = send


def call(kernel, name, grid, in_specs, out_specs, out_shape, work, scratch=(), weights=(), after=(), aliases=None):
    count, loaded = len(in_specs), 2 * len(weights)
    outs = len(out_specs) if isinstance(out_specs, list) else 1

    def run(up_ref, *refs):
        ins = refs[:count]
        pieces = refs[count : count + loaded]
        kernel(up_ref, *ins, pieces, *refs[count + loaded + len(after) :])

    anywhere = pl.BlockSpec(memory_space=pl.ANY)
    return lambda upper, *operands: pl.pallas_call(
        run if weights else lambda up_ref, *refs: kernel(up_ref, *refs[:count], *refs[count + len(after) :]),
        grid_spec=pltpu.PrefetchScalarGridSpec(
            num_scalar_prefetch=1,
            grid=grid,
            in_specs=in_specs + [anywhere] * (loaded + len(after)),
            out_specs=out_specs,
            scratch_shapes=scratch,
        ),
        out_shape=out_shape,
        input_output_aliases=aliases or {},
        compiler_params=pltpu.CompilerParams(
            dimension_semantics=("arbitrary",) * len(grid), vmem_limit_bytes=56 * 1024 * 1024
        ),
        cost_estimate=work,
        name=name,
    )(upper, *operands, *[piece for pair in weights for piece in pair], *after)


def fetch(pieces, store, sems, mats, upper):
    copies = []
    columns = store.shape[3] // len(mats)
    for place, (source, begin, half) in enumerate(mats):
        group = []
        for other in range(2):
            piece = pieces[4 * source + 2 * half + other]
            copy = pltpu.make_async_copy(
                piece.at[half % piece.shape[0], :, :, pl.ds(begin, columns)],
                store.at[:, (upper + other) % 2, :, pl.ds(place * columns, columns)],
                sems.at[place * 2 + other],
            )
            group.append(copy)
        copies.append(group)
    return copies


def start(copies):
    for group in copies:
        for copy in group:
            copy.start()


def wait(group):
    for copy in group:
        copy.wait()


def shape_of(shape, kind=jnp.bfloat16):
    return jax.ShapeDtypeStruct(shape, kind)


def kernel_of(store, place, width):
    return store[:, :, :, place * width : (place + 1) * width].reshape(store.shape[0] * 2 * store.shape[2], width)


def room(weights, count):
    _, blocks, rows, columns = weights[0][0].shape
    wide = count * (columns // 4)
    return [pltpu.VMEM((blocks, 2, rows, wide), jnp.bfloat16), pltpu.SemaphoreType.DMA((2 * count,))]


QKV, SO = (0, 1, 2), 3
CKV, CQ, CO = (0, 1), 2, 3


def placed(mats, pieces, source=0, halves=(0, 1)):
    columns = pieces[0].shape[3] // 4
    return [(source, which * columns, half) for which in mats for half in halves]


def project_kernel(half, up_ref, x_ref, gain_ref, pieces, n_ref, out_ref, store, sems):
    copies = fetch(pieces, store, sems, placed(QKV, pieces, 0, (half,)), up_ref[0])

    @pl.when(pl.program_id(0) == 0)
    def _():
        start(copies)
        hidden = x_ref[...].astype(jnp.float32)
        n_ref[...] = (hidden * row_scale(hidden) * gain_ref[0:1]).astype(jnp.bfloat16)

    width = out_ref.shape[1]
    for place in range(3):
        @pl.when(pl.program_id(0) == place)
        def _():
            wait(copies[place])
            out_ref[...] = dot(n_ref[...], kernel_of(store, place, width)).astype(jnp.bfloat16)


def own_spec(tokens, width):
    return pl.BlockSpec((tokens, width), lambda g, up: (up[1], 0))


def project(upper, inputs, gains, pieces, half):
    tokens, width = inputs.shape[0] // 2, inputs.shape[1]
    wide = width // 2
    return call(
        functools.partial(project_kernel, half), "project", (3,),
        [own_spec(tokens, width), whole(gains.shape)],
        [whole((tokens, width)), pl.BlockSpec((tokens, wide), lambda g, *_: (0, g))],
        [shape_of((tokens, width)), shape_of((tokens, 3 * wide))],
        cost(3 * tokens * width * width, 2 * width * (3 * tokens + 2 * width)), scratch=room(pieces, 3), weights=pieces,
    )(upper, inputs, gains)


def memory_project_kernel(up_ref, x_ref, pieces, out_ref, store, sems):
    copies = fetch(pieces, store, sems, placed(CKV, pieces), up_ref[0])

    @pl.when(pl.program_id(0) == 0)
    def _():
        start(copies)
        for group in copies:
            wait(group)

    width = x_ref.shape[1]
    out_ref[...] = dot(x_ref[...], kernel_of(store, 0, 2 * width)).astype(jnp.bfloat16)


def memory_project(upper, memory, pieces):
    tokens, width = memory.shape[0] // 2, memory.shape[1]
    tile = MEMORY_TILE
    steps = tokens // tile
    return call(
        memory_project_kernel, "memory_project", (steps,),
        [pl.BlockSpec((tile, width), lambda g, up: (up[1] * steps + g, 0))],
        pl.BlockSpec((tile, 2 * width), lambda g, *_: (g, 0)),
        shape_of((tokens, 2 * width)),
        cost(4 * tokens * width * width, 2 * width * (3 * tokens + 2 * width)), scratch=room(pieces, 4), weights=pieces,
    )(upper, memory)


def after_self_kernel(up_ref, x_ref, a_ref, b_ref, gain_ref, pieces, h_ref, n_ref, q_ref, store, sems):
    copies = fetch(pieces, store, sems, placed([SO], pieces) + placed([CQ], pieces, 1), up_ref[0])

    @pl.when(pl.program_id(0) == 0)
    def _():
        start(copies)
        for group in copies:
            wait(group)

    width = x_ref.shape[1]
    weight = kernel_of(store, 0, width)
    hidden = x_ref[...].astype(jnp.float32) + dot(a_ref[...], weight[:, : width // 2], NT)
    hidden += dot(b_ref[...], weight[:, width // 2 :], NT)
    h_ref[...] = hidden
    normed = (hidden * row_scale(hidden) * gain_ref[1:2]).astype(jnp.bfloat16)
    n_ref[...] = normed
    q_ref[...] = dot(normed, kernel_of(store, 1, width)).astype(jnp.bfloat16)


def after_self(upper, inputs, mixed, gains, pieces):
    tokens, width = inputs.shape[0] // 2, inputs.shape[1]
    tile = tokens // 2
    rows = pl.BlockSpec((tile, width), lambda g, *_: (g, 0))
    half = pl.BlockSpec((tile, width // 2), lambda g, *_: (g, 0))
    return call(
        after_self_kernel, "after_self", (2,),
        [pl.BlockSpec((tile, width), lambda g, up: (2 * up[1] + g, 0)), half, half, whole(gains.shape)],
        [rows, rows, rows],
        [shape_of((tokens, width), jnp.float32), shape_of((tokens, width)), shape_of((tokens, width))],
        cost(4 * tokens * width * width, width * (12 * tokens + 4 * width)), scratch=room(pieces, 4), weights=pieces,
    )(upper, inputs, *mixed, gains)


def feed_kernel(
    up_ref, h1_ref, a_ref, gy_ref, gain_ref, w_ref, pieces,
    y_ref, g_ref, gh_ref, ga_ref, keep_ref, send_ref,
    n_ref, nT_ref, gyT_ref, acc_ref, store, sems,
):
    step = pl.program_id(0)
    tile = FF_TILE
    width = y_ref.shape[1]
    copies = fetch(pieces, store, sems, placed([CO], pieces), up_ref[0])

    @pl.when(step == 0)
    def _():
        start(copies)
        gyT_ref[...] = gy_ref[...].T
        wait(copies[0])
        wait(copies[1])
        hidden = h1_ref[...] + dot(a_ref[...], kernel_of(store, 0, width), NT)
        gh_ref[...] = hidden
        y_ref[...] = hidden
        normed = (hidden * row_scale(hidden) * gain_ref[2:3]).astype(jnp.bfloat16)
        n_ref[...] = normed
        nT_ref[...] = normed.T
        acc_ref[...] = jnp.zeros(acc_ref.shape, jnp.float32)

    wi = w_ref[:, 0, :, :tile].reshape(width, tile)
    wf = w_ref[:, 0, :, tile:].reshape(width, tile)
    u = dot(n_ref[...], wi)
    square = u * u
    bent = jnp.tanh(u * (GELU_SCALE + (GELU_SCALE * GELU_CUBIC) * square))
    half = 0.5 + 0.5 * bent
    act = (u * half).astype(jnp.bfloat16)
    slope = half + (0.5 * u) * (1.0 - bent * bent) * (GELU_SCALE + SLOPE * square)
    gu = (dot(gy_ref[...], wf) * slope).astype(jnp.bfloat16)
    y_ref[...] += dot(act, wf, NT)
    acc_ref[...] += dot(gu, wi, NT)
    g_ref[:, 0, :, :tile] = dot(nT_ref[...], gu).reshape(g_ref.shape[0], g_ref.shape[2], tile).astype(jnp.bfloat16)
    g_ref[:, 0, :, tile:] = dot(gyT_ref[...], act).reshape(g_ref.shape[0], g_ref.shape[2], tile).astype(jnp.bfloat16)

    @pl.when(step == pl.num_programs(0) - 1)
    def _():
        back = row_back(gh_ref[...], gain_ref[2:3], acc_ref[...])
        total = gy_ref[...].astype(jnp.float32) + back
        gh_ref[...] = total
        low = total.astype(jnp.bfloat16)
        ga_ref[...] = dot(low, kernel_of(store, 0, width)).astype(jnp.bfloat16)
        emit(dot(low.T, a_ref[...]), keep_ref, send_ref, 0, up_ref[0] == 1)


def feed_forward(upper, hidden, mixed, cotangent, gains, pieces, weights, split):
    tokens, width = hidden.shape
    blocks, halves, rows, wide = weights.shape
    steps = wide // (2 * FF_TILE)
    spec = pl.BlockSpec((blocks, 1, rows, 2 * FF_TILE), lambda g, *_: (0, g // steps, 0, g % steps))
    full = whole((tokens, width))
    f32 = shape_of((tokens, width), jnp.float32)
    columns = width // halves
    return call(
        feed_kernel, "feed_forward", (halves * steps,),
        [full, full, own_spec(tokens, width), whole(gains.shape), spec],
        [full, spec, full, full, whole(split + (columns,)), whole(split + (columns,))],
        [f32, shape_of(weights.shape), f32, shape_of((tokens, width)),
         shape_of(split + (columns,)), shape_of(split + (columns,))],
        cost(6 * tokens * width * halves * wide, 40 * tokens * width, tokens * halves * wide / 2),
        scratch=[
            pltpu.VMEM((tokens, width), jnp.bfloat16), pltpu.VMEM((width, tokens), jnp.bfloat16),
            pltpu.VMEM((width, tokens), jnp.bfloat16), pltpu.VMEM((tokens, width), jnp.float32),
        ] + room(pieces, 2), weights=pieces,
    )(upper, hidden, mixed, cotangent, gains, weights)


def after_cross_kernel(
    up_ref, gq_ref, n_ref, h_ref, gh_ref, a_ref, b_ref, gain_ref, pieces,
    gh1_ref, ga_ref, keep_ref, send_ref, store, sems,
):
    copies = fetch(pieces, store, sems, placed([SO], pieces) + placed([CQ], pieces, 1), up_ref[0])
    start(copies)
    upper = up_ref[0] == 1
    columns = keep_ref.shape[3] // 2
    width = h_ref.shape[1]
    emit(dot(n_ref[...].T, gq_ref[...]), keep_ref, send_ref, 0, upper)
    wait(copies[2])
    wait(copies[3])
    back = row_back(h_ref[...], gain_ref[1:2], dot(gq_ref[...], kernel_of(store, 1, width), NT))
    total = gh_ref[...] + back
    gh1_ref[...] = total
    low = total.astype(jnp.bfloat16)
    wait(copies[0])
    wait(copies[1])
    ga_ref[...] = dot(low, kernel_of(store, 0, width)).astype(jnp.bfloat16)
    across = low.T
    emit(dot(across, a_ref[...]), keep_ref.at[0:1], send_ref.at[0:1], columns, upper)
    emit(dot(across, b_ref[...]), keep_ref.at[1:2], send_ref.at[1:2], columns, upper)


def after_cross(upper, slope_q, normed, hidden, slope_hidden, mixed, gains, pieces, split, after):
    tokens, width = hidden.shape
    full = whole((tokens, width))
    piece = split + (2 * (width // split[0]),)
    return call(
        after_cross_kernel, "after_cross", (1,),
        [full, full, full, full, whole((tokens, width // 2)), whole((tokens, width // 2)), whole(gains.shape)],
        [full, full, whole(piece), whole(piece)],
        [shape_of((tokens, width), jnp.float32), shape_of((tokens, width)),
         shape_of(piece), shape_of(piece)],
        cost(8 * tokens * width * width, tokens * width * 24 + 8 * width * width),
        scratch=room(pieces, 4), weights=pieces, after=after,
    )(upper, slope_q, normed, hidden, slope_hidden, *mixed, gains)


def outer_kernel(up_ref, x_ref, *refs):
    slopes, keep_ref, send_ref = refs[:-2], refs[-2], refs[-1]
    upper = up_ref[0] == 1
    columns = keep_ref.shape[3] // len(slopes)
    across = x_ref[...].T
    for place, slope in enumerate(slopes):
        emit(dot(across, slope[...]), keep_ref, send_ref, place * columns, upper)


def outer(upper, rows, slopes, split, name, after=()):
    tokens, width = slopes[0].shape[0], rows.shape[1]
    wide = slopes[0].shape[1]
    piece = split + (len(slopes) * (wide // split[0]),)
    return call(
        outer_kernel, name, (1,),
        [whole(rows.shape) if rows.shape[0] == tokens else own_spec(tokens, width)]
        + [whole(slope.shape) for slope in slopes],
        [whole(piece), whole(piece)],
        [shape_of(piece), shape_of(piece)],
        cost(2 * tokens * width * wide * len(slopes), 2 * (tokens + width) * (width + wide * len(slopes))),
        after=after,
    )(upper, rows, *slopes)


def memory_back_kernel(up_ref, gk_ref, gv_ref, pieces, out_ref, store, sems):
    copies = fetch(pieces, store, sems, placed(CKV, pieces), up_ref[0])

    @pl.when(pl.program_id(0) == 0)
    def _():
        start(copies)
        for group in copies:
            wait(group)

    width = gk_ref.shape[1]
    out_ref[...] = dot(gk_ref[...], kernel_of(store, 0, width), NT) + dot(gv_ref[...], kernel_of(store, 1, width), NT)


def memory_back(upper, slope_k, slope_v, pieces, part, earlier):
    tokens, width = slope_k.shape
    tile = MEMORY_TILE
    first = part * (tokens // 2 // tile)
    rows = pl.BlockSpec((tile, width), lambda g, *_: (g + first, 0))
    in_specs = [rows, rows] + [pl.BlockSpec(memory_space=pl.ANY)] * len(earlier)
    return call(
        lambda up_ref, gk_ref, gv_ref, *refs: memory_back_kernel(up_ref, gk_ref, gv_ref, *refs[len(earlier) :]),
        "memory_back", (tokens // 2 // tile,),
        in_specs, rows, shape_of((tokens, width), jnp.float32),
        cost(2 * tokens * width * width, width * (4 * tokens + 4 * width)),
        scratch=room(pieces, 4), weights=pieces, aliases={3: 0} if earlier else {},
    )(upper, slope_k, slope_v, *earlier)


def input_back_kernel(up_ref, *refs):
    slopes, (x_ref, gh_ref, gain_ref, pieces, out_ref, store, sems) = refs[:6], refs[6:]
    copies = fetch(pieces, store, sems, placed(QKV, pieces), up_ref[0])
    start(copies)
    width = x_ref.shape[1]
    half = width // 2
    upstream = 0.0
    for place in range(6):
        wait(copies[place])
        upstream += dot(slopes[place][...], kernel_of(store, place, half), NT)
    back = row_back(x_ref[...].astype(jnp.float32), gain_ref[0:1], upstream)
    out_ref[...] = (gh_ref[...] + back).astype(jnp.bfloat16)


def input_back(upper, slopes, inputs, slope_hidden, gains, pieces, after):
    tokens, width = inputs.shape[0] // 2, inputs.shape[1]
    full = whole((tokens, width))
    return call(
        input_back_kernel, "input_back", (1,),
        [whole((tokens, width // 2))] * 6 + [own_spec(tokens, width), full, whole(gains.shape)],
        [full],
        [shape_of((tokens, width))],
        cost(6 * tokens * width * width, width * (14 * tokens + 6 * width)),
        scratch=room(pieces, 6), weights=pieces, after=after,
    )(upper, *slopes, inputs, slope_hidden, gains)


def in_blocks(pairs, upper):
    if pairs[0][0].shape[2] % ROW_TILE == 0:
        return pairs
    result = []
    for own, other in pairs:
        both = in_order(own, other, upper[0] == 1, 2)
        halves, blocks, _, rows, columns = both.shape
        both = both.reshape(halves, 2, 1, blocks * rows, columns)
        result.append((pick(both, upper[0] == 1, 1), pick(both, upper[0] == 0, 1)))
    return result


def axis_bits(size):
    return size.bit_length() - 1


def swap_mask(values, mask):
    count = lax.axis_size("dp")
    return lax.ppermute(values, "dp", [(i, i ^ mask) for i in range(count)])


def swap_dp(values, bit):
    return swap_mask(values, 1 << bit)


def swap_tensor(values):
    return lax.ppermute(values, "tensor", [(0, 1), (1, 0)])


def bit_set(index, bit):
    return lax.rem(lax.shift_right_logical(index, bit), 2) == 1


def hold(values, *before):
    return lax.optimization_barrier((values,) + before)[0]


def in_order(own, other, upper, axis):
    return jnp.where(
        upper, jnp.stack([other, own], axis=axis), jnp.stack([own, other], axis=axis)
    )


def gather_bit(values, bit, index):
    return place_bit(values, swap_dp(values, bit), bit, index)


def place_bit(values, received, bit, index):
    both = in_order(values, received, bit_set(index, bit), 2)
    return both.reshape((values.shape[0], 2 * values.shape[1]) + values.shape[2:])


def gather_tensor(values):
    return jnp.concatenate([values, swap_tensor(values)], axis=0)


def gather_far(shard, index, before):
    bits = axis_bits(lax.axis_size("dp"))
    values = shard[None, None]
    for bit in range(bits - 1, 1, -1):
        values = gather_bit(values, bit, index)
        if bit == bits - 1:
            values = hold(values, *before)
    return values


def gather_near(values, index):
    cut = values.shape[-1] // 2
    return gather_bit(values[..., :cut], 1, index), gather_tensor(values[..., cut:])


def gather_rest(first, second, index):
    return gather_tensor(first), gather_bit(second, 1, index)


def gather_core(first, second, before):
    if before:
        first, second = hold(first, *before), hold(second, *before)
    return [(part, swap_dp(part, 0)) for part in (first, second)]


def pick(values, upper, axis):
    return jnp.where(
        upper,
        lax.index_in_dim(values, 1, axis, keepdims=False),
        lax.index_in_dim(values, 0, axis, keepdims=False),
    )


def add_low(left, right):
    return left.astype(jnp.float32) + right.astype(jnp.float32)


def send_bit(values, bit, index):
    shape = values.shape
    values = values.reshape((shape[0], shape[1] // 2, 2) + shape[2:])
    return swap_dp(pick(values, ~bit_set(index, bit), 2), bit)


def keep_bit(values, received, bit, index):
    shape = values.shape
    values = values.reshape((shape[0], shape[1] // 2, 2) + shape[2:])
    return add_low(pick(values, bit_set(index, bit), 2), received)


def reduce_bit(values, bit, index):
    values = values.astype(jnp.bfloat16)
    return keep_bit(values, send_bit(values, bit, index), bit, index)


def joined(pieces):
    return jnp.concatenate([add_low(*pair) for pair in pieces], axis=-1).astype(jnp.bfloat16)


def sum_everywhere(values):
    values = values + swap_tensor(values)
    for bit in range(axis_bits(lax.axis_size("dp"))):
        values = values + swap_dp(values, bit)
    return values


def reverse_distance(table):
    return jnp.roll(table[:, ::-1], 1, axis=1)


def statistics_kernel(up_ref, self_ref, cross_ref, feed_ref, in_ref, wide_ref, bias_ref, out_ref):
    own, cross, feed = self_ref[...], cross_ref[...], feed_ref[...].astype(jnp.float32)
    columns = in_ref.shape[2]
    rows = own.shape[0]
    lane = lanes((rows, 128))
    squares = sum(jnp.sum(x * x, axis=-1, keepdims=True) for x in (own, cross, feed))

    def along(gradient, weight):
        weight = weight.astype(jnp.bfloat16).astype(jnp.float32)
        return jnp.sum(gradient * weight, axis=-1, keepdims=True)

    zero = sum(along(own[:, i * columns : (i + 1) * columns], in_ref[i]) for i in range(3))
    one = along(cross[:, 3 * columns : 4 * columns], in_ref[3])
    two = 0.0
    for tile in range(wide_ref.shape[1] // FF_TILE):
        two += along(
            feed[:, 2 * tile * FF_TILE : (2 * tile + 1) * FF_TILE],
            wide_ref[:, tile * FF_TILE : (tile + 1) * FF_TILE],
        )
    out = jnp.where(lane == 0, zero, 0.0)
    for place, column in ((1, one), (2, two), (3, squares)):
        out = jnp.where(lane == place, column, out)
    out_ref[:rows] = out
    out_ref[rows:] = bias_ref[...]


def statistics(upper, own, cross, feed, attention_in, expand_weight, bias):
    operands = (own, cross, feed, attention_in, expand_weight, bias)
    rows = own.shape[0] + bias.shape[0]
    return call(
        statistics_kernel, "statistics", (1,), [whole(x.shape) for x in operands],
        whole((rows, 128)), shape_of((rows, 128), jnp.float32),
        cost(4 * own.size, 4 * sum(x.size for x in operands)),
    )(upper, *operands)


def adam_update(weight, gradient, moment, square, learn_rate, weight_decay):
    new_moment = BETA_ONE * moment + (1.0 - BETA_ONE) * gradient
    new_square = BETA_TWO * square + (1.0 - BETA_TWO) * gradient * gradient
    direction = (
        new_moment
        / (1.0 - BETA_ONE**STEP)
        / (jnp.sqrt(new_square / (1.0 - BETA_TWO**STEP)) + ADAM_EPS)
    )
    return (new_moment, new_square, weight - learn_rate * (direction + weight_decay * weight))


def update_kernel(up_ref, clip_ref, own_ref, cross_ref, feed_ref, *refs):
    ins, outs = refs[:12], refs[12:]
    clip = clip_ref[0]
    columns = ins[0].shape[2]

    def step(group, at, gradient):
        weight, moment, square = (ins[3 * group + i][at] for i in range(3))
        new = adam_update(weight, gradient * clip, moment, square, MATRIX_RATE, DECAY_RATE)
        for i in range(3):
            outs[3 * group + i][at] = new[i]

    every = slice(None)
    for place in range(3):
        step(0, place, own_ref[:, place * columns : (place + 1) * columns])
    for place, source in ((3, 3), (4, 1), (5, 2)):
        step(0, place, cross_ref[:, source * columns : (source + 1) * columns])
    for place, source in ((0, 4), (1, 0)):
        step(1, (every, place), cross_ref[:, source * columns : (source + 1) * columns])
    for tile in range(ins[6].shape[1] // FF_TILE):
        for group in (2, 3):
            first = (2 * tile + group - 2) * FF_TILE
            step(group, (every, slice(tile * FF_TILE, (tile + 1) * FF_TILE)), feed_ref[:, first : first + FF_TILE].astype(jnp.float32))


def update(upper, clip, own, cross, feed, states):
    operands = (own, cross, feed) + tuple(states)
    out = [shape_of(states[i].shape, jnp.float32) for i in range(12)]
    return call(
        update_kernel, "update", (1,),
        [pl.BlockSpec(memory_space=pltpu.SMEM)] + [whole(x.shape) for x in operands],
        [whole(x.shape) for x in out], out,
        cost(20 * own.size, 8 * sum(x.size for x in operands)),
    )(upper, clip, *operands)


def interleave(left, right):
    rows = left.shape[0]
    parts = [part.reshape(rows, -1, 1, FF_TILE) for part in (left, right)]
    return jnp.concatenate(parts, axis=2).reshape(rows, -1)


def on_device(
    inputs,
    memory,
    dec_segments,
    mem_segments,
    mem_lengths,
    buckets,
    cotangent,
    attention_in,
    attention_out,
    expand_weight,
    contract_weight,
    norm_gains,
    position_bias,
    moment_attention_in,
    square_attention_in,
    moment_attention_out,
    square_attention_out,
    moment_expand,
    square_expand,
    moment_contract,
    square_contract,
    moment_gains,
    square_gains,
    moment_bias,
    square_bias,
):
    low = jnp.bfloat16
    everywhere = ("dp", "tensor")
    tensor_count = lax.axis_size("tensor")
    tensor_index = lax.axis_index("tensor")
    index = lax.axis_index("dp")
    rows = inputs.shape[0] // tensor_count
    length, width = inputs.shape[1], inputs.shape[2]
    keys = memory.shape[1]
    shard_rows = attention_in.shape[0]
    shards = width // shard_rows
    columns = attention_in.shape[2]
    aligned = shard_rows % ROW_TILE == 0
    upper = jnp.stack([bit_set(index, 0).astype(jnp.int32), tensor_index])
    split = (tensor_count, shards // 2, shard_rows)

    def own_rows(values):
        return lax.dynamic_slice_in_dim(values, tensor_index * rows, rows, 0)

    def flat(values):
        return values.reshape(values.shape[0] * values.shape[1], values.shape[2])

    def in_rows(values, size):
        return values.reshape(rows, size, values.shape[-1])

    wa = attention_in.astype(low)
    wo = attention_out.astype(low)
    shard = jnp.concatenate([wa[:, i] for i in (0, 1, 2)] + [wo[:, 0]] + [wa[:, i] for i in (4, 5, 3)] + [wo[:, 1]], axis=1)
    other_bias = swap_tensor(position_bias)
    far = gather_far(shard, index, [other_bias])
    halves = gather_near(far, index)
    first, second = halves
    pair_own = (first, swap_dp(first, 0))
    pair_own = in_blocks([pair_own], upper)[0]
    first = swap_tensor(first)
    second_got = swap_dp(second, 1)
    feed_shard = interleave(expand_weight.astype(low), contract_weight.astype(low))
    feed_shard = hold(feed_shard, far)
    feed_weights = lax.all_gather(feed_shard, everywhere, axis=0, tiled=True).reshape(
        shards, tensor_count, shard_rows, feed_shard.shape[1]
    )
    if not aligned:
        feed_weights = jnp.transpose(feed_weights, (1, 0, 2, 3)).reshape(
            1, tensor_count, width, feed_shard.shape[1]
        )

    decoder_ids = own_rows(dec_segments)
    key_index = jnp.arange(keys, dtype=jnp.int32)
    memory_ids = jnp.where(
        key_index[None, :] < own_rows(mem_lengths)[:, None], own_rows(mem_segments), -1
    )
    dec = decoder_ids[:, :, None]
    dec_across = jnp.pad(decoder_ids, ((0, 0), (0, TABLE - length)), constant_values=-1)[:, None]
    mem_across = memory_ids[:, None]
    own_heads = position_bias.shape[1]
    heads = own_heads * tensor_count
    both_bias = jnp.concatenate([position_bias, other_bias], axis=1)
    lookup = (
        buckets[None, :] == jnp.arange(position_bias.shape[0], dtype=jnp.int32)[:, None]
    ).astype(jnp.float32)
    lookup = jnp.pad(lookup, ((0, 0), (0, TABLE - length)))
    table = jnp.einsum(
        "gd,gm->md", lookup, both_bias, precision=lax.Precision.HIGHEST,
        preferred_element_type=jnp.float32,
    )
    table = reverse_distance(table).reshape(heads // 2, 2, TABLE)
    gains = norm_gains.T

    all_inputs, all_memory, all_cotangent = flat(inputs), flat(memory), flat(cotangent)
    normed_zero, qkv_own = project(upper, all_inputs, gains, [pair_own, pair_own], 0)
    qkv_own = in_rows(qkv_own, length)
    mixed_own, logs_own = self_forward(qkv_own, dec, dec_across, table, 0)
    first, second_got = hold(first, mixed_own), hold(second_got, mixed_own)
    second = place_bit(second, second_got, 1, index)
    pair_other, piece_cross = in_blocks(gather_core(first, second, []), upper)
    piece_self, piece_cross = [pair_own, pair_other], [piece_cross, piece_cross]
    qkv_other = in_rows(project(upper, all_inputs, gains, piece_self, 1)[1], length)
    mixed_other, logs_other = self_forward(qkv_other, dec, dec_across, table, 1)
    self_mixed = [flat(mixed_own), flat(mixed_other)]
    hidden_one, normed_one, cross_query = after_self(
        upper, all_inputs, self_mixed, gains, piece_self + piece_cross
    )
    cross_kv = in_rows(memory_project(upper, all_memory, piece_cross), keys)
    cross_query = in_rows(cross_query, length)
    cross_mixed, cross_logs = cross_forward(cross_query, cross_kv, dec, mem_across)
    split_or_whole = split if aligned else (tensor_count, 1, width // 2)
    output, feed_slopes, slope_two, slope_cm, keep_co, send_co = feed_forward(
        upper, hidden_one, flat(cross_mixed), all_cotangent, gains, piece_cross, feed_weights, split_or_whole
    )
    output = in_rows(output, length)

    def halves_of(kept, sent):
        if aligned:
            return kept, sent
        low_half = jnp.where(upper[0] == 1, sent, kept)
        high_half = jnp.where(upper[0] == 1, kept, sent)
        both = jnp.concatenate([low_half, high_half], axis=2)
        both = both.reshape((both.shape[0], shards // 2, 2, shard_rows, both.shape[-1]))
        return pick(both, upper[0] == 1, 2), pick(both, upper[0] == 0, 2)

    if not aligned:
        feed_slopes = jnp.transpose(
            feed_slopes.reshape(tensor_count, shards, shard_rows, feed_slopes.shape[-1]), (1, 0, 2, 3)
        )
    share_feed = lax.psum_scatter(
        feed_slopes.reshape(-1, feed_slopes.shape[-1]), everywhere, scatter_dimension=0, tiled=True
    )

    slope_cq, slope_ck, slope_cv = cross_backward(
        cross_query, cross_kv, dec, mem_across, cross_mixed, cross_logs, in_rows(slope_cm, length)
    )
    keep_co, send_co = halves_of(keep_co, send_co)
    got_co = swap_dp(send_co, 0)
    keep_kv, send_kv = halves_of(*outer(
        upper, all_memory, [flat(slope_ck), flat(slope_cv)], split_or_whole, "memory_outer", [got_co]
    ))
    got_kv = swap_dp(send_kv, 0)
    slope_one, slope_sm, keep_qo, send_qo = after_cross(
        upper, flat(slope_cq), normed_one, hidden_one, slope_two, self_mixed, gains,
        piece_self + piece_cross, split_or_whole, [keep_kv],
    )
    keep_qo, send_qo = halves_of(keep_qo, send_qo)
    got_qo = swap_dp(send_qo, 0)
    cross_sum = joined([(keep_co, got_co), (keep_kv, got_kv), (keep_qo, got_qo)])
    first, second = cross_sum[..., :1024], cross_sum[..., 1024:]
    first_got, second_got = swap_tensor(first[1:2]), send_bit(second, 1, index)
    slope_sm = in_rows(slope_sm, length)

    def self_half(half, qkv, mixed, logs, after):
        *slopes, diagonals = self_backward(
            qkv, dec, dec_across, table, mixed, logs, slope_sm, half, after
        )
        return [flat(slope) for slope in slopes], diagonals

    one_half = (1,) + split_or_whole[1:]
    slopes_other, diagonals_other = self_half(1, qkv_other, mixed_other, logs_other, [got_qo])
    first = hold(add_low(first[0:1], first_got).astype(low), slopes_other[0])
    second = hold(keep_bit(second, second_got, 1, index).astype(low), slopes_other[0])
    first_got, second_got = send_bit(first, 1, index), swap_tensor(second[1:2])
    keep_other, send_other = halves_of(
        *outer(upper, normed_zero, slopes_other, one_half, "self_outer")
    )
    got_other = swap_dp(send_other, 0)
    other_sum = add_low(keep_other, got_other).astype(low)
    cross_sum = jnp.concatenate(
        [keep_bit(first, first_got, 1, index), add_low(second[0:1], second_got)], axis=-1
    ).astype(low)
    cross_sum = hold(cross_sum, keep_other)
    cross_ready = cross_sum
    cross_got = send_bit(cross_sum, 2, index)
    other_got = swap_tensor(other_sum)
    slopes_own, diagonals_own = self_half(0, qkv_own, mixed_own, logs_own, [other_sum])
    cross_sum = hold(keep_bit(cross_sum, cross_got, 2, index), slopes_own[0])
    bits = axis_bits(lax.axis_size("dp"))
    for bit in range(3, bits):
        cross_sum = reduce_bit(cross_sum, bit, index)
    keep_own, send_own = halves_of(
        *outer(upper, normed_zero, slopes_own, one_half, "self_outer", [cross_ready])
    )
    got_own = swap_dp(send_own, 0)
    memory_slopes = [hold(flat(slope_ck), keep_own), flat(slope_cv)]
    memory_grad = memory_back(upper, *memory_slopes, piece_cross, 0, [])
    other_got = hold(other_got, memory_grad)
    self_sum = (add_low(keep_own, got_own) + other_got.astype(jnp.float32)).astype(low)
    self_got = send_bit(self_sum, 1, index)
    slopes_self = [part for pair in zip(slopes_own, slopes_other) for part in pair]
    diagonals = jnp.concatenate([diagonals_own, diagonals_other], axis=0)
    (input_slope,) = input_back(
        upper, slopes_self, all_inputs, slope_one, gains, piece_self, [got_own]
    )
    input_got = swap_tensor(input_slope)
    self_sum = hold(keep_bit(self_sum, self_got, 1, index), input_slope)
    for bit in range(2, bits):
        if bit == 2:
            self_got = send_bit(self_sum.astype(low), bit, index)
            memory_slopes[0] = hold(memory_slopes[0], input_slope)
            memory_grad = memory_back(upper, *memory_slopes, piece_cross, 1, [memory_grad])
            self_sum = keep_bit(self_sum.astype(low), hold(self_got, memory_grad), bit, index)
        else:
            self_got = send_bit(self_sum.astype(low), bit, index)
            if bit == bits - 1 and False:
                self_got = hold(self_got, input_got)
            self_sum = keep_bit(self_sum.astype(low), self_got, bit, index)
    memory_grad = in_rows(memory_grad, keys)
    share_cross, share_self = cross_sum[0, 0], self_sum[0, 0]
    input_grad = (
        in_order(in_rows(input_slope, length), in_rows(input_got, length), tensor_index == 1, 0)
        .reshape(inputs.shape)
        .astype(jnp.float32)
    )

    bias_local = jnp.einsum(
        "gd,md->gm", lookup, reverse_distance(diagonals.reshape(heads, TABLE)),
        precision=lax.Precision.HIGHEST, preferred_element_type=jnp.float32,
    )
    bias_local = jnp.where(
        tensor_index == 1, jnp.roll(bias_local, own_heads, axis=1), bias_local
    )
    bias_rows = bias_local.size // 128
    bias_tile = jnp.pad(bias_local.reshape(bias_rows, 128), ((0, 8 - bias_rows), (0, 0)))
    table_rows = statistics(
        upper, share_self, share_cross, share_feed, jnp.swapaxes(attention_in, 0, 1), expand_weight, bias_tile
    )
    table_rows = table_rows + hold(swap_tensor(table_rows), input_got)
    totals = table_rows[shard_rows:]
    table_rows = table_rows[:shard_rows]
    old_gains = lax.dynamic_slice_in_dim(norm_gains, index * shard_rows, shard_rows, 0)
    shared_gains = table_rows[:, :3] / old_gains
    square_sum = jnp.sum(table_rows[:, 3]) + jnp.sum(shared_gains * shared_gains)
    totals = totals + jnp.where(
        lax.broadcasted_iota(jnp.int32, totals.shape, 0) == bias_rows, square_sum, 0.0
    )
    for bit in range(bits):
        totals = totals + swap_dp(totals, bit)
    bias_sums = totals[:bias_rows].reshape(bias_local.shape)
    grad_norm = jnp.sqrt(totals[bias_rows, 0] + jnp.sum(bias_sums * bias_sums))
    clip_factor = jnp.minimum(1.0, CLIP_NORM / (grad_norm + 1e-06))

    bias_share = lax.dynamic_slice_in_dim(bias_sums, tensor_index * own_heads, own_heads, 1)
    new = update(
        upper, clip_factor[None], share_self, share_cross, share_feed,
        tuple(
            jnp.swapaxes(state, 0, 1)
            for state in (attention_in, moment_attention_in, square_attention_in)
        )
        + (
            attention_out, moment_attention_out, square_attention_out,
            expand_weight, moment_expand, square_expand,
            contract_weight, moment_contract, square_contract,
        ),
    )
    new = [jnp.swapaxes(state, 0, 1) for state in new[:3]] + list(new[3:])
    new_gains = adam_update(
        old_gains, shared_gains * clip_factor, moment_gains, square_gains, SMALL_RATE, 0.0
    )
    new_bias = adam_update(
        position_bias, bias_share * clip_factor, moment_bias, square_bias, SMALL_RATE, 0.0
    )
    return (
        (output, input_grad, memory_grad, grad_norm)
        + tuple(new) + new_gains + new_bias
    )


def solution(mesh):
    return jax.shard_map(
        on_device,
        mesh=mesh,
        in_specs=(
            P("dp", None, None),
            P("dp", None, None),
            P("dp", None),
            P("dp", None),
            P("dp"),
            P(),
            P("dp", None, None),
            P("dp", None, "tensor"),
            P("dp", None, "tensor"),
            P("dp", "tensor"),
            P("dp", "tensor"),
            P(),
            P(None, "tensor"),
            P("dp", None, "tensor"),
            P("dp", None, "tensor"),
            P("dp", None, "tensor"),
            P("dp", None, "tensor"),
            P("dp", "tensor"),
            P("dp", "tensor"),
            P("dp", "tensor"),
            P("dp", "tensor"),
            P("dp", None),
            P("dp", None),
            P(None, "tensor"),
            P(None, "tensor"),
        ),
        out_specs=(
            P(("dp", "tensor"), None, None),
            P("dp", None, None),
            P(("dp", "tensor"), None, None),
            P(),
            P("dp", None, "tensor"),
            P("dp", None, "tensor"),
            P("dp", None, "tensor"),
            P("dp", None, "tensor"),
            P("dp", None, "tensor"),
            P("dp", None, "tensor"),
            P("dp", "tensor"),
            P("dp", "tensor"),
            P("dp", "tensor"),
            P("dp", "tensor"),
            P("dp", "tensor"),
            P("dp", "tensor"),
            P("dp", None),
            P("dp", None),
            P("dp", None),
            P(None, "tensor"),
            P(None, "tensor"),
            P(None, "tensor"),
        ),
        check_vma=False,
    )
```

```python
import functools

import jax
import jax.numpy as jnp
from jax import lax
from jax.experimental import pallas as pl
from jax.experimental.pallas import tpu as pltpu
from jax.sharding import PartitionSpec as P

STEP = 10
NORM_EPS = 1e-06
CLIP_NORM = 1.0
BETA_ONE = 0.9
BETA_TWO = 0.95
ADAM_EPS = 1e-08
MATRIX_RATE = 0.08
SMALL_RATE = 0.8
DECAY_RATE = 0.1
GELU_SCALE = 0.7978845608028654
GELU_CUBIC = 0.044715
MASKED = -1e30
TABLE = 384
NT = (((1,), (1,)), ((), ()))
TN = (((0,), (0,)), ((), ()))


def dot(a, b, dims=(((1,), (0,)), ((), ()))):
    return lax.dot_general(a, b, dims, preferred_element_type=jnp.float32)


def lanes(shape):
    return lax.broadcasted_iota(jnp.int32, shape, len(shape) - 1)


def half_of(values, which):
    return jnp.where((lanes(values.shape) >= 64) == (which == 1), values, jnp.zeros_like(values))


def column(values, index):
    return jnp.sum(jnp.where(lanes(values.shape) == index, values, 0.0), axis=-1, keepdims=True)


def cross_forward_kernel(q_ref, k_ref, v_ref, dec_ref, mem_ref, o_ref, lse_ref):
    pair = pl.program_id(1)
    query, key, value = q_ref[0], k_ref[0], v_ref[0]
    allowed = dec_ref[0] == mem_ref[0]
    mixed, logs = forward_pair(query, key, value, [None, None], allowed)
    o_ref[0] = mixed.astype(o_ref.dtype)
    store_logs(lse_ref, logs, pair)


def store_logs(lse_ref, logs, pair):
    @pl.when(pair == 0)
    def _():
        lse_ref[0] = jnp.zeros(lse_ref.shape[1:], jnp.float32)

    lane = lanes(lse_ref.shape[1:])
    kept = lse_ref[0]
    for which in range(2):
        kept = jnp.where(lane == 2 * pair + which, logs[which], kept)
    lse_ref[0] = kept


def forward_pair(query, key, value, biases, allowed):
    mixed = jnp.zeros(query.shape, jnp.float32)
    logs = []
    for which in range(2):
        scores = dot(half_of(query, which), key, NT)
        if biases[which] is not None:
            scores = scores + biases[which]
        scores = jnp.where(allowed, scores, MASKED)
        top = jnp.max(scores, axis=-1, keepdims=True)
        weights = jnp.exp(scores - top)
        total = jnp.sum(weights, axis=-1, keepdims=True)
        logs.append(top + jnp.log(total))
        mixed = mixed + dot(weights.astype(jnp.bfloat16), half_of(value, which)) * (1.0 / total)
    return mixed, logs


def backward_pair(query, key, value, mixed, upstream, logs, biases, allowed):
    slope_q = jnp.zeros(query.shape, jnp.float32)
    slope_k = jnp.zeros(key.shape, jnp.float32)
    slope_v = jnp.zeros(key.shape, jnp.float32)
    grads = []
    product = upstream.astype(jnp.float32) * mixed.astype(jnp.float32)
    for which in range(2):
        query_half = half_of(query, which)
        up_half = half_of(upstream, which)
        scores = dot(query_half, key, NT)
        if biases[which] is not None:
            scores = scores + biases[which]
        prob = jnp.exp(jnp.where(allowed, scores - logs[which], MASKED))
        slope_p = dot(up_half, value, NT)
        inner = jnp.sum(half_of(product, which), axis=-1, keepdims=True)
        grad = (prob * (slope_p - inner)).astype(jnp.bfloat16)
        slope_q = slope_q + dot(grad, half_of(key, which))
        slope_k = slope_k + dot(grad, query_half, TN)
        slope_v = slope_v + dot(prob.astype(jnp.bfloat16), up_half, TN)
        grads.append(grad)
    return slope_q, slope_k, slope_v, grads


def cross_backward_kernel(
    q_ref, k_ref, v_ref, dec_ref, mem_ref, o_ref, lse_ref, up_ref, dq_ref, dk_ref, dv_ref
):
    pair = pl.program_id(1)
    allowed = dec_ref[0] == mem_ref[0]
    logs = [column(lse_ref[0], 2 * pair + which) for which in range(2)]
    slope_q, slope_k, slope_v, _ = backward_pair(
        q_ref[0], k_ref[0], v_ref[0], o_ref[0], up_ref[0], logs, [None, None], allowed
    )
    dq_ref[0] = slope_q.astype(jnp.bfloat16)
    dk_ref[0] = slope_k.astype(jnp.bfloat16)
    dv_ref[0] = slope_v.astype(jnp.bfloat16)


def pad_keys(values):
    extra = TABLE - values.shape[0]
    return jnp.concatenate([values, jnp.zeros((extra, values.shape[1]), values.dtype)], axis=0)


def self_allowed(dec_ref, decT_ref):
    length = dec_ref.shape[1]
    rows = lax.broadcasted_iota(jnp.int32, (length, TABLE), 0)
    return (dec_ref[0] == decT_ref[0]) & (lanes((length, TABLE)) <= rows)


def toeplitz(table_ref, which, length):
    spread = jnp.broadcast_to(table_ref[0, which : which + 1, :], (length, TABLE))
    return pltpu.roll(spread, 0, 1, stride=1, stride_axis=0)


def self_forward_kernel(q_ref, k_ref, v_ref, dec_ref, decT_ref, table_ref, o_ref, lse_ref):
    pair = pl.program_id(1)
    length = q_ref.shape[1]
    biases = [toeplitz(table_ref, which, length) for which in range(2)]
    mixed, logs = forward_pair(
        q_ref[0], pad_keys(k_ref[0]), pad_keys(v_ref[0]), biases, self_allowed(dec_ref, decT_ref)
    )
    o_ref[0] = mixed.astype(o_ref.dtype)
    store_logs(lse_ref, logs, pair)


def self_backward_kernel(ties, *refs):
    q_ref, k_ref, v_ref, dec_ref, decT_ref, table_ref, o_ref, lse_ref, up_ref = refs[:9]
    dq_ref, dk_ref, dv_ref, diag_ref = refs[9 + ties :]
    pair, row = pl.program_id(0), pl.program_id(1)
    length = q_ref.shape[1]
    biases = [toeplitz(table_ref, which, length) for which in range(2)]
    logs = [column(lse_ref[0], 2 * pair + which) for which in range(2)]
    slope_q, slope_k, slope_v, grads = backward_pair(
        q_ref[0], pad_keys(k_ref[0]), pad_keys(v_ref[0]), o_ref[0], up_ref[0], logs, biases,
        self_allowed(dec_ref, decT_ref),
    )
    dq_ref[0] = slope_q.astype(jnp.bfloat16)
    dk_ref[0] = slope_k[:length].astype(jnp.bfloat16)
    dv_ref[0] = slope_v[:length].astype(jnp.bfloat16)

    @pl.when(row == 0)
    def _():
        diag_ref[...] = jnp.zeros(diag_ref.shape, jnp.float32)

    for which in range(2):
        diag_ref[0, which : which + 1, :] += diagonal_sums(grads[which].astype(jnp.float32))


def diagonal_sums(values):
    groups = jnp.zeros((8, TABLE), jnp.float32)
    for start in range(0, values.shape[0], 8):
        groups = groups + pltpu.roll(values[start : start + 8], (TABLE - start) % TABLE, 1)
    total = groups[0:1]
    for row in range(1, 8):
        total = total + pltpu.roll(groups, TABLE - row, 1)[row : row + 1]
    return total


def params(count):
    return pltpu.CompilerParams(
        dimension_semantics=("arbitrary",) * count, vmem_limit_bytes=48 * 1024 * 1024
    )


def cross_forward(q, kv, dec, mem):
    rows, length, width = q.shape
    keys = kv.shape[1]
    pairs = width // 128
    lanes_q = pl.BlockSpec((1, length, 128), lambda r, p: (r, 0, p))
    lanes_k = pl.BlockSpec((1, keys, 128), lambda r, p: (r, 0, p))
    lanes_v = pl.BlockSpec((1, keys, 128), lambda r, p: (r, 0, p + pairs))
    return pl.pallas_call(
        cross_forward_kernel,
        grid=(rows, width // 128),
        in_specs=[
            lanes_q, lanes_k, lanes_v,
            pl.BlockSpec((1, length, 1), lambda r, p: (r, 0, 0)),
            pl.BlockSpec((1, 1, keys), lambda r, p: (r, 0, 0)),
        ],
        out_specs=[lanes_q, pl.BlockSpec((1, length, 128), lambda r, p: (r, 0, 0))],
        out_shape=[
            jax.ShapeDtypeStruct((rows, length, width), jnp.bfloat16),
            jax.ShapeDtypeStruct((rows, length, 128), jnp.float32),
        ],
        compiler_params=params(2),
        cost_estimate=cost(4 * rows * length * keys * width, 2 * rows * width * (2 * length + 2 * keys), 2 * rows * length * keys * pairs),
        name="cross_forward",
    )(q, kv, kv, dec, mem)


def cross_backward(q, kv, dec, mem, mixed, logs, upstream):
    rows, length, width = q.shape
    keys = kv.shape[1]
    pairs = width // 128
    lanes_q = pl.BlockSpec((1, length, 128), lambda r, p: (r, 0, p))
    lanes_k = pl.BlockSpec((1, keys, 128), lambda r, p: (r, 0, p))
    lanes_v = pl.BlockSpec((1, keys, 128), lambda r, p: (r, 0, p + pairs))
    return pl.pallas_call(
        cross_backward_kernel,
        grid=(rows, width // 128),
        in_specs=[
            lanes_q, lanes_k, lanes_v,
            pl.BlockSpec((1, length, 1), lambda r, p: (r, 0, 0)),
            pl.BlockSpec((1, 1, keys), lambda r, p: (r, 0, 0)),
            lanes_q, pl.BlockSpec((1, length, 128), lambda r, p: (r, 0, 0)), lanes_q,
        ],
        out_specs=[lanes_q, lanes_k, lanes_k],
        out_shape=[
            jax.ShapeDtypeStruct((rows, length, width), jnp.bfloat16),
            jax.ShapeDtypeStruct((rows, keys, width), jnp.bfloat16),
            jax.ShapeDtypeStruct((rows, keys, width), jnp.bfloat16),
        ],
        compiler_params=params(2),
        cost_estimate=cost(10 * rows * length * keys * width, 2 * rows * width * (4 * length + 4 * keys), 2 * rows * length * keys * pairs),
        name="cross_backward",
    )(q, kv, kv, dec, mem, mixed, logs, upstream)


def self_forward(qkv, dec, decT, table, half):
    rows, length, width = qkv.shape
    count = width // 384
    first = half * count
    spec = pl.BlockSpec((1, length, 128), lambda r, p: (r, 0, p))
    spec_k = pl.BlockSpec((1, length, 128), lambda r, p: (r, 0, p + count))
    spec_v = pl.BlockSpec((1, length, 128), lambda r, p: (r, 0, p + 2 * count))
    return pl.pallas_call(
        self_forward_kernel,
        grid=(rows, count),
        in_specs=[
            spec, spec_k, spec_v,
            pl.BlockSpec((1, length, 1), lambda r, p: (r, 0, 0)),
            pl.BlockSpec((1, 1, TABLE), lambda r, p: (r, 0, 0)),
            pl.BlockSpec((1, 2, TABLE), lambda r, p: (p + first, 0, 0)),
        ],
        out_specs=[
            pl.BlockSpec((1, length, 128), lambda r, p: (r, 0, p)),
            pl.BlockSpec((1, length, 128), lambda r, p: (r, 0, 0)),
        ],
        out_shape=[
            jax.ShapeDtypeStruct((rows, length, width // 3), jnp.bfloat16),
            jax.ShapeDtypeStruct((rows, length, 128), jnp.float32),
        ],
        compiler_params=params(2),
        cost_estimate=cost(2 * rows * length * TABLE * width // 3, 8 * rows * width * length // 3, 2 * rows * length * TABLE * count),
        name="self_forward",
    )(qkv, qkv, qkv, dec, decT, table)


def self_backward(qkv, dec, decT, table, mixed, logs, upstream, half, after):
    rows, length, width = qkv.shape
    count = width // 384
    first = half * count
    spec = pl.BlockSpec((1, length, 128), lambda p, r: (r, 0, p))
    spec_k = pl.BlockSpec((1, length, 128), lambda p, r: (r, 0, p + count))
    spec_v = pl.BlockSpec((1, length, 128), lambda p, r: (r, 0, p + 2 * count))
    spec_up = pl.BlockSpec((1, length, 128), lambda p, r: (r, 0, p + first))
    out = jax.ShapeDtypeStruct((rows, length, width // 3), jnp.bfloat16)
    return pl.pallas_call(
        functools.partial(self_backward_kernel, len(after)),
        grid=(count, rows),
        in_specs=[
            spec, spec_k, spec_v,
            pl.BlockSpec((1, length, 1), lambda p, r: (r, 0, 0)),
            pl.BlockSpec((1, 1, TABLE), lambda p, r: (r, 0, 0)),
            pl.BlockSpec((1, 2, TABLE), lambda p, r: (p + first, 0, 0)), spec,
            pl.BlockSpec((1, length, 128), lambda p, r: (r, 0, 0)), spec_up,
        ] + [pl.BlockSpec(memory_space=pl.ANY)] * len(after),
        out_specs=[spec, spec, spec, pl.BlockSpec((1, 2, TABLE), lambda p, r: (p, 0, 0))],
        out_shape=[out, out, out, jax.ShapeDtypeStruct((count, 2, TABLE), jnp.float32)],
        compiler_params=params(2),
        cost_estimate=cost(5 * rows * length * TABLE * width // 3, 16 * rows * width * length // 3, 2 * rows * length * TABLE * count),
        name="self_backward",
    )(qkv, qkv, qkv, dec, decT, table, mixed, logs, upstream, *after)


SLOPE = GELU_SCALE * 3.0 * GELU_CUBIC
ROW_TILE = 16
FF_TILE = 512
MEMORY_TILE = 512


def whole(shape):
    return pl.BlockSpec(shape, lambda *_: (0,) * len(shape))


def cost(flops, moved, exps=0):
    return pl.CostEstimate(flops=int(flops), bytes_accessed=int(moved), transcendentals=int(exps))


def row_scale(hidden):
    return lax.rsqrt(jnp.mean(hidden * hidden, axis=-1, keepdims=True) + NORM_EPS)


def row_back(hidden, gain, upstream):
    factor = row_scale(hidden)
    scaled = upstream * hidden
    inner = jnp.mean(scaled * gain, axis=-1, keepdims=True)
    slope = factor * (upstream * gain) - (factor * factor * factor * inner) * hidden
    return slope


def emit(gradient, keep_ref, send_ref, start, upper):
    halves, blocks, rows, _ = keep_ref.shape
    columns = gradient.shape[1] // halves
    for half in range(halves):
        part = gradient[:, half * columns : (half + 1) * columns]
        part = part.reshape(blocks, 2, rows, columns)
        low, high = part[:, 0], part[:, 1]
        keep = jnp.where(upper, high, low).astype(jnp.bfloat16)
        send = jnp.where(upper, low, high).astype(jnp.bfloat16)
        keep_ref[half, :, :, start : start + columns] = keep
        send_ref[half, :, :, start : start + columns] = send


def call(kernel, name, grid, in_specs, out_specs, out_shape, work, scratch=(), weights=(), after=(), aliases=None):
    count, loaded = len(in_specs), 2 * len(weights)
    outs = len(out_specs) if isinstance(out_specs, list) else 1

    def run(up_ref, *refs):
        ins = refs[:count]
        pieces = refs[count : count + loaded]
        kernel(up_ref, *ins, pieces, *refs[count + loaded + len(after) :])

    anywhere = pl.BlockSpec(memory_space=pl.ANY)
    return lambda upper, *operands: pl.pallas_call(
        run if weights else lambda up_ref, *refs: kernel(up_ref, *refs[:count], *refs[count + len(after) :]),
        grid_spec=pltpu.PrefetchScalarGridSpec(
            num_scalar_prefetch=1,
            grid=grid,
            in_specs=in_specs + [anywhere] * (loaded + len(after)),
            out_specs=out_specs,
            scratch_shapes=scratch,
        ),
        out_shape=out_shape,
        input_output_aliases=aliases or {},
        compiler_params=pltpu.CompilerParams(
            dimension_semantics=("arbitrary",) * len(grid), vmem_limit_bytes=56 * 1024 * 1024
        ),
        cost_estimate=work,
        name=name,
    )(upper, *operands, *[piece for pair in weights for piece in pair], *after)


def fetch(pieces, store, sems, mats, upper):
    copies = []
    columns = store.shape[3] // len(mats)
    for place, (source, begin, half) in enumerate(mats):
        group = []
        for other in range(2):
            piece = pieces[4 * source + 2 * half + other]
            copy = pltpu.make_async_copy(
                piece.at[half % piece.shape[0], :, :, pl.ds(begin, columns)],
                store.at[:, (upper + other) % 2, :, pl.ds(place * columns, columns)],
                sems.at[place * 2 + other],
            )
            group.append(copy)
        copies.append(group)
    return copies


def start(copies):
    for group in copies:
        for copy in group:
            copy.start()


def wait(group):
    for copy in group:
        copy.wait()


def shape_of(shape, kind=jnp.bfloat16):
    return jax.ShapeDtypeStruct(shape, kind)


def kernel_of(store, place, width):
    return store[:, :, :, place * width : (place + 1) * width].reshape(store.shape[0] * 2 * store.shape[2], width)


def room(weights, count):
    _, blocks, rows, columns = weights[0][0].shape
    wide = count * (columns // 4)
    return [pltpu.VMEM((blocks, 2, rows, wide), jnp.bfloat16), pltpu.SemaphoreType.DMA((2 * count,))]


QKV, SO = (0, 1, 2), 3
CKV, CQ, CO = (0, 1), 2, 3


def placed(mats, pieces, source=0, halves=(0, 1)):
    columns = pieces[0].shape[3] // 4
    return [(source, which * columns, half) for which in mats for half in halves]


def project_kernel(half, up_ref, x_ref, gain_ref, pieces, n_ref, out_ref, store, sems):
    copies = fetch(pieces, store, sems, placed(QKV, pieces, 0, (half,)), up_ref[0])

    @pl.when(pl.program_id(0) == 0)
    def _():
        start(copies)
        hidden = x_ref[...].astype(jnp.float32)
        n_ref[...] = (hidden * row_scale(hidden) * gain_ref[0:1]).astype(jnp.bfloat16)

    width = out_ref.shape[1]
    for place in range(3):
        @pl.when(pl.program_id(0) == place)
        def _():
            wait(copies[place])
            out_ref[...] = dot(n_ref[...], kernel_of(store, place, width)).astype(jnp.bfloat16)


def project_again_kernel(half, up_ref, n_ref, pieces, out_ref, store, sems):
    copies = fetch(pieces, store, sems, placed(QKV, pieces, 0, (half,)), up_ref[0])

    @pl.when(pl.program_id(0) == 0)
    def _():
        start(copies)

    width = out_ref.shape[1]
    for place in range(3):
        @pl.when(pl.program_id(0) == place)
        def _():
            wait(copies[place])
            out_ref[...] = dot(n_ref[...], kernel_of(store, place, width)).astype(jnp.bfloat16)


def project_again(upper, normed, pieces, half):
    tokens, width = normed.shape
    wide = width // 2
    return call(
        functools.partial(project_again_kernel, half), "project_again", (3,),
        [whole((tokens, width))], pl.BlockSpec((tokens, wide), lambda g, *_: (0, g)),
        shape_of((tokens, 3 * wide)),
        cost(3 * tokens * width * width, 2 * width * (3 * tokens + 2 * width)),
        scratch=room(pieces, 3), weights=pieces,
    )(upper, normed)


def own_spec(tokens, width):
    return pl.BlockSpec((tokens, width), lambda g, up: (up[1], 0))


def project(upper, inputs, gains, pieces, half):
    tokens, width = inputs.shape[0] // 2, inputs.shape[1]
    wide = width // 2
    return call(
        functools.partial(project_kernel, half), "project", (3,),
        [own_spec(tokens, width), whole(gains.shape)],
        [whole((tokens, width)), pl.BlockSpec((tokens, wide), lambda g, *_: (0, g))],
        [shape_of((tokens, width)), shape_of((tokens, 3 * wide))],
        cost(3 * tokens * width * width, 2 * width * (3 * tokens + 2 * width)), scratch=room(pieces, 3), weights=pieces,
    )(upper, inputs, gains)


def memory_project_kernel(up_ref, x_ref, pieces, out_ref, store, sems):
    copies = fetch(pieces, store, sems, placed(CKV, pieces), up_ref[0])

    @pl.when(pl.program_id(0) == 0)
    def _():
        start(copies)
        for group in copies:
            wait(group)

    width = x_ref.shape[1]
    out_ref[...] = dot(x_ref[...], kernel_of(store, 0, 2 * width)).astype(jnp.bfloat16)


def memory_project(upper, memory, pieces):
    tokens, width = memory.shape[0] // 2, memory.shape[1]
    tile = MEMORY_TILE
    steps = tokens // tile
    return call(
        memory_project_kernel, "memory_project", (steps,),
        [pl.BlockSpec((tile, width), lambda g, up: (up[1] * steps + g, 0))],
        pl.BlockSpec((tile, 2 * width), lambda g, *_: (g, 0)),
        shape_of((tokens, 2 * width)),
        cost(4 * tokens * width * width, 2 * width * (3 * tokens + 2 * width)), scratch=room(pieces, 4), weights=pieces,
    )(upper, memory)


def after_self_kernel(up_ref, x_ref, a_ref, b_ref, gain_ref, pieces, h_ref, n_ref, q_ref, store, sems):
    copies = fetch(pieces, store, sems, placed([SO], pieces) + placed([CQ], pieces, 1), up_ref[0])

    @pl.when(pl.program_id(0) == 0)
    def _():
        start(copies)
        for group in copies:
            wait(group)

    width = x_ref.shape[1]
    weight = kernel_of(store, 0, width)
    hidden = x_ref[...].astype(jnp.float32) + dot(a_ref[...], weight[:, : width // 2], NT)
    hidden += dot(b_ref[...], weight[:, width // 2 :], NT)
    h_ref[...] = hidden
    normed = (hidden * row_scale(hidden) * gain_ref[1:2]).astype(jnp.bfloat16)
    n_ref[...] = normed
    q_ref[...] = dot(normed, kernel_of(store, 1, width)).astype(jnp.bfloat16)


def after_self(upper, inputs, mixed, gains, pieces):
    tokens, width = inputs.shape[0] // 2, inputs.shape[1]
    tile = tokens // 2
    rows = pl.BlockSpec((tile, width), lambda g, *_: (g, 0))
    half = pl.BlockSpec((tile, width // 2), lambda g, *_: (g, 0))
    return call(
        after_self_kernel, "after_self", (2,),
        [pl.BlockSpec((tile, width), lambda g, up: (2 * up[1] + g, 0)), half, half, whole(gains.shape)],
        [rows, rows, rows],
        [shape_of((tokens, width), jnp.float32), shape_of((tokens, width)), shape_of((tokens, width))],
        cost(4 * tokens * width * width, width * (12 * tokens + 4 * width)), scratch=room(pieces, 4), weights=pieces,
    )(upper, inputs, *mixed, gains)


def feed_kernel(
    up_ref, h1_ref, a_ref, gy_ref, gain_ref, w_ref, pieces,
    y_ref, g_ref, gh_ref, ga_ref, keep_ref, send_ref,
    n_ref, nT_ref, gyT_ref, acc_ref, store, sems,
):
    step = pl.program_id(0)
    tile = FF_TILE
    width = y_ref.shape[1]
    copies = fetch(pieces, store, sems, placed([CO], pieces), up_ref[0])

    @pl.when(step == 0)
    def _():
        start(copies)
        gyT_ref[...] = gy_ref[...].T
        wait(copies[0])
        wait(copies[1])
        hidden = h1_ref[...] + dot(a_ref[...], kernel_of(store, 0, width), NT)
        gh_ref[...] = hidden
        y_ref[...] = hidden
        normed = (hidden * row_scale(hidden) * gain_ref[2:3]).astype(jnp.bfloat16)
        n_ref[...] = normed
        nT_ref[...] = normed.T
        acc_ref[...] = jnp.zeros(acc_ref.shape, jnp.float32)

    wi = w_ref[:, 0, :, :tile].reshape(width, tile)
    wf = w_ref[:, 0, :, tile:].reshape(width, tile)
    u = dot(n_ref[...], wi)
    square = u * u
    bent = jnp.tanh(u * (GELU_SCALE + (GELU_SCALE * GELU_CUBIC) * square))
    half = 0.5 + 0.5 * bent
    act = (u * half).astype(jnp.bfloat16)
    slope = half + (0.5 * u) * (1.0 - bent * bent) * (GELU_SCALE + SLOPE * square)
    gu = (dot(gy_ref[...], wf) * slope).astype(jnp.bfloat16)
    y_ref[...] += dot(act, wf, NT)
    acc_ref[...] += dot(gu, wi, NT)
    g_ref[:, 0, :, :tile] = dot(nT_ref[...], gu).reshape(g_ref.shape[0], g_ref.shape[2], tile).astype(jnp.bfloat16)
    g_ref[:, 0, :, tile:] = dot(gyT_ref[...], act).reshape(g_ref.shape[0], g_ref.shape[2], tile).astype(jnp.bfloat16)

    @pl.when(step == pl.num_programs(0) - 1)
    def _():
        back = row_back(gh_ref[...], gain_ref[2:3], acc_ref[...])
        total = gy_ref[...].astype(jnp.float32) + back
        gh_ref[...] = total
        low = total.astype(jnp.bfloat16)
        ga_ref[...] = dot(low, kernel_of(store, 0, width)).astype(jnp.bfloat16)
        emit(dot(low.T, a_ref[...]), keep_ref, send_ref, 0, up_ref[0] == 1)


def feed_forward(upper, hidden, mixed, cotangent, gains, pieces, weights, split):
    tokens, width = hidden.shape
    blocks, halves, rows, wide = weights.shape
    steps = wide // (2 * FF_TILE)
    spec = pl.BlockSpec((blocks, 1, rows, 2 * FF_TILE), lambda g, *_: (0, g // steps, 0, g % steps))
    full = whole((tokens, width))
    f32 = shape_of((tokens, width), jnp.float32)
    columns = width // halves
    return call(
        feed_kernel, "feed_forward", (halves * steps,),
        [full, full, own_spec(tokens, width), whole(gains.shape), spec],
        [full, spec, full, full, whole(split + (columns,)), whole(split + (columns,))],
        [f32, shape_of(weights.shape), f32, shape_of((tokens, width)),
         shape_of(split + (columns,)), shape_of(split + (columns,))],
        cost(6 * tokens * width * halves * wide, 40 * tokens * width, tokens * halves * wide / 2),
        scratch=[
            pltpu.VMEM((tokens, width), jnp.bfloat16), pltpu.VMEM((width, tokens), jnp.bfloat16),
            pltpu.VMEM((width, tokens), jnp.bfloat16), pltpu.VMEM((tokens, width), jnp.float32),
        ] + room(pieces, 2), weights=pieces,
    )(upper, hidden, mixed, cotangent, gains, weights)


def after_cross_kernel(
    up_ref, gq_ref, n_ref, h_ref, gh_ref, a_ref, b_ref, gain_ref, pieces,
    gh1_ref, ga_ref, keep_ref, send_ref, store, sems,
):
    copies = fetch(pieces, store, sems, placed([SO], pieces) + placed([CQ], pieces, 1), up_ref[0])
    start(copies)
    upper = up_ref[0] == 1
    columns = keep_ref.shape[3] // 2
    width = h_ref.shape[1]
    emit(dot(n_ref[...].T, gq_ref[...]), keep_ref, send_ref, 0, upper)
    wait(copies[2])
    wait(copies[3])
    back = row_back(h_ref[...], gain_ref[1:2], dot(gq_ref[...], kernel_of(store, 1, width), NT))
    total = gh_ref[...] + back
    gh1_ref[...] = total
    low = total.astype(jnp.bfloat16)
    wait(copies[0])
    wait(copies[1])
    ga_ref[...] = dot(low, kernel_of(store, 0, width)).astype(jnp.bfloat16)
    across = low.T
    emit(dot(across, a_ref[...]), keep_ref.at[0:1], send_ref.at[0:1], columns, upper)
    emit(dot(across, b_ref[...]), keep_ref.at[1:2], send_ref.at[1:2], columns, upper)


def after_cross(upper, slope_q, normed, hidden, slope_hidden, mixed, gains, pieces, split, after):
    tokens, width = hidden.shape
    full = whole((tokens, width))
    piece = split + (2 * (width // split[0]),)
    return call(
        after_cross_kernel, "after_cross", (1,),
        [full, full, full, full, whole((tokens, width // 2)), whole((tokens, width // 2)), whole(gains.shape)],
        [full, full, whole(piece), whole(piece)],
        [shape_of((tokens, width), jnp.float32), shape_of((tokens, width)),
         shape_of(piece), shape_of(piece)],
        cost(8 * tokens * width * width, tokens * width * 24 + 8 * width * width),
        scratch=room(pieces, 4), weights=pieces, after=after,
    )(upper, slope_q, normed, hidden, slope_hidden, *mixed, gains)


def outer_kernel(up_ref, x_ref, *refs):
    slopes, keep_ref, send_ref = refs[:-2], refs[-2], refs[-1]
    upper = up_ref[0] == 1
    columns = keep_ref.shape[3] // len(slopes)
    across = x_ref[...].T
    for place, slope in enumerate(slopes):
        emit(dot(across, slope[...]), keep_ref, send_ref, place * columns, upper)


def outer(upper, rows, slopes, split, name, after=()):
    tokens, width = slopes[0].shape[0], rows.shape[1]
    wide = slopes[0].shape[1]
    piece = split + (len(slopes) * (wide // split[0]),)
    return call(
        outer_kernel, name, (1,),
        [whole(rows.shape) if rows.shape[0] == tokens else own_spec(tokens, width)]
        + [whole(slope.shape) for slope in slopes],
        [whole(piece), whole(piece)],
        [shape_of(piece), shape_of(piece)],
        cost(2 * tokens * width * wide * len(slopes), 2 * (tokens + width) * (width + wide * len(slopes))),
        after=after,
    )(upper, rows, *slopes)


def memory_back_kernel(up_ref, gk_ref, gv_ref, pieces, out_ref, store, sems):
    copies = fetch(pieces, store, sems, placed(CKV, pieces), up_ref[0])

    @pl.when(pl.program_id(0) == 0)
    def _():
        start(copies)
        for group in copies:
            wait(group)

    width = gk_ref.shape[1]
    out_ref[...] = dot(gk_ref[...], kernel_of(store, 0, width), NT) + dot(gv_ref[...], kernel_of(store, 1, width), NT)


def memory_back(upper, slope_k, slope_v, pieces, part, earlier):
    tokens, width = slope_k.shape
    tile = MEMORY_TILE
    first = part * (tokens // 2 // tile)
    rows = pl.BlockSpec((tile, width), lambda g, *_: (g + first, 0))
    in_specs = [rows, rows] + [pl.BlockSpec(memory_space=pl.ANY)] * len(earlier)
    return call(
        lambda up_ref, gk_ref, gv_ref, *refs: memory_back_kernel(up_ref, gk_ref, gv_ref, *refs[len(earlier) :]),
        "memory_back", (tokens // 2 // tile,),
        in_specs, rows, shape_of((tokens, width), jnp.float32),
        cost(2 * tokens * width * width, width * (4 * tokens + 4 * width)),
        scratch=room(pieces, 4), weights=pieces, aliases={3: 0} if earlier else {},
    )(upper, slope_k, slope_v, *earlier)


def input_back_kernel(up_ref, *refs):
    slopes, (x_ref, gh_ref, gain_ref, pieces, out_ref, store, sems) = refs[:6], refs[6:]
    copies = fetch(pieces, store, sems, placed(QKV, pieces), up_ref[0])
    start(copies)
    width = x_ref.shape[1]
    half = width // 2
    upstream = 0.0
    for place in range(6):
        wait(copies[place])
        upstream += dot(slopes[place][...], kernel_of(store, place, half), NT)
    back = row_back(x_ref[...].astype(jnp.float32), gain_ref[0:1], upstream)
    out_ref[...] = (gh_ref[...] + back).astype(jnp.bfloat16)


def input_back(upper, slopes, inputs, slope_hidden, gains, pieces, after):
    tokens, width = inputs.shape[0] // 2, inputs.shape[1]
    full = whole((tokens, width))
    return call(
        input_back_kernel, "input_back", (1,),
        [whole((tokens, width // 2))] * 6 + [own_spec(tokens, width), full, whole(gains.shape)],
        [full],
        [shape_of((tokens, width))],
        cost(6 * tokens * width * width, width * (14 * tokens + 6 * width)),
        scratch=room(pieces, 6), weights=pieces, after=after,
    )(upper, *slopes, inputs, slope_hidden, gains)


def in_blocks(pairs, upper):
    if pairs[0][0].shape[2] % ROW_TILE == 0:
        return pairs
    result = []
    for own, other in pairs:
        both = in_order(own, other, upper[0] == 1, 2)
        halves, blocks, _, rows, columns = both.shape
        both = both.reshape(halves, 2, 1, blocks * rows, columns)
        result.append((pick(both, upper[0] == 1, 1), pick(both, upper[0] == 0, 1)))
    return result


def axis_bits(size):
    return size.bit_length() - 1


def swap_mask(values, mask):
    count = lax.axis_size("dp")
    return lax.ppermute(values, "dp", [(i, i ^ mask) for i in range(count)])


def swap_dp(values, bit):
    return swap_mask(values, 1 << bit)


def swap_tensor(values):
    return lax.ppermute(values, "tensor", [(0, 1), (1, 0)])


def bit_set(index, bit):
    return lax.rem(lax.shift_right_logical(index, bit), 2) == 1


def hold(values, *before):
    return lax.optimization_barrier((values,) + before)[0]


def in_order(own, other, upper, axis):
    return jnp.where(
        upper, jnp.stack([other, own], axis=axis), jnp.stack([own, other], axis=axis)
    )


def gather_bit(values, bit, index):
    return place_bit(values, swap_dp(values, bit), bit, index)


def place_bit(values, received, bit, index):
    both = in_order(values, received, bit_set(index, bit), 2)
    return both.reshape((values.shape[0], 2 * values.shape[1]) + values.shape[2:])


def gather_tensor(values):
    return jnp.concatenate([values, swap_tensor(values)], axis=0)


def gather_far(shard, index, before):
    bits = axis_bits(lax.axis_size("dp"))
    values = shard[None, None]
    for bit in range(bits - 1, 1, -1):
        values = gather_bit(values, bit, index)
        if bit == bits - 1:
            values = hold(values, *before)
    return values


def gather_near(values, index):
    cut = values.shape[-1] // 2
    return gather_bit(values[..., :cut], 1, index), gather_tensor(values[..., cut:])


def gather_rest(first, second, index):
    return gather_tensor(first), gather_bit(second, 1, index)


def gather_core(first, second, before):
    if before:
        first, second = hold(first, *before), hold(second, *before)
    return [(part, swap_dp(part, 0)) for part in (first, second)]


def pick(values, upper, axis):
    return jnp.where(
        upper,
        lax.index_in_dim(values, 1, axis, keepdims=False),
        lax.index_in_dim(values, 0, axis, keepdims=False),
    )


def add_low(left, right):
    return left.astype(jnp.float32) + right.astype(jnp.float32)


def send_bit(values, bit, index):
    shape = values.shape
    values = values.reshape((shape[0], shape[1] // 2, 2) + shape[2:])
    return swap_dp(pick(values, ~bit_set(index, bit), 2), bit)


def keep_bit(values, received, bit, index):
    shape = values.shape
    values = values.reshape((shape[0], shape[1] // 2, 2) + shape[2:])
    return add_low(pick(values, bit_set(index, bit), 2), received)


def reduce_bit(values, bit, index):
    values = values.astype(jnp.bfloat16)
    return keep_bit(values, send_bit(values, bit, index), bit, index)


def joined(pieces):
    return jnp.concatenate([add_low(*pair) for pair in pieces], axis=-1).astype(jnp.bfloat16)


def sum_everywhere(values):
    values = values + swap_tensor(values)
    for bit in range(axis_bits(lax.axis_size("dp"))):
        values = values + swap_dp(values, bit)
    return values


def reverse_distance(table):
    return jnp.roll(table[:, ::-1], 1, axis=1)


def statistics_kernel(up_ref, self_ref, cross_ref, feed_ref, in_ref, wide_ref, bias_ref, out_ref):
    own, cross, feed = self_ref[...], cross_ref[...], feed_ref[...].astype(jnp.float32)
    columns = in_ref.shape[2]
    rows = own.shape[0]
    lane = lanes((rows, 128))
    squares = sum(jnp.sum(x * x, axis=-1, keepdims=True) for x in (own, cross, feed))

    def along(gradient, weight):
        weight = weight.astype(jnp.bfloat16).astype(jnp.float32)
        return jnp.sum(gradient * weight, axis=-1, keepdims=True)

    zero = sum(along(own[:, i * columns : (i + 1) * columns], in_ref[i]) for i in range(3))
    one = along(cross[:, 3 * columns : 4 * columns], in_ref[3])
    two = 0.0
    for tile in range(wide_ref.shape[1] // FF_TILE):
        two += along(
            feed[:, 2 * tile * FF_TILE : (2 * tile + 1) * FF_TILE],
            wide_ref[:, tile * FF_TILE : (tile + 1) * FF_TILE],
        )
    out = jnp.where(lane == 0, zero, 0.0)
    for place, column in ((1, one), (2, two), (3, squares)):
        out = jnp.where(lane == place, column, out)
    out_ref[:rows] = out
    out_ref[rows:] = bias_ref[...]


def statistics(upper, own, cross, feed, attention_in, expand_weight, bias):
    operands = (own, cross, feed, attention_in, expand_weight, bias)
    rows = own.shape[0] + bias.shape[0]
    return call(
        statistics_kernel, "statistics", (1,), [whole(x.shape) for x in operands],
        whole((rows, 128)), shape_of((rows, 128), jnp.float32),
        cost(4 * own.size, 4 * sum(x.size for x in operands)),
    )(upper, *operands)


def adam_update(weight, gradient, moment, square, learn_rate, weight_decay):
    new_moment = BETA_ONE * moment + (1.0 - BETA_ONE) * gradient
    new_square = BETA_TWO * square + (1.0 - BETA_TWO) * gradient * gradient
    direction = (
        new_moment
        / (1.0 - BETA_ONE**STEP)
        / (jnp.sqrt(new_square / (1.0 - BETA_TWO**STEP)) + ADAM_EPS)
    )
    return (new_moment, new_square, weight - learn_rate * (direction + weight_decay * weight))


def update_kernel(up_ref, clip_ref, own_ref, cross_ref, feed_ref, *refs):
    ins, outs = refs[:12], refs[12:]
    clip = clip_ref[0]
    columns = ins[0].shape[2]

    def step(group, at, gradient):
        weight, moment, square = (ins[3 * group + i][at] for i in range(3))
        new = adam_update(weight, gradient * clip, moment, square, MATRIX_RATE, DECAY_RATE)
        for i in range(3):
            outs[3 * group + i][at] = new[i]

    every = slice(None)
    for place in range(3):
        step(0, place, own_ref[:, place * columns : (place + 1) * columns])
    for place, source in ((3, 3), (4, 1), (5, 2)):
        step(0, place, cross_ref[:, source * columns : (source + 1) * columns])
    for place, source in ((0, 4), (1, 0)):
        step(1, (every, place), cross_ref[:, source * columns : (source + 1) * columns])
    for tile in range(ins[6].shape[1] // FF_TILE):
        for group in (2, 3):
            first = (2 * tile + group - 2) * FF_TILE
            step(group, (every, slice(tile * FF_TILE, (tile + 1) * FF_TILE)), feed_ref[:, first : first + FF_TILE].astype(jnp.float32))


def update(upper, clip, own, cross, feed, states):
    operands = (own, cross, feed) + tuple(states)
    out = [shape_of(states[i].shape, jnp.float32) for i in range(12)]
    return call(
        update_kernel, "update", (1,),
        [pl.BlockSpec(memory_space=pltpu.SMEM)] + [whole(x.shape) for x in operands],
        [whole(x.shape) for x in out], out,
        cost(20 * own.size, 8 * sum(x.size for x in operands)),
    )(upper, clip, *operands)


def interleave(left, right):
    rows = left.shape[0]
    parts = [part.reshape(rows, -1, 1, FF_TILE) for part in (left, right)]
    return jnp.concatenate(parts, axis=2).reshape(rows, -1)


def on_device(
    inputs,
    memory,
    dec_segments,
    mem_segments,
    mem_lengths,
    buckets,
    cotangent,
    attention_in,
    attention_out,
    expand_weight,
    contract_weight,
    norm_gains,
    position_bias,
    moment_attention_in,
    square_attention_in,
    moment_attention_out,
    square_attention_out,
    moment_expand,
    square_expand,
    moment_contract,
    square_contract,
    moment_gains,
    square_gains,
    moment_bias,
    square_bias,
):
    low = jnp.bfloat16
    everywhere = ("dp", "tensor")
    tensor_count = lax.axis_size("tensor")
    tensor_index = lax.axis_index("tensor")
    index = lax.axis_index("dp")
    rows = inputs.shape[0] // tensor_count
    length, width = inputs.shape[1], inputs.shape[2]
    keys = memory.shape[1]
    shard_rows = attention_in.shape[0]
    shards = width // shard_rows
    columns = attention_in.shape[2]
    aligned = shard_rows % ROW_TILE == 0
    upper = jnp.stack([bit_set(index, 0).astype(jnp.int32), tensor_index])
    split = (tensor_count, shards // 2, shard_rows)

    def own_rows(values):
        return lax.dynamic_slice_in_dim(values, tensor_index * rows, rows, 0)

    def flat(values):
        return values.reshape(values.shape[0] * values.shape[1], values.shape[2])

    def in_rows(values, size):
        return values.reshape(rows, size, values.shape[-1])

    wa = attention_in.astype(low)
    wo = attention_out.astype(low)
    shard = jnp.concatenate([wa[:, i] for i in (0, 1, 2)] + [wo[:, 0]] + [wa[:, i] for i in (4, 5, 3)] + [wo[:, 1]], axis=1)
    other_bias = swap_tensor(position_bias)
    far = gather_far(shard, index, [other_bias])
    halves = gather_near(far, index)
    first, second = halves
    pair_own = (first, swap_dp(first, 0))
    pair_own = in_blocks([pair_own], upper)[0]
    first = swap_tensor(first)
    second_got = swap_dp(second, 1)
    feed_shard = interleave(expand_weight.astype(low), contract_weight.astype(low))
    feed_shard = hold(feed_shard, far)
    feed_weights = lax.all_gather(feed_shard, everywhere, axis=0, tiled=True).reshape(
        shards, tensor_count, shard_rows, feed_shard.shape[1]
    )
    if not aligned:
        feed_weights = jnp.transpose(feed_weights, (1, 0, 2, 3)).reshape(
            1, tensor_count, width, feed_shard.shape[1]
        )

    decoder_ids = own_rows(dec_segments)
    key_index = jnp.arange(keys, dtype=jnp.int32)
    memory_ids = jnp.where(
        key_index[None, :] < own_rows(mem_lengths)[:, None], own_rows(mem_segments), -1
    )
    dec = decoder_ids[:, :, None]
    dec_across = jnp.pad(decoder_ids, ((0, 0), (0, TABLE - length)), constant_values=-1)[:, None]
    mem_across = memory_ids[:, None]
    own_heads = position_bias.shape[1]
    heads = own_heads * tensor_count
    both_bias = jnp.concatenate([position_bias, other_bias], axis=1)
    lookup = (
        buckets[None, :] == jnp.arange(position_bias.shape[0], dtype=jnp.int32)[:, None]
    ).astype(jnp.float32)
    lookup = jnp.pad(lookup, ((0, 0), (0, TABLE - length)))
    table = jnp.einsum(
        "gd,gm->md", lookup, both_bias, precision=lax.Precision.HIGHEST,
        preferred_element_type=jnp.float32,
    )
    table = reverse_distance(table).reshape(heads // 2, 2, TABLE)
    gains = norm_gains.T

    all_inputs, all_memory, all_cotangent = flat(inputs), flat(memory), flat(cotangent)
    normed_zero, qkv_own = project(upper, all_inputs, gains, [pair_own, pair_own], 0)
    qkv_own = in_rows(qkv_own, length)
    mixed_own, logs_own = self_forward(qkv_own, dec, dec_across, table, 0)
    first, second_got = hold(first, mixed_own), hold(second_got, mixed_own)
    second = place_bit(second, second_got, 1, index)
    pair_other, piece_cross = in_blocks(gather_core(first, second, []), upper)
    piece_self, piece_cross = [pair_own, pair_other], [piece_cross, piece_cross]
    qkv_other = in_rows(project_again(upper, normed_zero, piece_self, 1), length)
    mixed_other, logs_other = self_forward(qkv_other, dec, dec_across, table, 1)
    self_mixed = [flat(mixed_own), flat(mixed_other)]
    hidden_one, normed_one, cross_query = after_self(
        upper, all_inputs, self_mixed, gains, piece_self + piece_cross
    )
    cross_kv = in_rows(memory_project(upper, all_memory, piece_cross), keys)
    cross_query = in_rows(cross_query, length)
    cross_mixed, cross_logs = cross_forward(cross_query, cross_kv, dec, mem_across)
    split_or_whole = split if aligned else (tensor_count, 1, width // 2)
    output, feed_slopes, slope_two, slope_cm, keep_co, send_co = feed_forward(
        upper, hidden_one, flat(cross_mixed), all_cotangent, gains, piece_cross, feed_weights, split_or_whole
    )
    output = in_rows(output, length)

    def halves_of(kept, sent):
        if aligned:
            return kept, sent
        low_half = jnp.where(upper[0] == 1, sent, kept)
        high_half = jnp.where(upper[0] == 1, kept, sent)
        both = jnp.concatenate([low_half, high_half], axis=2)
        both = both.reshape((both.shape[0], shards // 2, 2, shard_rows, both.shape[-1]))
        return pick(both, upper[0] == 1, 2), pick(both, upper[0] == 0, 2)

    if not aligned:
        feed_slopes = jnp.transpose(
            feed_slopes.reshape(tensor_count, shards, shard_rows, feed_slopes.shape[-1]), (1, 0, 2, 3)
        )
    share_feed = lax.psum_scatter(
        feed_slopes.reshape(-1, feed_slopes.shape[-1]), everywhere, scatter_dimension=0, tiled=True
    )

    slope_cq, slope_ck, slope_cv = cross_backward(
        cross_query, cross_kv, dec, mem_across, cross_mixed, cross_logs, in_rows(slope_cm, length)
    )
    keep_co, send_co = halves_of(keep_co, send_co)
    got_co = swap_dp(send_co, 0)
    keep_kv, send_kv = halves_of(*outer(
        upper, all_memory, [flat(slope_ck), flat(slope_cv)], split_or_whole, "memory_outer", [got_co]
    ))
    got_kv = swap_dp(send_kv, 0)
    slope_one, slope_sm, keep_qo, send_qo = after_cross(
        upper, flat(slope_cq), normed_one, hidden_one, slope_two, self_mixed, gains,
        piece_self + piece_cross, split_or_whole, [keep_kv],
    )
    keep_qo, send_qo = halves_of(keep_qo, send_qo)
    got_qo = swap_dp(send_qo, 0)
    cross_sum = joined([(keep_co, got_co), (keep_kv, got_kv), (keep_qo, got_qo)])
    first, second = cross_sum[..., :1024], cross_sum[..., 1024:]
    first_got, second_got = swap_tensor(first[1:2]), send_bit(second, 1, index)
    slope_sm = in_rows(slope_sm, length)

    def self_half(half, qkv, mixed, logs, after):
        *slopes, diagonals = self_backward(
            qkv, dec, dec_across, table, mixed, logs, slope_sm, half, after
        )
        return [flat(slope) for slope in slopes], diagonals

    one_half = (1,) + split_or_whole[1:]
    slopes_other, diagonals_other = self_half(1, qkv_other, mixed_other, logs_other, [got_qo])
    first = hold(add_low(first[0:1], first_got).astype(low), slopes_other[0])
    second = hold(keep_bit(second, second_got, 1, index).astype(low), slopes_other[0])
    first_got, second_got = send_bit(first, 1, index), swap_tensor(second[1:2])
    keep_other, send_other = halves_of(
        *outer(upper, normed_zero, slopes_other, one_half, "self_outer")
    )
    got_other = swap_dp(send_other, 0)
    other_sum = add_low(keep_other, got_other).astype(low)
    cross_sum = jnp.concatenate(
        [keep_bit(first, first_got, 1, index), add_low(second[0:1], second_got)], axis=-1
    ).astype(low)
    cross_sum = hold(cross_sum, keep_other)
    cross_ready = cross_sum
    cross_got = send_bit(cross_sum, 2, index)
    other_got = swap_tensor(other_sum)
    slopes_own, diagonals_own = self_half(0, qkv_own, mixed_own, logs_own, [other_sum])
    cross_sum = hold(keep_bit(cross_sum, cross_got, 2, index), slopes_own[0])
    bits = axis_bits(lax.axis_size("dp"))
    for bit in range(3, bits):
        cross_sum = reduce_bit(cross_sum, bit, index)
    keep_own, send_own = halves_of(
        *outer(upper, normed_zero, slopes_own, one_half, "self_outer", [cross_ready])
    )
    got_own = swap_dp(send_own, 0)
    memory_slopes = [hold(flat(slope_ck), keep_own), flat(slope_cv)]
    memory_grad = memory_back(upper, *memory_slopes, piece_cross, 0, [])
    other_got = hold(other_got, memory_grad)
    self_sum = (add_low(keep_own, got_own) + other_got.astype(jnp.float32)).astype(low)
    self_got = send_bit(self_sum, 1, index)
    slopes_self = [part for pair in zip(slopes_own, slopes_other) for part in pair]
    diagonals = jnp.concatenate([diagonals_own, diagonals_other], axis=0)
    (input_slope,) = input_back(
        upper, slopes_self, all_inputs, slope_one, gains, piece_self, [got_own]
    )
    input_got = swap_tensor(input_slope)
    self_sum = hold(keep_bit(self_sum, self_got, 1, index), input_slope)
    for bit in range(2, bits):
        if bit == 2:
            self_got = send_bit(self_sum.astype(low), bit, index)
            memory_slopes[0] = hold(memory_slopes[0], input_slope)
            memory_grad = memory_back(upper, *memory_slopes, piece_cross, 1, [memory_grad])
            self_sum = keep_bit(self_sum.astype(low), hold(self_got, memory_grad), bit, index)
        else:
            self_got = send_bit(self_sum.astype(low), bit, index)
            if bit == bits - 1 and False:
                self_got = hold(self_got, input_got)
            self_sum = keep_bit(self_sum.astype(low), self_got, bit, index)
    memory_grad = in_rows(memory_grad, keys)
    share_cross, share_self = cross_sum[0, 0], self_sum[0, 0]
    input_grad = (
        in_order(in_rows(input_slope, length), in_rows(input_got, length), tensor_index == 1, 0)
        .reshape(inputs.shape)
        .astype(jnp.float32)
    )

    bias_local = jnp.einsum(
        "gd,md->gm", lookup, reverse_distance(diagonals.reshape(heads, TABLE)),
        precision=lax.Precision.HIGHEST, preferred_element_type=jnp.float32,
    )
    bias_local = jnp.where(
        tensor_index == 1, jnp.roll(bias_local, own_heads, axis=1), bias_local
    )
    bias_rows = bias_local.size // 128
    bias_tile = jnp.pad(bias_local.reshape(bias_rows, 128), ((0, 8 - bias_rows), (0, 0)))
    table_rows = statistics(
        upper, share_self, share_cross, share_feed, jnp.swapaxes(attention_in, 0, 1), expand_weight, bias_tile
    )
    table_rows = table_rows + hold(swap_tensor(table_rows), input_got)
    totals = table_rows[shard_rows:]
    table_rows = table_rows[:shard_rows]
    old_gains = lax.dynamic_slice_in_dim(norm_gains, index * shard_rows, shard_rows, 0)
    shared_gains = table_rows[:, :3] / old_gains
    square_sum = jnp.sum(table_rows[:, 3]) + jnp.sum(shared_gains * shared_gains)
    totals = totals + jnp.where(
        lax.broadcasted_iota(jnp.int32, totals.shape, 0) == bias_rows, square_sum, 0.0
    )
    for bit in range(bits):
        totals = totals + swap_dp(totals, bit)
    bias_sums = totals[:bias_rows].reshape(bias_local.shape)
    grad_norm = jnp.sqrt(totals[bias_rows, 0] + jnp.sum(bias_sums * bias_sums))
    clip_factor = jnp.minimum(1.0, CLIP_NORM / (grad_norm + 1e-06))

    bias_share = lax.dynamic_slice_in_dim(bias_sums, tensor_index * own_heads, own_heads, 1)
    new = update(
        upper, clip_factor[None], share_self, share_cross, share_feed,
        tuple(
            jnp.swapaxes(state, 0, 1)
            for state in (attention_in, moment_attention_in, square_attention_in)
        )
        + (
            attention_out, moment_attention_out, square_attention_out,
            expand_weight, moment_expand, square_expand,
            contract_weight, moment_contract, square_contract,
        ),
    )
    new = [jnp.swapaxes(state, 0, 1) for state in new[:3]] + list(new[3:])
    new_gains = adam_update(
        old_gains, shared_gains * clip_factor, moment_gains, square_gains, SMALL_RATE, 0.0
    )
    new_bias = adam_update(
        position_bias, bias_share * clip_factor, moment_bias, square_bias, SMALL_RATE, 0.0
    )
    return (
        (output, input_grad, memory_grad, grad_norm)
        + tuple(new) + new_gains + new_bias
    )


def solution(mesh):
    return jax.shard_map(
        on_device,
        mesh=mesh,
        in_specs=(
            P("dp", None, None),
            P("dp", None, None),
            P("dp", None),
            P("dp", None),
            P("dp"),
            P(),
            P("dp", None, None),
            P("dp", None, "tensor"),
            P("dp", None, "tensor"),
            P("dp", "tensor"),
            P("dp", "tensor"),
            P(),
            P(None, "tensor"),
            P("dp", None, "tensor"),
            P("dp", None, "tensor"),
            P("dp", None, "tensor"),
            P("dp", None, "tensor"),
            P("dp", "tensor"),
            P("dp", "tensor"),
            P("dp", "tensor"),
            P("dp", "tensor"),
            P("dp", None),
            P("dp", None),
            P(None, "tensor"),
            P(None, "tensor"),
        ),
        out_specs=(
            P(("dp", "tensor"), None, None),
            P("dp", None, None),
            P(("dp", "tensor"), None, None),
            P(),
            P("dp", None, "tensor"),
            P("dp", None, "tensor"),
            P("dp", None, "tensor"),
            P("dp", None, "tensor"),
            P("dp", None, "tensor"),
            P("dp", None, "tensor"),
            P("dp", "tensor"),
            P("dp", "tensor"),
            P("dp", "tensor"),
            P("dp", "tensor"),
            P("dp", "tensor"),
            P("dp", "tensor"),
            P("dp", None),
            P("dp", None),
            P("dp", None),
            P(None, "tensor"),
            P(None, "tensor"),
            P(None, "tensor"),
        ),
        check_vma=False,
    )
```
